128 devices in a mesh: gx: 16 (over z_lo, y, core), gy: 8 (over z_hi, x).
Axes of the slice: x: 4, y: 4, z: 4 (z_hi: 2, z_lo: 2; z = z_hi * 2 + z_lo), core: 2. Of those that a mesh axis runs over, the one named last changes fastest.
Arguments:
- hopping_blocks: float32 [512, 5, 128, 128], P('gx'), may hold values from -0.5 to 0.5, as said below
- neighbors: int32 [512, 5], P('gx'), may hold values from 0 to 511, as said below
- orbital_grid: int32 [3, 65536], P(None, 'gx'), may hold values from 0 to 63
- trial_block: float32 [65536, 512], P('gx', 'gy'), may hold values from -6 to 6
Outputs:
- orthonormal_block: float32 [65536, 512], P('gx', 'gy')
- projected: float32 [512, 512], P('gx', 'gy')
- dipoles: float32 [3, 512, 512], P(None, 'gx', 'gy')
- spectrum: float32 [256], replicated
The draws below stay inside these ranges and needn't reach their ends.
Inputs may be any that keep to these rules, and one draw needn't show every extreme that they name: `neighbors`: row block i names each of the column blocks i - 2, i - 1, i, i + 1, i + 2 once, in an order of its own, each clamped to 0 to 511. `hopping_blocks`: H is symmetric: block k of row block i is the transpose of the block of row block neighbors[i, k] that refers back to i, and the block of a row block with itself is symmetric; a block whose unclamped column block lies outside 0 to 511 is zero.
All inputs are finite; a program needn't handle non-finite values.
Results may differ from the reference program's by a relative error of at most 0.0003.
Values sent between devices are 32-bit elements; how exact they have to be, the bound alone decides.
No kernel may reach another device: no remote copies, remote signals or barrier semaphores. Data moves between devices by JAX's collectives and lax.ppermute only.
A program may use at most 320 MiB of HBM per device.

```python
import math
import jax
import jax.numpy as jnp
from jax import lax

BS = 128
K = 512
NW = 256
NB = 512
NTOT = 65536


def slot_offsets(key):
    order_key = jax.random.fold_in(key, 101)
    scores = jax.random.randint(order_key, (NB, 5), 0, 1 << 20, dtype=jnp.int32)
    scores = scores * 5 + jnp.arange(5, dtype=jnp.int32)[None, :]
    return jnp.argsort(scores, axis=1, stable=True).astype(jnp.int32)


def draw_neighbors(key, part):
    offsets = slot_offsets(key)
    own_rows = jnp.arange(NB, dtype=jnp.int32)[:, None]
    return jnp.clip(own_rows + offsets - 2, 0, NB - 1).astype(jnp.int32)


def draw_hopping_blocks(key, part):
    offsets = slot_offsets(key)
    key = jax.random.fold_in(key, 13)
    upper_key, diag_key = jax.random.split(key)
    spread = 0.5 / math.sqrt(5.0 * BS)
    upper = jax.random.truncated_normal(upper_key, -6.0, 6.0, (NB, 2, BS, BS), jnp.float32) * spread
    diag = jax.random.truncated_normal(diag_key, -6.0, 6.0, (NB, BS, BS), jnp.float32) * spread
    sym = (diag + jnp.swapaxes(diag, 1, 2)) / math.sqrt(2.0)
    near_up = upper[:, 0]
    far_up = upper[:, 1]
    near_down = jnp.roll(jnp.swapaxes(near_up, 1, 2), 1, axis=0)
    far_down = jnp.roll(jnp.swapaxes(far_up, 1, 2), 2, axis=0)
    canonical = jnp.stack([far_down, near_down, sym, near_up, far_up], axis=1)
    own_rows = jnp.arange(NB, dtype=jnp.int32)[:, None]
    target = own_rows + jnp.arange(5, dtype=jnp.int32)[None, :] - 2
    inside = ((target >= 0) & (target < NB)).astype(jnp.float32)
    canonical = canonical * inside[:, :, None, None]
    placed = jnp.take_along_axis(canonical, offsets[:, :, None, None], axis=1)
    return placed.astype(jnp.float32)


def set_ends(array, rng, least, high):
    place = [jax.random.randint(jax.random.fold_in(rng, axis), (), 0, length) for axis, length in enumerate(array.shape)]
    widest = array.shape.index(max(array.shape))
    beside = place[:widest] + [(place[widest] + 1) % array.shape[widest]] + place[widest + 1:]
    return array.at[tuple(place)].set(least).at[tuple(beside)].set(high)


def level_of(stream_key, shape, shards, least, high):
    loudness, own = 1.0, jax.random.fold_in(stream_key, 6)
    for dim, shards_of in shards:
        steps = jnp.exp(jax.random.uniform(jax.random.fold_in(own, dim), (shards_of,), jnp.float32, least / len(shards), high / len(shards)))
        loudness = loudness * jnp.repeat(steps, shape[dim] // shards_of).reshape([-1 if axis == dim else 1 for axis in range(len(shape))])
    return loudness


def gaussian(own_key, shape, deviation, most, cuts=(), held_as=jnp.bfloat16):
    loudness = level_of(own_key, shape, cuts, -0.22, 0.18) if cuts else 1.0
    values = jax.random.normal(own_key, shape, jnp.float32) * deviation * loudness
    return jnp.minimum(jnp.maximum(values, -most), most).astype(held_as)


def setup_inputs(seed: int = 0) -> dict:
    keys = jax.random.split(jax.random.key(seed), 5)
    hopping_blocks = draw_hopping_blocks(jax.random.fold_in(keys[4], 71), 0)
    neighbors = draw_neighbors(jax.random.fold_in(keys[4], 71), 0)
    orbital_grid = set_ends(jax.random.randint(keys[2], (3, NTOT), 0, 64), jax.random.fold_in(keys[2], 1), 0, 63).astype(jnp.int32)
    trial_block = gaussian(keys[3], (NTOT, K), 1.0, 6.0, ((0, 16), (1, 8)), jnp.float32)
    return dict(hopping_blocks=hopping_blocks, neighbors=neighbors, orbital_grid=orbital_grid, trial_block=trial_block)


FILTER_CENTER = -0.3
FILTER_HALF = 0.9
OMEGA_EDGE = 0.3
BROAD = 0.01
GRID_HALF = 32.0

def hamiltonian(hopping_blocks, neighbors, vectors):
    slab_rows = vectors.reshape(NB, BS, K)
    result = jnp.zeros((NB, BS, K), jnp.float32)
    for slot in range(5):
        picked = slab_rows[neighbors[:, slot]]
        result = result + jnp.einsum('rab,rbc->rac', hopping_blocks[:, slot], picked, precision=lax.Precision.HIGHEST)
    return result.reshape(NTOT, K)

def shifted(hopping_blocks, neighbors, vectors):
    return (hamiltonian(hopping_blocks, neighbors, vectors) - FILTER_CENTER * vectors) / FILTER_HALF

def reference(hopping_blocks, neighbors, orbital_grid, trial_block):
    places = (orbital_grid.astype(jnp.float32) + 0.5) / GRID_HALF - 1.0
    previous = trial_block
    current = shifted(hopping_blocks, neighbors, trial_block)
    for degree in range(3):
        following = 2.0 * shifted(hopping_blocks, neighbors, current) - previous
        previous, current = (current, following)
    filtered = current
    applied = hamiltonian(hopping_blocks, neighbors, filtered)
    gram_matrix = jnp.dot(filtered.T, filtered, precision=lax.Precision.HIGHEST) / NTOT
    factor = jnp.linalg.cholesky(gram_matrix)
    identity = jnp.eye(K, dtype=gram_matrix.dtype)
    inverse = lax.linalg.triangular_solve(factor, identity, left_side=True, lower=True)
    orthonormal_block = jnp.dot(filtered, inverse.T, precision=lax.Precision.HIGHEST)
    rotated_applied = jnp.dot(applied, inverse.T, precision=lax.Precision.HIGHEST)
    projected = jnp.dot(orthonormal_block.T, rotated_applied, precision=lax.Precision.HIGHEST) / NTOT
    dipoles = jnp.stack([jnp.dot(orthonormal_block.T, places[comp][:, None] * orthonormal_block, precision=lax.Precision.HIGHEST) for comp in range(3)]) / math.sqrt(NTOT)
    energies = jnp.diagonal(projected)
    strength = lax.optimization_barrier(jnp.sum(dipoles * dipoles, axis=0))
    energy_gaps = energies[None, :] - energies[:, None]
    omegas = -OMEGA_EDGE + 2.0 * OMEGA_EDGE * (jnp.arange(NW, dtype=jnp.float32) + 0.5) / NW

    def line_value(omega):
        profile = BROAD / math.pi / ((omega - energy_gaps) ** 2 + BROAD * BROAD)
        return jnp.sum(strength * profile)
    spectrum = lax.map(line_value, omegas) / (K * K)
    return (orthonormal_block, projected, dipoles, spectrum)
```

```python
import functools
import math

import jax
import jax.numpy as jnp
from jax import lax
from jax.experimental import pallas as pl
from jax.experimental.pallas import tpu as pltpu
f32=jnp.float32; bf16=jnp.bfloat16
MB=1<<20

def split(x):
    hi = x.astype(bf16)
    return hi, (x - hi.astype(f32)).astype(bf16)

def inv_chol_128(read, write):
    lane = lax.broadcasted_iota(jnp.int32,(8,128),1)
    sub = lax.broadcasted_iota(jnp.int32,(8,128),0)
    full = lambda v: jnp.broadcast_to(v,(8,128))
    m = [read(g) for g in range(16)]
    for p in range(16):
        j0 = 8*p
        d = m[p]
        c = [full(d[:,j0+l:j0+l+1]) for l in range(8)]
        s = {}; rp = []; rows = []; fin = d
        inpanel = (lane>=j0)&(lane<j0+8)
        for l in range(8):
            piv = full(c[l][l:l+1,:])
            r = 1.0/piv
            rp.append(r)
            mult = jnp.where(sub>l,c[l]*r,0.0)
            for q in range(l+1,8):
                s[l,q] = full(c[q][l:l+1,:])
                c[q] = c[q]-mult*s[l,q]
            row = jnp.where(lane==j0+l,1.0,full(d[l:l+1,:]))
            row = jnp.where(inpanel&(lane>j0+l),0.0,row)
            rows.append(row)
            d = jnp.where((lane==j0+l)&(sub>l),0.0,d)-mult*row
            fin = jnp.where(sub==l,row*lax.rsqrt(piv),fin)
        m[p] = fin
        for g in range(p+1,16):
            v = m[g]
            cg = [full(v[:,j0+l:j0+l+1]) for l in range(8)]
            v = jnp.where(inpanel,0.0,v)
            for l in range(8):
                mult = cg[l]*rp[l]
                for q in range(l+1,8):
                    cg[q] = cg[q]-mult*s[l,q]
                v = v-mult*rows[l]
            m[g] = v
    for g in range(16):
        write(g, jnp.where(lane<=sub+8*g, m[g], 0.0))

def hdot(a,b,dims):
    return lax.dot_general(a,b,(dims,((),())),precision=lax.Precision.HIGHEST,preferred_element_type=f32)

def chol_kernel(scale, g_ref, out_ref):
    out_ref[...] = g_ref[...]*scale
    def outer(k, c):
        k0 = pl.multiple_of(k*128,128)
        def read(g): return out_ref[pl.ds(k0+8*g,8), pl.ds(k0,128)]
        def write(g,v): out_ref[pl.ds(k0+8*g,8), pl.ds(k0,128)] = v
        inv_chol_128(read,write)
        return c
    for k in range(4):
        outer(k,0)
        x = out_ref[128*k:128*k+128,128*k:128*k+128]
        for j in range(4):
            if j==k: continue
            out_ref[128*k:128*k+128,128*j:128*j+128] = hdot(x,out_ref[128*k:128*k+128,128*j:128*j+128],((1,),(0,)))
        bk = out_ref[128*k:128*k+128,:]
        for i in range(k+1,4):
            w = bk[:,128*i:128*i+128]
            upd = hdot(w,bk,((0,),(0,)))
            for j in range(4):
                if k<j<i: continue
                o = -upd[:,128*j:128*j+128] if j==k else out_ref[128*i:128*i+128,128*j:128*j+128]-upd[:,128*j:128*j+128]
                out_ref[128*i:128*i+128,128*j:128*j+128]=o
        for j in range(k+1,4):
            out_ref[128*k:128*k+128,128*j:128*j+128]=jnp.zeros((128,128),f32)

def chol(g, scale):
    return pl.pallas_call(functools.partial(chol_kernel,scale),
        out_shape=jax.ShapeDtypeStruct((512,512),f32), name="chol",
        compiler_params=pltpu.CompilerParams(vmem_limit_bytes=24*MB))(g)

def dup_pack(y, lane):
    hi = y.astype(bf16).astype(f32)
    return jnp.where(lane<64, hi, y-hi).astype(bf16)

def prep_kernel(h_ref, v_ref, a2_ref, y_ref, p_ref):
    for r in range(4):
        for k in range(5):
            hi, lo = split(h_ref[r,k])
            a2_ref[r,0:128,128*k:128*k+128] = hi
            a2_ref[r,128:256,128*k:128*k+128] = lo
    v = v_ref[...]
    y = jnp.concatenate([v,v],axis=0).T
    lane = lax.broadcasted_iota(jnp.int32,(512,128),1)
    y_ref[...] = y
    p_ref[...] = dup_pack(y,lane)

def prep(h, vt):
    return pl.pallas_call(prep_kernel, grid=(8,), name="prep",
        in_specs=[pl.BlockSpec((4,5,128,128),lambda g:(g,0,0,0)), pl.BlockSpec((64,512),lambda g:(0,g))],
        out_specs=[pl.BlockSpec((4,256,640),lambda g:(g,0,0)), pl.BlockSpec((512,128),lambda g:(g,0)), pl.BlockSpec((512,128),lambda g:(g,0))],
        out_shape=[jax.ShapeDtypeStruct((32,256,640),bf16), jax.ShapeDtypeStruct((4096,128),f32), jax.ShapeDtypeStruct((4096,128),bf16)],
        cost_estimate=pl.CostEstimate(flops=1000000,bytes_accessed=25*MB,transcendentals=0),
        compiler_params=pltpu.CompilerParams(vmem_limit_bytes=24*MB))(h,vt)

C0, HALF = -0.3, 0.9

def apply_row(a2, pieces):
    rhs = jnp.concatenate(pieces,axis=0)
    res = jnp.dot(a2, rhs, preferred_element_type=f32)
    u = res[:128]+res[128:]
    return u + pltpu.roll(u, 64, 1)

def recur(hy, y, yp):
    t = (hy - C0*y)/HALF
    return t if yp is None else 2.0*t - yp

def edge_kernel(first, nloc, alo, ahi, vlo, vhi, ylo, yhi, *rest):
    if first:
        hlo, hhi, ye, slo, shi, ext = rest
    else:
        plo, phi, hlo, hhi, ye, slo, shi, ext = rest
    lane = lax.broadcasted_iota(jnp.int32,(128,128),1)
    lane2 = lax.broadcasted_iota(jnp.int32,(256,128),1)
    for ref, at in ((hlo,0),(hhi,1280)):
        if first:
            v = ref[...]
            y = jnp.concatenate([v,v],axis=0).T
        else:
            x = ref[...]; xr = pltpu.roll(x,64,1)
            y = jnp.concatenate([jnp.where(lane<64,x,xr),jnp.where(lane<64,xr,x)],axis=0)
        ext[at:at+256,:] = dup_pack(y,lane2)
    ext[256:768,:] = vlo[...]
    ext[768:1280,:] = vhi[...]
    new = []
    for e in range(4):
        i = (0,1,30,31)[e]
        off = 2 if e<2 else -22
        a = (alo if e<2 else ahi)[e%2]
        hy = apply_row(a,[ext[pl.ds(pl.multiple_of((nloc[5*i+k]+off)*128,128),128),:] for k in range(5)])
        sl = slice(128*(e%2),128*(e%2)+128)
        y = (ylo if e<2 else yhi)[sl,:]
        yp = None if first else (plo if e<2 else phi)[sl,:]
        new.append(recur(hy,y,yp))
        ye[128*e:128*e+128,:] = new[-1]
    slo[...] = jnp.where(lane<64,new[0],new[1])
    shi[...] = jnp.where(lane<64,new[2],new[3])

def edge(nloc, a2, vp, y, yp, hlo, hhi):
    first = yp is None
    B = pl.BlockSpec
    w = lambda shape,*idx: B(shape, lambda g,n: idx)
    ys = [w((256,128),0,0), w((256,128),15,0)]
    hs = [w((64,256),0,0)]*2 if first else [w((128,128),0,0)]*2
    return pl.pallas_call(functools.partial(edge_kernel,first), name="edge",
        grid_spec=pltpu.PrefetchScalarGridSpec(num_scalar_prefetch=1, grid=(1,),
            in_specs=[w((2,256,640),0,0,0), w((2,256,640),15,0,0), w((512,128),0,0), w((512,128),7,0)]+ys+([] if first else ys)+hs,
            out_specs=[w((512,128),0,0), w((128,128),0,0), w((128,128),0,0)],
            scratch_shapes=[pltpu.VMEM((1536,128),bf16)]),
        out_shape=[jax.ShapeDtypeStruct((512,128),f32)]+[jax.ShapeDtypeStruct((128,128),f32)]*2,
        cost_estimate=pl.CostEstimate(flops=4*2*256*640*128,bytes_accessed=3*MB,transcendentals=0),
        compiler_params=pltpu.CompilerParams(vmem_limit_bytes=16*MB))(
            nloc,a2,a2,vp,vp,y,y,*([] if first else [yp,yp]),hlo,hhi)

def inner_kernel(first, last, nloc, a2, vp, ye, y, *rest):
    if first: yp=None; outs=rest
    else: yp=rest[0]; outs=rest[1:]
    g = pl.program_id(0)
    lane = lax.broadcasted_iota(jnp.int32,(128,128),1)
    def put(r, new):
        if last:
            outs[0][0,:,128*r:128*r+128] = new.T[:64]
        else:
            outs[0][128*r:128*r+128,:] = new
            outs[1][128*r:128*r+128,:] = dup_pack(new,lane)
    def inner(r):
        i = 4*g+r
        hy = apply_row(a2[r],[vp[pl.ds(pl.multiple_of(nloc[5*i+k]*128,128),128),:] for k in range(5)])
        sl = slice(128*r,128*r+128)
        put(r, recur(hy,y[sl,:],None if yp is None else yp[sl,:]))
    @pl.when(g==0)
    def _():
        put(0,ye[0:128,:]); put(1,ye[128:256,:]); inner(2); inner(3)
    @pl.when((g>0)&(g<7))
    def _():
        for r in range(4): inner(r)
    @pl.when(g==7)
    def _():
        inner(0); inner(1); put(2,ye[256:384,:]); put(3,ye[384:512,:])

def inner(nloc, a2, vp, ye, y, yp, last):
    first = yp is None
    B = pl.BlockSpec
    yb = B((512,128),lambda g,n:(g,0))
    if last:
        outs=[B((1,64,512),lambda g,n:(g,0,0))]; shapes=[jax.ShapeDtypeStruct((8,64,512),f32)]
    else:
        outs=[yb,yb]; shapes=[jax.ShapeDtypeStruct((4096,128),f32),jax.ShapeDtypeStruct((4096,128),bf16)]
    return pl.pallas_call(functools.partial(inner_kernel,first,last), name="inner",
        grid_spec=pltpu.PrefetchScalarGridSpec(num_scalar_prefetch=1, grid=(8,),
            in_specs=[B((4,256,640),lambda g,n:(g,0,0)), B((4096,128),lambda g,n:(0,0)), B((512,128),lambda g,n:(0,0)), yb]+([] if first else [yb]),
            out_specs=outs),
        out_shape=shapes,
        cost_estimate=pl.CostEstimate(flops=28*2*256*640*128*4,bytes_accessed=16*MB,transcendentals=0),
        compiler_params=pltpu.CompilerParams(vmem_limit_bytes=24*MB))(
            nloc,a2,vp,ye,y,*([] if first else [yp]))

NT = ((1,),(1,))
NN = ((1,),(0,))
NORB = 65536

def bdot(a, b, dims):
    return lax.dot_general(a,b,(dims,((),())),preferred_element_type=f32)

def gram_kernel(x_ref, g_ref):
    xh, xl = split(x_ref[...])
    for i in range(4):
        sl = slice(128*i,128*i+128)
        g_ref[sl,:] = bdot(xh[sl],xh,NT)+bdot(xl[sl],xh,NT)+bdot(xh[sl],xl,NT)

def gram(x):
    return pl.pallas_call(gram_kernel, out_shape=jax.ShapeDtypeStruct((512,512),f32), name="gram",
        cost_estimate=pl.CostEstimate(flops=3*2*512**3,bytes_accessed=2*MB,transcendentals=0),
        compiler_params=pltpu.CompilerParams(vmem_limit_bytes=16*MB))(x)

def moment_kernel(n4, gy, x_ref, lo_ref, hi_ref, a2, grid_ref, s_ref, xh, xl, yt):
    x = x_ref[...]
    for ref, at, w in ((lo_ref,0,256),(x_ref,256,512),(hi_ref,768,256)):
        h, l = split(ref[...])
        xh[:,at:at+w] = h; xl[:,at:at+w] = l
    for i in range(4):
        at = [pl.ds(pl.multiple_of((n4[5*i+k]+2)*128,128),128) for k in range(5)]
        h = jnp.concatenate([xh[:,a] for a in at],axis=1)
        l = jnp.concatenate([xl[:,a] for a in at],axis=1)
        r = bdot(h,a2[0,i],NT)
        yt[:,128*i:128*i+128] = r[:,:128]+r[:,128:]+bdot(l,a2[0,i,:128,:],NT)
    ch = xh[:,256:768]; cl = xl[:,256:768]
    for q in range(4):
        if q==0: y = yt[...]
        else: y = x*((grid_ref[q-1:q,:].astype(f32)+0.5)/32.0-1.0)
        yh, yl = split(y)
        for i in range(4):
            sl = slice(128*i,128*i+128)
            s_ref[q,sl,:] = bdot(ch[sl],yh,NT)+bdot(cl[sl],yh,NT)+bdot(ch[sl],yl,NT)

def moments(n4, gy, x, lo, hi, a2, grid):
    B = pl.BlockSpec
    w = lambda shape: B(shape, lambda g,n,y: (0,)*len(shape))
    return pl.pallas_call(moment_kernel, name="moments",
        grid_spec=pltpu.PrefetchScalarGridSpec(num_scalar_prefetch=2, grid=(1,),
            in_specs=[w((512,512)),w((512,256)),w((512,256)),B((1,4,256,640),lambda g,n,y:(y[0],0,0,0)),B((3,512),lambda g,n,y:(0,y[0]))],
            out_specs=w((4,512,512)),
            scratch_shapes=[pltpu.VMEM((512,1024),bf16),pltpu.VMEM((512,1024),bf16),pltpu.VMEM((512,512),f32)]),
        out_shape=jax.ShapeDtypeStruct((4,512,512),f32),
        cost_estimate=pl.CostEstimate(flops=15*2*512**3,bytes_accessed=8*MB,transcendentals=0),
        compiler_params=pltpu.CompilerParams(vmem_limit_bytes=32*MB))(n4,gy,x,lo,hi,a2.reshape(8,4,256,640),grid)

def half_kernel(pos, s_ref, li_ref, out_ref):
    gx = pos[0]; gy = pos[1]
    la = li_ref[pl.ds(pl.multiple_of(32*gx,32),32),:]
    z = jnp.zeros((64,128),f32)
    for q in range(4):
        parts = [la if p==q else jnp.zeros_like(la) for p in range(4)]
        z = z + hdot(s_ref[q],jnp.concatenate(parts,axis=0),NT)
    za = hdot(li_ref[...],s_ref[0],NT)
    lb = li_ref[:,pl.ds(pl.multiple_of((gy//2)*128,128),128)]
    lb = pltpu.roll(lb,64*(gy%2),1)
    e = hdot(jnp.ones((8,64),f32),za*lb[:,:64],NT)
    for p in range(8):
        out_ref[p,0:64,:] = z
        for c in range(4):
            out_ref[p,64+c:65+c,:] = e[0:1,128*c:128*c+128]
        out_ref[p,68:72,:] = jnp.zeros((4,128),f32)

def half(pos, s, li):
    return pl.pallas_call(half_kernel, name="half",
        in_specs=[pl.BlockSpec(memory_space=pltpu.SMEM),pl.BlockSpec(memory_space=pltpu.VMEM),pl.BlockSpec(memory_space=pltpu.VMEM)],
        out_shape=jax.ShapeDtypeStruct((8,72,128),f32),
        cost_estimate=pl.CostEstimate(flops=2*5*64*512*512*6,bytes_accessed=2*MB,transcendentals=0),
        compiler_params=pltpu.CompilerParams(vmem_limit_bytes=16*MB))(pos,s,li)

def tile_kernel(pos, r_ref, li_ref, p_ref, d_ref, w_ref, e_ref, acc):
    gx = pos[0]; gy = pos[1]
    z = r_ref[:,0:64,:].reshape(512,128)
    lb = li_ref[pl.ds(pl.multiple_of(64*gy,64),64),:]
    t = hdot(lb,z,NN)
    tt = jnp.concatenate([t,t],axis=0).T
    p_ref[...] = tt[0:32,0:64]*(1.0/NORB)
    for q in range(3):
        d_ref[q] = tt[32*q+32:32*q+64,0:64]*(1.0/math.sqrt(NORB))
    lane = lax.broadcasted_iota(jnp.int32,(64,128),1)
    lane8 = lax.broadcasted_iota(jnp.int32,(8,128),1)
    e = r_ref[0,64:72,:]
    for p in range(1,8): e = e + r_ref[p,64:72,:]
    e_ref[...] = e*(1.0/NORB)
    ea = jnp.broadcast_to(e_ref[pl.ds(gx//4,1),:],(8,128))
    ea = pltpu.roll(ea,(128-32*(gx%4))%128,1)
    ea = jnp.where(lane8<32,ea,0.0)
    ea = ea+pltpu.roll(ea,32,1)+pltpu.roll(ea,64,1)+pltpu.roll(ea,96,1)
    eb = jnp.broadcast_to(e_ref[pl.ds(gy//2,1),:],(8,128))
    eb = pltpu.roll(eb,64*(gy%2),1)
    eb = jnp.broadcast_to(eb[0:1,:],(128,128)).T[0:64,:]
    gap = eb-jnp.broadcast_to(ea[0:1,:],(64,128))
    dip = t*(1.0/math.sqrt(NORB))
    sq = jnp.where(lane>=32,dip*dip,0.0)
    st = (sq+pltpu.roll(sq,32,1)+pltpu.roll(sq,64,1)+pltpu.roll(sq,96,1))*(0.01/math.pi)
    base = (64*(lane8//32)).astype(f32)+0.5
    for w in range(64):
        om = -0.3+0.6*(base+float(w))/256.0
        tot = jnp.zeros((8,128),f32)
        for b in range(8):
            x = om-gap[8*b:8*b+8,:]
            tot = tot+st[8*b:8*b+8,:]/(x*x+0.0001)
        acc[w:w+1,:] = jnp.sum(tot,axis=0,keepdims=True)
    sel = (lane8//32==lax.broadcasted_iota(jnp.int32,(8,128),0)).astype(f32)
    w_ref[...] = hdot(sel,acc[...],NT)

def tile(pos, r, li):
    V = pl.BlockSpec(memory_space=pltpu.VMEM)
    return pl.pallas_call(tile_kernel, name="tile",
        in_specs=[pl.BlockSpec(memory_space=pltpu.SMEM),V,V], out_specs=[V,V,V],
        out_shape=[jax.ShapeDtypeStruct((32,64),f32),jax.ShapeDtypeStruct((3,32,64),f32),jax.ShapeDtypeStruct((8,64),f32)],
        scratch_shapes=[pltpu.VMEM((8,128),f32),pltpu.VMEM((64,128),f32)],
        cost_estimate=pl.CostEstimate(flops=10000000,bytes_accessed=2*MB,transcendentals=0),
        compiler_params=pltpu.CompilerParams(vmem_limit_bytes=16*MB))(pos,r,li)

def rotate_kernel(x_ref, li_ref, o_ref):
    xh, xl = split(x_ref[...])
    for i in range(8):
        lh, ll = split(li_ref[64*i:64*i+64,:])
        o_ref[i] = bdot(lh,xh,NN)+bdot(ll,xh,NN)+bdot(lh,xl,NN)

def rotate(x, li):
    return pl.pallas_call(rotate_kernel, out_shape=jax.ShapeDtypeStruct((8,64,512),f32), name="rotate",
        cost_estimate=pl.CostEstimate(flops=3*2*512**3,bytes_accessed=3*MB,transcendentals=0),
        compiler_params=pltpu.CompilerParams(vmem_limit_bytes=16*MB))(x,li)

BOTH = ("gx","gy")

def swap(x, axis):
    return lax.all_to_all(x,axis,split_axis=0,concat_axis=0,tiled=True)

def shards(hopping_blocks, neighbors, orbital_grid, trial_block):
    gx = lax.axis_index("gx"); gy = lax.axis_index("gy")
    nloc = neighbors.reshape(-1) - 32*gx
    up = [(i,i+1) for i in range(15)]
    down = [(i+1,i) for i in range(15)]
    vt = trial_block.T
    halo = (lax.ppermute(vt[:,3840:],"gx",up), lax.ppermute(vt[:,:256],"gx",down))
    a2, y, packed = prep(hopping_blocks, vt)
    yp = None
    for degree in range(4):
        ye, slo, shi = edge(nloc,a2,packed,y,yp,*halo)
        if degree < 3:
            halo = (lax.ppermute(shi,"gx",up), lax.ppermute(slo,"gx",down))
            new, packed = inner(nloc,a2,packed,ye,y,yp,False)
            y, yp = new, y
        else:
            sent, = inner(nloc,a2,packed,ye,y,yp,True)
    x = swap(sent,"gy").reshape(512,512)
    part = gram(x).reshape(128,4,512)
    mine = jnp.sum(swap(part,BOTH),axis=0)
    full = swap(jnp.broadcast_to(mine[None],(128,4,512)),BOTH).reshape(512,512)
    li = chol(full, 1.0/NORB)
    up = [(i,i+1) for i in range(127)]
    down = [(i+1,i) for i in range(127)]
    lo = lax.ppermute(x[:,256:],BOTH,up)
    hi = lax.ppermute(x[:,:256],BOTH,down)
    n4 = lax.dynamic_slice_in_dim(neighbors,4*gy,4,0).reshape(-1) - (32*gx+4*gy)
    s = moments(n4,gy[None],x,lo,hi,a2,orbital_grid)
    s = s.reshape(4,8,16,4,512).transpose(2,1,0,3,4).reshape(128,16,512)
    s = jnp.sum(swap(s,BOTH),axis=0)
    s = swap(jnp.broadcast_to(s[None],(16,16,512)),"gx")
    s = s.reshape(16,4,4,512).transpose(1,0,2,3).reshape(4,64,512)
    pos = jnp.stack([gx,gy])
    rows = swap(half(pos,s,li),"gy")
    projected, dipoles, spec = tile(pos,rows,li)
    q = swap(rotate(x,li),"gy")
    orthonormal = q.transpose(1,0,2).reshape(64,4096).T
    spec = jnp.sum(swap(jnp.broadcast_to(spec[None,:4],(128,4,64)),BOTH),axis=0)
    return orthonormal, projected, dipoles, spec.reshape(256)/(512.0*512.0)

def solution(mesh):
    P = jax.sharding.PartitionSpec
    return jax.shard_map(shards, mesh=mesh,
        in_specs=(P("gx",None,None,None),P("gx",None),P(None,"gx"),P("gx","gy")),
        out_specs=(P("gx","gy"),P("gx","gy"),P(None,"gx","gy"),P()),
        check_vma=False)
```

```python
import functools
import math

import jax
import jax.numpy as jnp
from jax import lax
from jax.experimental import pallas as pl
from jax.experimental.pallas import tpu as pltpu
f32=jnp.float32; bf16=jnp.bfloat16
MB=1<<20

def split(x):
    hi = x.astype(bf16)
    return hi, (x - hi.astype(f32)).astype(bf16)

def inv_chol_128(read, write):
    lane = lax.broadcasted_iota(jnp.int32,(8,128),1)
    sub = lax.broadcasted_iota(jnp.int32,(8,128),0)
    full = lambda v: jnp.broadcast_to(v,(8,128))
    m = [read(g) for g in range(16)]
    for p in range(16):
        j0 = 8*p
        d = m[p]
        c = [full(d[:,j0+l:j0+l+1]) for l in range(8)]
        s = {}; rp = []; rows = []; fin = d
        inpanel = (lane>=j0)&(lane<j0+8)
        for l in range(8):
            piv = full(c[l][l:l+1,:])
            r = 1.0/piv
            rp.append(r)
            mult = jnp.where(sub>l,c[l]*r,0.0)
            for q in range(l+1,8):
                s[l,q] = full(c[q][l:l+1,:])
                c[q] = c[q]-mult*s[l,q]
            row = jnp.where(lane==j0+l,1.0,full(d[l:l+1,:]))
            row = jnp.where(inpanel&(lane>j0+l),0.0,row)
            rows.append(row)
            d = jnp.where((lane==j0+l)&(sub>l),0.0,d)-mult*row
            fin = jnp.where(sub==l,row*lax.rsqrt(piv),fin)
        m[p] = fin
        for g in range(p+1,16):
            v = m[g]
            cg = [full(v[:,j0+l:j0+l+1]) for l in range(8)]
            v = jnp.where(inpanel,0.0,v)
            for l in range(8):
                mult = cg[l]*rp[l]
                for q in range(l+1,8):
                    cg[q] = cg[q]-mult*s[l,q]
                v = v-mult*rows[l]
            m[g] = v
    for g in range(16):
        write(g, jnp.where(lane<=sub+8*g, m[g], 0.0))

def hdot(a,b,dims):
    return lax.dot_general(a,b,(dims,((),())),precision=lax.Precision.HIGHEST,preferred_element_type=f32)

def chol_kernel(scale, pos, g_ref, o_ref, out_ref):
    c = pos[1]
    out_ref[:,pl.ds(pl.multiple_of(256*c,256),256)] = g_ref[...]*scale
    out_ref[:,pl.ds(pl.multiple_of(256-256*c,256),256)] = o_ref[...]*scale
    for k in range(4):
        k0 = 128*k
        def read(g): return out_ref[k0+8*g:k0+8*g+8,k0:k0+128]
        def write(g,v): out_ref[k0+8*g:k0+8*g+8,k0:k0+128] = v
        inv_chol_128(read,write)
        x = out_ref[128*k:128*k+128,128*k:128*k+128]
        for j in range(4):
            if j==k: continue
            out_ref[128*k:128*k+128,128*j:128*j+128] = hdot(x,out_ref[128*k:128*k+128,128*j:128*j+128],((1,),(0,)))
        bk = out_ref[128*k:128*k+128,:]
        for i in range(k+1,4):
            w = bk[:,128*i:128*i+128]
            upd = hdot(w,bk,((0,),(0,)))
            for j in range(4):
                if k<j<i: continue
                o = -upd[:,128*j:128*j+128] if j==k else out_ref[128*i:128*i+128,128*j:128*j+128]-upd[:,128*j:128*j+128]
                out_ref[128*i:128*i+128,128*j:128*j+128]=o
        for j in range(k+1,4):
            out_ref[128*k:128*k+128,128*j:128*j+128]=jnp.zeros((128,128),f32)

def chol(pos, mine, other, scale):
    V = pl.BlockSpec(memory_space=pltpu.VMEM)
    return pl.pallas_call(functools.partial(chol_kernel,scale),
        in_specs=[pl.BlockSpec(memory_space=pltpu.SMEM),V,V],
        out_shape=jax.ShapeDtypeStruct((512,512),f32), name="chol",
        cost_estimate=pl.CostEstimate(flops=8000000000,bytes_accessed=2*MB,transcendentals=0),
        compiler_params=pltpu.CompilerParams(vmem_limit_bytes=24*MB))(pos,mine,other)

def dup_pack(y):
    lane = lax.broadcasted_iota(jnp.int32,y.shape,1)
    hi = y.astype(bf16).astype(f32)
    return jnp.where(lane<64, hi, y-hi).astype(bf16)

def prep_kernel(h_ref, v_ref, a2_ref, y_ref, p_ref):
    for r in range(4):
        for k in range(5):
            hi, lo = split(h_ref[r,k])
            a2_ref[r,0:128,128*k:128*k+128] = hi
            a2_ref[r,128:256,128*k:128*k+128] = lo
    v = v_ref[...]
    y = jnp.concatenate([v,v],axis=0).T
    y_ref[...] = y
    p_ref[...] = dup_pack(y)

def prep(h, vt):
    return pl.pallas_call(prep_kernel, grid=(8,), name="prep",
        in_specs=[pl.BlockSpec((4,5,128,128),lambda g:(g,0,0,0)), pl.BlockSpec((64,512),lambda g:(0,g))],
        out_specs=[pl.BlockSpec((4,256,640),lambda g:(g,0,0)), pl.BlockSpec((512,128),lambda g:(g,0)), pl.BlockSpec((512,128),lambda g:(g,0))],
        out_shape=[jax.ShapeDtypeStruct((32,256,640),bf16), jax.ShapeDtypeStruct((4096,128),f32), jax.ShapeDtypeStruct((4096,128),bf16)],
        cost_estimate=pl.CostEstimate(flops=1000000,bytes_accessed=25*MB,transcendentals=0),
        compiler_params=pltpu.CompilerParams(vmem_limit_bytes=56*MB))(h,vt)

def halo_prep_kernel(lo_ref, hi_ref, a2_ref, y_ref, p_ref):
    for s, ref in ((0,lo_ref),(1,hi_ref)):
        for r in range(2):
            for k in range(5):
                at = 128*(5*r+k)
                hi, lo = split(ref[at:at+128,:])
                a2_ref[2*s+r,0:128,128*k:128*k+128] = hi
                a2_ref[2*s+r,128:256,128*k:128*k+128] = lo
        for b in range(4):
            v = ref[1280+64*b:1344+64*b,:]
            y = jnp.concatenate([v,v],axis=0).T
            p_ref[512*s+128*b:512*s+128*b+128,:] = dup_pack(y)
            e = b-2 if s==0 else b
            if 0<=e<2: y_ref[256*s+128*e:256*s+128*e+128,:] = y

def halo_prep(lo, hi):
    return pl.pallas_call(halo_prep_kernel, name="halo_prep",
        out_shape=[jax.ShapeDtypeStruct((4,256,640),bf16), jax.ShapeDtypeStruct((512,128),f32), jax.ShapeDtypeStruct((1024,128),bf16)],
        cost_estimate=pl.CostEstimate(flops=1000000,bytes_accessed=4*MB,transcendentals=0),
        compiler_params=pltpu.CompilerParams(vmem_limit_bytes=16*MB))(lo,hi)

def unpack_kernel(lo_ref, hi_ref, y_ref, p_ref):
    lane = lax.broadcasted_iota(jnp.int32,(128,128),1)
    for s, ref in ((0,lo_ref),(1,hi_ref)):
        for h in range(2):
            x = ref[128*h:128*h+128,:]; xr = pltpu.roll(x,64,1)
            pair = (jnp.where(lane<64,x,xr),jnp.where(lane<64,xr,x))
            for w in range(2):
                b = 2*h+w
                p_ref[512*s+128*b:512*s+128*b+128,:] = dup_pack(pair[w])
                e = b-2 if s==0 else b
                if 0<=e<2: y_ref[256*s+128*e:256*s+128*e+128,:] = pair[w]

def unpack(lo, hi):
    return pl.pallas_call(unpack_kernel, name="unpack",
        out_shape=[jax.ShapeDtypeStruct((512,128),f32), jax.ShapeDtypeStruct((1024,128),bf16)],
        cost_estimate=pl.CostEstimate(flops=1000000,bytes_accessed=MB,transcendentals=0),
        compiler_params=pltpu.CompilerParams(vmem_limit_bytes=16*MB))(lo,hi)

C0, HALF = -0.3, 0.9

def apply_row(a2, pieces):
    rhs = jnp.concatenate(pieces,axis=0)
    res = jnp.dot(a2, rhs, preferred_element_type=f32)
    u = res[:128]+res[128:]
    return u + pltpu.roll(u, 64, 1)

def recur(hy, y, yp):
    t = (hy - C0*y)/HALF
    return t if yp is None else 2.0*t - yp

def block(ref, slot):
    return ref[pl.ds(pl.multiple_of(slot*128,128),128),:]

def step_kernel(first, wide, last, ns, a2, a2h, p, ph, y, yh, *rest):
    rest = list(rest); ext = rest.pop()
    yp = yph = None
    if not first:
        yp = rest.pop(0); yph = rest.pop(0)
    outs = rest
    g = pl.program_id(0)
    @pl.when(g==0)
    def _():
        ext[0:4096,:] = p[...]
        if wide: ext[4096:5120,:] = ph[...]
        else: ext[4352:4864,:] = ph[...]
    @pl.when(g<8)
    def _():
        for r in range(4):
            hy = apply_row(a2[r],[block(ext,ns[20*g+5*r+k]) for k in range(5)])
            sl = slice(128*r,128*r+128)
            new = recur(hy,y[sl,:],None if first else yp[sl,:])
            if last:
                outs[0][0,:,sl] = new.T[:64]
            else:
                outs[0][sl,:] = new
                outs[1][sl,:] = dup_pack(new)
    if wide:
        @pl.when(g==8)
        def _():
            for r in range(4):
                hy = apply_row(a2h[r],[block(ext,ns[160+5*r+k]) for k in range(5)])
                sl = slice(128*r,128*r+128)
                new = recur(hy,yh[sl,:],None if first else yph[sl,:])
                outs[2][sl,:] = new
                outs[3][sl,:] = dup_pack(new)

def step(ns, a2, a2h, p, ph, y, yh, yp=None, yph=None, wide=False, last=False):
    first = yp is None
    B = pl.BlockSpec
    at = lambda g: jnp.minimum(g,7)
    w = lambda *shape: B(shape, lambda g,n: (0,)*len(shape))
    yb = B((512,128),lambda g,n:(at(g),0))
    sds = jax.ShapeDtypeStruct
    if last:
        outs=[B((1,64,512),lambda g,n:(at(g),0,0))]; shapes=[sds((8,64,512),f32)]
    else:
        outs=[yb,yb]; shapes=[sds((4096,128),f32),sds((4096,128),bf16)]
    if wide:
        outs+=[w(512,128)]*2; shapes+=[sds((512,128),f32),sds((512,128),bf16)]
    return pl.pallas_call(functools.partial(step_kernel,first,wide,last), name="step",
        grid_spec=pltpu.PrefetchScalarGridSpec(num_scalar_prefetch=1, grid=(9 if wide else 8,),
            in_specs=[B((4,256,640),lambda g,n:(at(g),0,0)), w(4,256,640), w(4096,128), w(*ph.shape), yb, w(512,128)]+([] if first else [yb,w(512,128)]),
            out_specs=outs, scratch_shapes=[pltpu.VMEM((5120,128),bf16)]),
        out_shape=shapes,
        cost_estimate=pl.CostEstimate(flops=36*2*256*640*128*4,bytes_accessed=16*MB,transcendentals=0),
        compiler_params=pltpu.CompilerParams(vmem_limit_bytes=24*MB))(
            ns,a2,a2h,p,ph,y,yh,*([] if first else [yp,yph]))

def edge_kernel(ne, alo, ahi, vlo, vhi, ph, ylo, yhi, plo, phi, ye, slo, shi, ext):
    lane = lax.broadcasted_iota(jnp.int32,(128,128),1)
    ext[0:256,:] = ph[0:256,:]
    ext[256:1024,:] = vlo[0:768,:]
    ext[1024:1792,:] = vhi[256:1024,:]
    ext[1792:2048,:] = ph[256:512,:]
    new = []
    for e in range(8):
        a, yr, pr = (alo,ylo,plo) if e<4 else (ahi,yhi,phi)
        hy = apply_row(a[e%4],[block(ext,ne[5*e+k]) for k in range(5)])
        sl = slice(128*(e%4),128*(e%4)+128)
        new.append(recur(hy,yr[sl,:],pr[sl,:]))
        ye[128*e:128*e+128,:] = new[-1]
    for h in range(2):
        slo[128*h:128*h+128,:] = jnp.where(lane<64,new[2*h],new[2*h+1])
        shi[128*h:128*h+128,:] = jnp.where(lane<64,new[4+2*h],new[5+2*h])

def edge(ne, a2, p, ph, y, yp):
    B = pl.BlockSpec
    w = lambda shape,*idx: B(shape, lambda g,n: idx)
    ys = [w((512,128),0,0), w((512,128),7,0)]
    sds = jax.ShapeDtypeStruct
    return pl.pallas_call(edge_kernel, name="edge",
        grid_spec=pltpu.PrefetchScalarGridSpec(num_scalar_prefetch=1, grid=(1,),
            in_specs=[w((4,256,640),0,0,0), w((4,256,640),7,0,0), w((1024,128),0,0), w((1024,128),3,0), w((512,128),0,0)]+ys+ys,
            out_specs=[w((1024,128),0,0), w((256,128),0,0), w((256,128),0,0)],
            scratch_shapes=[pltpu.VMEM((2048,128),bf16)]),
        out_shape=[sds((1024,128),f32)]+[sds((256,128),f32)]*2,
        cost_estimate=pl.CostEstimate(flops=8*2*256*640*128,bytes_accessed=5*MB,transcendentals=0),
        compiler_params=pltpu.CompilerParams(vmem_limit_bytes=24*MB))(
            ne,a2,a2,p,p,ph,y,y,yp,yp)

def inner_kernel(ns, a2, p, ye, y, yp, yo, po):
    g = pl.program_id(0)
    @pl.when((g==0)|(g==7))
    def _():
        new = ye[...]
        yo[...] = new
        po[...] = dup_pack(new)
    @pl.when((g>0)&(g<7))
    def _():
        for r in range(4):
            hy = apply_row(a2[r],[block(p,ns[20*g+5*r+k]) for k in range(5)])
            sl = slice(128*r,128*r+128)
            new = recur(hy,y[sl,:],yp[sl,:])
            yo[sl,:] = new
            po[sl,:] = dup_pack(new)

def inner(ns, a2, p, ye, y, yp):
    B = pl.BlockSpec
    yb = B((512,128),lambda g,n:(g,0))
    sds = jax.ShapeDtypeStruct
    return pl.pallas_call(inner_kernel, name="inner",
        grid_spec=pltpu.PrefetchScalarGridSpec(num_scalar_prefetch=1, grid=(8,),
            in_specs=[B((4,256,640),lambda g,n:(g,0,0)), B((4096,128),lambda g,n:(0,0)), B((512,128),lambda g,n:(g//7,0)), yb, yb],
            out_specs=[yb,yb]),
        out_shape=[sds((4096,128),f32),sds((4096,128),bf16)],
        cost_estimate=pl.CostEstimate(flops=24*2*256*640*128*4,bytes_accessed=16*MB,transcendentals=0),
        compiler_params=pltpu.CompilerParams(vmem_limit_bytes=24*MB))(ns,a2,p,ye,y,yp)

NT = ((1,),(1,))
NN = ((1,),(0,))
NORB = 65536

def bdot(a, b, dims):
    return lax.dot_general(a,b,(dims,((),())),preferred_element_type=f32)

def params(mb):
    return pltpu.CompilerParams(vmem_limit_bytes=mb*MB)

SMEM = pl.BlockSpec(memory_space=pltpu.SMEM)
VMEM = pl.BlockSpec(memory_space=pltpu.VMEM)

def gram_kernel(pos, x_ref, o_ref, g_ref):
    half = pl.ds(pl.multiple_of(256*pos[1],256),256)
    xs = [split(x_ref[...]),split(o_ref[...])]
    hs = [split(x_ref[half,:]),split(o_ref[half,:])]
    for i in range(2):
        sl = slice(256*i,256*i+256)
        s = None
        for (xh,xl),(hh,hl) in zip(xs,hs):
            t = bdot(xh[sl],hh,NT)+bdot(xl[sl],hh,NT)+bdot(xh[sl],hl,NT)
            s = t if s is None else s+t
        g_ref[32*i:32*i+32] = s.reshape(32,8,256)

def gram(pos, x, o):
    return pl.pallas_call(gram_kernel, out_shape=jax.ShapeDtypeStruct((64,8,256),f32), name="gram",
        in_specs=[SMEM,VMEM,VMEM],
        cost_estimate=pl.CostEstimate(flops=3*2*512**3,bytes_accessed=3*MB,transcendentals=0),
        compiler_params=params(16))(pos,x,o)

def applied_kernel(n4, gy, x_ref, lo_ref, hi_ref, a2, yt, xh, xl):
    for ref, at, w in ((lo_ref,0,256),(x_ref,256,512),(hi_ref,768,256)):
        h, l = split(ref[...])
        xh[:,at:at+w] = h; xl[:,at:at+w] = l
    for i in range(4):
        at = [pl.ds(pl.multiple_of((n4[5*i+k]+2)*128,128),128) for k in range(5)]
        h = jnp.concatenate([xh[:,a] for a in at],axis=1)
        l = jnp.concatenate([xl[:,a] for a in at],axis=1)
        r = bdot(h,a2[0,i],NT)
        yt[:,128*i:128*i+128] = r[:,:128]+r[:,128:]+bdot(l,a2[0,i,:128,:],NT)

def applied(n4, gy, x, lo, hi, a2):
    B = pl.BlockSpec
    w = lambda shape: B(shape, lambda g,n,y: (0,)*len(shape))
    return pl.pallas_call(applied_kernel, name="applied",
        grid_spec=pltpu.PrefetchScalarGridSpec(num_scalar_prefetch=2, grid=(1,),
            in_specs=[w((512,512)),w((512,256)),w((512,256)),B((1,4,256,640),lambda g,n,y:(y[0],0,0,0))],
            out_specs=w((512,512)),
            scratch_shapes=[pltpu.VMEM((512,1024),bf16),pltpu.VMEM((512,1024),bf16)]),
        out_shape=jax.ShapeDtypeStruct((512,512),f32),
        cost_estimate=pl.CostEstimate(flops=4*2*512*512*640,bytes_accessed=5*MB,transcendentals=0),
        compiler_params=params(56))(n4,gy,x,lo,hi,a2.reshape(8,4,256,640))

def moment_kernel(pos, x_ref, o_ref, yt_ref, ot_ref, g_ref, og_ref, s_ref):
    c = pos[1]
    xs = [split(x_ref[...]),split(o_ref[...])]
    for q in range(2):
        ws = []
        for x, y, g in ((x_ref,yt_ref,g_ref),(o_ref,ot_ref,og_ref)):
            places = (g[...]+0.5)/32.0-1.0
            if q==0:
                w = jnp.where(c==0,y[...],x[...]*places[1:2,:])
            else:
                w = x[...]*jnp.where(c==0,places[0:1,:],places[2:3,:])
            ws.append(split(w))
        for i in range(2):
            sl = slice(256*i,256*i+256)
            s = None
            for (xh,xl),(yh,yl) in zip(xs,ws):
                t = bdot(xh[sl],yh,NT)+bdot(xl[sl],yh,NT)+bdot(xh[sl],yl,NT)
                s = t if s is None else s+t
            s_ref[32*i:32*i+32,8*q:8*q+8,:] = s.reshape(32,8,512)

def moments(pos, x, o, yt, ot, g, og):
    return pl.pallas_call(moment_kernel, name="moments", in_specs=[SMEM]+[VMEM]*6,
        out_shape=jax.ShapeDtypeStruct((64,16,512),f32),
        cost_estimate=pl.CostEstimate(flops=12*2*512**3,bytes_accessed=8*MB,transcendentals=0),
        compiler_params=params(40))(pos,x,o,yt,ot,g,og)

def half_kernel(pos, s_ref, li_ref, out_ref):
    lane = lax.broadcasted_iota(jnp.int32,(8,128),1)
    sub = lax.broadcasted_iota(jnp.int32,(8,128),0)
    z = hdot(s_ref[...],li_ref[...],NT)
    z0 = z[0:8]; z1 = z[8:16]
    k8 = 8*(8*pos[0]+pos[2])
    pick = (lax.broadcasted_iota(jnp.int32,(8,512),1)==lax.broadcasted_iota(jnp.int32,(8,512),0)+k8).astype(f32)
    e = jnp.sum(z0*hdot(pick,li_ref[...],NT),axis=0,keepdims=True)
    ee = jnp.zeros((8,128),f32)
    for g in range(8):
        b = jnp.broadcast_to(e[:,128*(g//2):128*(g//2)+128],(8,128))
        if g%2==0: b = pltpu.roll(b,64,1)
        ee = jnp.where(sub==g,b,ee)
    for u in range(4):
        for v in range(4):
            a = z0[:,128*u:128*u+128]; b = z1[:,128*u:128*u+128]
            if v: a = pltpu.roll(a,128-32*v,1)
            if v!=1: b = pltpu.roll(b,(160-32*v)%128,1)
            t = jnp.where(lane<32,a,jnp.where(lane<64,b,ee))
            for y in range(8):
                out_ref[8*(4*u+v)+y] = t

def half(pos, s, li):
    return pl.pallas_call(half_kernel, name="half", in_specs=[SMEM,VMEM,VMEM],
        out_shape=jax.ShapeDtypeStruct((128,8,128),f32),
        cost_estimate=pl.CostEstimate(flops=2*24*512*512*6,bytes_accessed=2*MB,transcendentals=0),
        compiler_params=params(16))(pos,s,li)

def tile_kernel(pos, r_ref, li_ref, p_ref, d_ref, w_ref, e_ref, acc):
    c = pos[1]; gx = 2*pos[0]+c; gy = pos[2]
    lane = lax.broadcasted_iota(jnp.int32,(64,128),1)
    lane8 = lax.broadcasted_iota(jnp.int32,(8,128),1)
    lb = li_ref[pl.ds(pl.multiple_of(64*gy,64),64),:]
    t0 = hdot(lb,r_ref[:,0].reshape(512,128),NN)
    t1 = hdot(lb,r_ref[:,1].reshape(512,128),NN)
    t = jnp.where(lane<64,t0,pltpu.roll(t1,64,1))
    tt = jnp.concatenate([t,t],axis=0).T
    p_ref[...] = tt[0:32,0:64]*(1.0/NORB)
    for q in range(3):
        d_ref[q] = tt[32*q+32:32*q+64,0:64]*(1.0/math.sqrt(NORB))
    e = jnp.sum(r_ref[:,0].reshape(64,8,128),axis=0)
    e_ref[...] = e*(1.0/NORB)
    ea = jnp.broadcast_to(e_ref[pl.ds(pos[0],1),:],(8,128))
    ea = pltpu.roll(ea,64-32*c,1)
    ea = jnp.where(lane8<32,ea,0.0)
    ea = ea+pltpu.roll(ea,32,1)+pltpu.roll(ea,64,1)+pltpu.roll(ea,96,1)
    eb = pltpu.roll(jnp.broadcast_to(e_ref[pl.ds(gy,1),:],(8,128)),64,1)
    eb = jnp.broadcast_to(eb[0:1,:],(128,128)).T[0:64,:]
    gap = eb-jnp.broadcast_to(ea[0:1,:],(64,128))
    dip = t*(1.0/math.sqrt(NORB))
    sq = jnp.where(lane>=32,dip*dip,0.0)
    st = (sq+pltpu.roll(sq,32,1)+pltpu.roll(sq,64,1)+pltpu.roll(sq,96,1))*(0.01/math.pi)
    base = (64*(lane8//32)).astype(f32)+0.5
    for w in range(64):
        om = -0.3+0.6*(base+float(w))/256.0
        tot = jnp.zeros((8,128),f32)
        for b in range(8):
            x = om-gap[8*b:8*b+8,:]
            tot = tot+st[8*b:8*b+8,:]/(x*x+0.0001)
        acc[w:w+1,:] = jnp.sum(tot,axis=0,keepdims=True)
    sel = (lane8//32==lax.broadcasted_iota(jnp.int32,(8,128),0)).astype(f32)
    m = hdot(sel,jnp.concatenate([acc[...],acc[...]],axis=0),NT)*(1.0/(512.0*512.0))
    m = jnp.concatenate([jnp.where(lane8[0:1]<64,m[0:1],m[1:2]),jnp.where(lane8[0:1]<64,m[2:3],m[3:4])],axis=0)
    w_ref[...] = jnp.broadcast_to(m[None],(128,2,128))

def tile(pos, r, li):
    sds = jax.ShapeDtypeStruct
    return pl.pallas_call(tile_kernel, name="tile", in_specs=[SMEM,VMEM,VMEM], out_specs=[VMEM]*3,
        out_shape=[sds((32,64),f32),sds((3,32,64),f32),sds((128,2,128),f32)],
        scratch_shapes=[pltpu.VMEM((8,128),f32),pltpu.VMEM((64,128),f32)],
        cost_estimate=pl.CostEstimate(flops=10000000,bytes_accessed=2*MB,transcendentals=0),
        compiler_params=params(16))(pos,r,li)

def rotate_kernel(x_ref, li_ref, o_ref):
    xh, xl = split(x_ref[...])
    for i in range(2):
        lh, ll = split(li_ref[256*i:256*i+256,:])
        o_ref[4*i:4*i+4] = (bdot(lh,xh,NN)+bdot(ll,xh,NN)+bdot(lh,xl,NN)).reshape(4,64,512)

def rotate(x, li):
    return pl.pallas_call(rotate_kernel, out_shape=jax.ShapeDtypeStruct((8,64,512),f32), name="rotate",
        cost_estimate=pl.CostEstimate(flops=3*2*512**3,bytes_accessed=3*MB,transcendentals=0),
        compiler_params=params(16))(x,li)

SLABS = ("gq","c")
PEERS = ("gq","gy")
ALL = ("gq","c","gy")

def swap(x, axis):
    return lax.all_to_all(x,axis,split_axis=0,concat_axis=0,tiled=True)

def chain(n):
    return [(i,i+1) for i in range(n-1)], [(i+1,i) for i in range(n-1)]

def shards(hopping_blocks, neighbors, orbital_grid, trial_block):
    gq = lax.axis_index("gq"); c = lax.axis_index("c"); gy = lax.axis_index("gy")
    gx = 2*gq+c
    pos = jnp.stack([gq,c,gy])
    up, down = chain(16)
    vt = trial_block.T
    grid = lax.dynamic_slice_in_dim(orbital_grid,512*gy,512,1).astype(f32)
    near = neighbors.astype(f32)

    def payload(row, col):
        v = vt[:,col:col+512].reshape(64,4,128).transpose(1,0,2).reshape(256,128)
        n = jnp.pad(near[row:row+2].reshape(1,10),((0,0),(0,118)))
        return jnp.concatenate([hopping_blocks[row:row+2].reshape(1280,128),v,n,grid.reshape(12,128),jnp.zeros((3,128),f32)],axis=0)

    lo = lax.ppermute(payload(30,3584),SLABS,up)
    hi = lax.ppermute(payload(0,0),SLABS,down)
    a2, y0, p0 = prep(hopping_blocks, vt)
    a2h, y0h, p0h = halo_prep(lo,hi)
    other_grid = jnp.where(c==0,hi[1537:1549],lo[1537:1549]).reshape(3,512)
    halo_near = jnp.concatenate([lo[1536,:10].reshape(2,5),hi[1536,:10].reshape(2,5)],axis=0).astype(jnp.int32)
    n = jnp.clip(jnp.concatenate([neighbors,halo_near],axis=0)-32*gx,-4,35)
    ns = jnp.where(n<0,n+36,jnp.where(n>=32,n+4,n)).reshape(-1)
    ne = jnp.concatenate([n[0:4]+2,n[28:32]-18],axis=0).reshape(-1)

    y1, p1, y1h, p1h = step(ns,a2,a2h,p0,p0h,y0,y0h,wide=True)
    ye, slo, shi = edge(ne,a2,p1,p1h,y1,y0)
    lo = lax.ppermute(shi,SLABS,up)
    hi = lax.ppermute(slo,SLABS,down)
    y2, p2 = inner(ns,a2,p1,ye,y1,y0)
    y2h, p2h = unpack(lo,hi)
    y3, p3, y3h, p3h = step(ns,a2,a2h,p2,p2h,y2,y2h,y1,y1h,wide=True)
    sent, = step(ns,a2,a2h,p3,p3h,y3,y3h,y2,y2h,last=True)

    x = swap(sent,"gy").reshape(512,512)
    pair = [(i,i^1) for i in range(16)]
    other = lax.ppermute(x,SLABS,pair)
    part = gram(pos,x,other)
    mine = jnp.sum(swap(part,PEERS),axis=0)
    up, down = chain(128)
    lo = lax.ppermute(x[:,256:],ALL,up)
    hi = lax.ppermute(x[:,:256],ALL,down)
    n4 = lax.dynamic_slice_in_dim(neighbors,4*gy,4,0).reshape(-1) - (32*gx+4*gy)
    yt = applied(n4,gy[None],x,lo,hi,a2)
    ot = lax.ppermute(yt,SLABS,pair)
    ga = swap(jnp.broadcast_to(mine[None],(64,8,256)),PEERS).reshape(512,256)
    ot, mine = lax.optimization_barrier((ot,mine))
    s = moments(pos,x,other,yt,ot,grid,other_grid)
    gb = lax.ppermute(ga,SLABS,pair)
    s, gb = lax.optimization_barrier((s,gb))
    li = chol(pos,ga,gb,1.0/NORB)
    s = jnp.sum(swap(s,PEERS),axis=0)
    rows = swap(half(pos,s,li),ALL).reshape(8,2,64,128)
    projected, dipoles, spec = tile(pos,rows,li)
    q = swap(rotate(x,li),"gy")
    orthonormal = q.transpose(1,0,2).reshape(64,4096).T
    spectrum = jnp.sum(swap(spec,ALL),axis=0).reshape(256)
    return orthonormal, projected, dipoles, spectrum

def solution(mesh):
    P = jax.sharding.PartitionSpec
    fine = jax.sharding.Mesh(mesh.devices.reshape(8,2,8),ALL)
    return jax.shard_map(shards, mesh=fine,
        in_specs=(P(SLABS,None,None,None),P(SLABS,None),P(None,SLABS),P(SLABS,"gy")),
        out_specs=(P(SLABS,"gy"),P(SLABS,"gy"),P(None,SLABS,"gy"),P()),
        check_vma=False)
```

```python
import functools
import math

import jax
import jax.numpy as jnp
from jax import lax
from jax.experimental import pallas as pl
from jax.experimental.pallas import tpu as pltpu
f32=jnp.float32; bf16=jnp.bfloat16
MB=1<<20

def split(x):
    hi = x.astype(bf16)
    return hi, (x - hi.astype(f32)).astype(bf16)

def inv_chol_128(read, write):
    lane = lax.broadcasted_iota(jnp.int32,(8,128),1)
    sub = lax.broadcasted_iota(jnp.int32,(8,128),0)
    full = lambda v: jnp.broadcast_to(v,(8,128))
    m = [read(g) for g in range(16)]
    for p in range(16):
        j0 = 8*p
        d = m[p]
        c = [full(d[:,j0+l:j0+l+1]) for l in range(8)]
        s = {}; rp = []; rows = []; fin = d
        inpanel = (lane>=j0)&(lane<j0+8)
        for l in range(8):
            piv = full(c[l][l:l+1,:])
            r = 1.0/piv
            rp.append(r)
            mult = jnp.where(sub>l,c[l]*r,0.0)
            for q in range(l+1,8):
                s[l,q] = full(c[q][l:l+1,:])
                c[q] = c[q]-mult*s[l,q]
            row = jnp.where(lane==j0+l,1.0,full(d[l:l+1,:]))
            row = jnp.where(inpanel&(lane>j0+l),0.0,row)
            rows.append(row)
            d = jnp.where((lane==j0+l)&(sub>l),0.0,d)-mult*row
            fin = jnp.where(sub==l,row*lax.rsqrt(piv),fin)
        m[p] = fin
        for g in range(p+1,16):
            v = m[g]
            cg = [full(v[:,j0+l:j0+l+1]) for l in range(8)]
            v = jnp.where(inpanel,0.0,v)
            for l in range(8):
                mult = cg[l]*rp[l]
                for q in range(l+1,8):
                    cg[q] = cg[q]-mult*s[l,q]
                v = v-mult*rows[l]
            m[g] = v
    for g in range(16):
        write(g, jnp.where(lane<=sub+8*g, m[g], 0.0))

def hdot(a,b,dims):
    return lax.dot_general(a,b,(dims,((),())),precision=lax.Precision.HIGHEST,preferred_element_type=f32)

def chol_kernel(scale, pos, g_ref, o_ref, out_ref):
    c = pos[1]
    out_ref[:,pl.ds(pl.multiple_of(256*c,256),256)] = g_ref[...]*scale
    out_ref[:,pl.ds(pl.multiple_of(256-256*c,256),256)] = o_ref[...]*scale
    for k in range(4):
        k0 = 128*k
        def read(g): return out_ref[k0+8*g:k0+8*g+8,k0:k0+128]
        def write(g,v): out_ref[k0+8*g:k0+8*g+8,k0:k0+128] = v
        inv_chol_128(read,write)
        x = out_ref[128*k:128*k+128,128*k:128*k+128]
        for j in range(4):
            if j==k: continue
            out_ref[128*k:128*k+128,128*j:128*j+128] = hdot(x,out_ref[128*k:128*k+128,128*j:128*j+128],((1,),(0,)))
        bk = out_ref[128*k:128*k+128,:]
        for i in range(k+1,4):
            w = bk[:,128*i:128*i+128]
            upd = hdot(w,bk,((0,),(0,)))
            for j in range(4):
                if k<j<i: continue
                o = -upd[:,128*j:128*j+128] if j==k else out_ref[128*i:128*i+128,128*j:128*j+128]-upd[:,128*j:128*j+128]
                out_ref[128*i:128*i+128,128*j:128*j+128]=o
        for j in range(k+1,4):
            out_ref[128*k:128*k+128,128*j:128*j+128]=jnp.zeros((128,128),f32)

def chol(pos, mine, other, scale):
    V = pl.BlockSpec(memory_space=pltpu.VMEM)
    return pl.pallas_call(functools.partial(chol_kernel,scale),
        in_specs=[pl.BlockSpec(memory_space=pltpu.SMEM),V,V],
        out_shape=jax.ShapeDtypeStruct((512,512),f32), name="chol",
        cost_estimate=pl.CostEstimate(flops=8000000000,bytes_accessed=2*MB,transcendentals=0),
        compiler_params=pltpu.CompilerParams(vmem_limit_bytes=24*MB))(pos,mine,other)

def dup_pack(y):
    lane = lax.broadcasted_iota(jnp.int32,y.shape,1)
    hi = y.astype(bf16).astype(f32)
    return jnp.where(lane<64, hi, y-hi).astype(bf16)

def prep_kernel(pos, h_ref, v_ref, a2_ref, y_ref, p_ref, own_ref):
    for r in range(4):
        for k in range(5):
            hi, lo = split(h_ref[r,k])
            a2_ref[r,0:128,128*k:128*k+128] = hi
            a2_ref[r,128:256,128*k:128*k+128] = lo
    @pl.when(pl.program_id(0)==pos[2])
    def _():
        own_ref[...] = a2_ref[...]
    v = v_ref[...]
    y = jnp.concatenate([v,v],axis=0).T
    y_ref[...] = y
    p_ref[...] = dup_pack(y)

def prep(pos, h, vt):
    B = pl.BlockSpec
    yb = B((512,128),lambda g,n:(g,0))
    sds = jax.ShapeDtypeStruct
    return pl.pallas_call(prep_kernel, name="prep",
        grid_spec=pltpu.PrefetchScalarGridSpec(num_scalar_prefetch=1, grid=(8,),
            in_specs=[B((4,5,128,128),lambda g,n:(g,0,0,0)), B((64,512),lambda g,n:(0,g))],
            out_specs=[B((4,256,640),lambda g,n:(g,0,0)), yb, yb, B((4,256,640),lambda g,n:(0,0,0))]),
        out_shape=[sds((32,256,640),bf16), sds((4096,128),f32), sds((4096,128),bf16), sds((4,256,640),bf16)],
        cost_estimate=pl.CostEstimate(flops=1000000,bytes_accessed=25*MB,transcendentals=0),
        compiler_params=pltpu.CompilerParams(vmem_limit_bytes=24*MB))(pos,h,vt)

def payload_kernel(pos, near, ha, hb, va, vb, grid, up_ref, down_ref, g_ref):
    g = grid[...].astype(f32)
    g_ref[...] = g
    base = 32*(2*pos[0]+pos[1])
    for out, h, v, n in ((up_ref,ha,va,30),(down_ref,hb,vb,0)):
        for r in range(2):
            for k in range(5):
                o = near[n+r,k]-base-(n+r)+2
                out[pl.ds(pl.multiple_of(640*r+128*o,128),128),:] = h[r,k]
        for b in range(4):
            out[1280+64*b:1344+64*b,:] = v[:,128*b:128*b+128]
        out[1536:1568,:] = jnp.zeros((32,128),f32)
        for u in range(4):
            out[1539+8*u:1542+8*u,:] = g[:,128*u:128*u+128]

def payload(pos, near, h, vt, grid):
    B = pl.BlockSpec
    w = lambda shape,*idx: B(shape, lambda g,p,n: idx)
    sds = jax.ShapeDtypeStruct
    return pl.pallas_call(payload_kernel, name="payload",
        grid_spec=pltpu.PrefetchScalarGridSpec(num_scalar_prefetch=2, grid=(1,),
            in_specs=[w((2,5,128,128),15,0,0,0),w((2,5,128,128),0,0,0,0),w((64,512),0,7),w((64,512),0,0),B((3,512),lambda g,p,n:(0,p[2]))],
            out_specs=[w((1568,128),0,0)]*2+[w((3,512),0,0)]),
        out_shape=[sds((1568,128),f32)]*2+[sds((3,512),f32)],
        cost_estimate=pl.CostEstimate(flops=1000000,bytes_accessed=4*MB,transcendentals=0),
        compiler_params=pltpu.CompilerParams(vmem_limit_bytes=56*MB))(pos,near,h,h,vt,vt,grid)

def halo_prep_kernel(lo_ref, hi_ref, a2_ref, y_ref, p_ref):
    for s, ref in ((0,lo_ref),(1,hi_ref)):
        for r in range(2):
            for k in range(5):
                at = 128*(5*r+k)
                hi, lo = split(ref[at:at+128,:])
                a2_ref[2*s+r,0:128,128*k:128*k+128] = hi
                a2_ref[2*s+r,128:256,128*k:128*k+128] = lo
        for b in range(4):
            v = ref[1280+64*b:1344+64*b,:]
            y = jnp.concatenate([v,v],axis=0).T
            p_ref[512*s+128*b:512*s+128*b+128,:] = dup_pack(y)
            e = b-2 if s==0 else b
            if 0<=e<2: y_ref[256*s+128*e:256*s+128*e+128,:] = y

def halo_prep(lo, hi):
    return pl.pallas_call(halo_prep_kernel, name="halo_prep",
        out_shape=[jax.ShapeDtypeStruct((4,256,640),bf16), jax.ShapeDtypeStruct((512,128),f32), jax.ShapeDtypeStruct((1024,128),bf16)],
        cost_estimate=pl.CostEstimate(flops=1000000,bytes_accessed=4*MB,transcendentals=0),
        compiler_params=pltpu.CompilerParams(vmem_limit_bytes=16*MB))(lo,hi)

def unpack_kernel(lo_ref, hi_ref, y_ref, p_ref):
    lane = lax.broadcasted_iota(jnp.int32,(128,128),1)
    for s, ref in ((0,lo_ref),(1,hi_ref)):
        for h in range(2):
            x = ref[128*h:128*h+128,:]; xr = pltpu.roll(x,64,1)
            pair = (jnp.where(lane<64,x,xr),jnp.where(lane<64,xr,x))
            for w in range(2):
                b = 2*h+w
                p_ref[512*s+128*b:512*s+128*b+128,:] = dup_pack(pair[w])
                e = b-2 if s==0 else b
                if 0<=e<2: y_ref[256*s+128*e:256*s+128*e+128,:] = pair[w]

def unpack(lo, hi):
    return pl.pallas_call(unpack_kernel, name="unpack",
        out_shape=[jax.ShapeDtypeStruct((512,128),f32), jax.ShapeDtypeStruct((1024,128),bf16)],
        cost_estimate=pl.CostEstimate(flops=1000000,bytes_accessed=MB,transcendentals=0),
        compiler_params=pltpu.CompilerParams(vmem_limit_bytes=16*MB))(lo,hi)

C0, HALF = -0.3, 0.9

def apply_row(a2, pieces):
    rhs = jnp.concatenate(pieces,axis=0)
    res = jnp.dot(a2, rhs, preferred_element_type=f32)
    u = res[:128]+res[128:]
    return u + pltpu.roll(u, 64, 1)

def recur(hy, y, yp):
    t = (hy - C0*y)/HALF
    return t if yp is None else 2.0*t - yp

def local(pos, near, i, k):
    return near[i,k]-32*(2*pos[0]+pos[1])

def slot_of(n):
    return jnp.where(n<0,n+36,jnp.where(n>31,n+4,n))

HALO_SLOTS = ((32,33,34,35,0),(33,34,35,0,1),(30,31,36,37,38),(31,36,37,38,39))

def block(ref, slot):
    return ref[pl.ds(pl.multiple_of(slot*128,128),128),:]

def step_kernel(first, wide, last, pos, near, a2, a2h, p, ph, y, yh, *rest):
    rest = list(rest); ext = rest.pop()
    yp = yph = None
    if not first:
        yp = rest.pop(0); yph = rest.pop(0)
    outs = rest
    g = pl.program_id(0)
    @pl.when(g==0)
    def _():
        ext[0:4096,:] = p[...]
        if wide: ext[4096:5120,:] = ph[...]
        else: ext[4352:4864,:] = ph[...]
    @pl.when(g<8)
    def _():
        for r in range(4):
            hy = apply_row(a2[r],[block(ext,slot_of(local(pos,near,4*g+r,k))) for k in range(5)])
            sl = slice(128*r,128*r+128)
            new = recur(hy,y[sl,:],None if first else yp[sl,:])
            if last:
                outs[0][0,:,sl] = new.T[:64]
            else:
                outs[0][sl,:] = new
                outs[1][sl,:] = dup_pack(new)
    if wide:
        @pl.when(g==8)
        def _():
            for r in range(4):
                hy = apply_row(a2h[r],[ext[128*b:128*b+128,:] for b in HALO_SLOTS[r]])
                sl = slice(128*r,128*r+128)
                new = recur(hy,yh[sl,:],None if first else yph[sl,:])
                outs[2][sl,:] = new
                outs[3][sl,:] = dup_pack(new)

def step(pos, near, a2, a2h, p, ph, y, yh, yp=None, yph=None, wide=False, last=False):
    first = yp is None
    B = pl.BlockSpec
    at = lambda g: jnp.minimum(g,7)
    w = lambda *shape: B(shape, lambda g,p,n: (0,)*len(shape))
    yb = B((512,128),lambda g,p,n:(at(g),0))
    sds = jax.ShapeDtypeStruct
    if last:
        outs=[B((1,64,512),lambda g,p,n:(at(g),0,0))]; shapes=[sds((8,64,512),f32)]
    else:
        outs=[yb,yb]; shapes=[sds((4096,128),f32),sds((4096,128),bf16)]
    if wide:
        outs+=[w(512,128)]*2; shapes+=[sds((512,128),f32),sds((512,128),bf16)]
    return pl.pallas_call(functools.partial(step_kernel,first,wide,last), name="step",
        grid_spec=pltpu.PrefetchScalarGridSpec(num_scalar_prefetch=2, grid=(9 if wide else 8,),
            in_specs=[B((4,256,640),lambda g,p,n:(at(g),0,0)), w(4,256,640), w(4096,128), w(*ph.shape), yb, w(512,128)]+([] if first else [yb,w(512,128)]),
            out_specs=outs, scratch_shapes=[pltpu.VMEM((5120,128),bf16)]),
        out_shape=shapes,
        cost_estimate=pl.CostEstimate(flops=36*2*256*640*128*4,bytes_accessed=16*MB,transcendentals=0),
        compiler_params=pltpu.CompilerParams(vmem_limit_bytes=24*MB))(
            pos,near,a2,a2h,p,ph,y,yh,*([] if first else [yp,yph]))

def edge_kernel(pos, near, alo, ahi, vlo, vhi, ph, ylo, yhi, plo, phi, ye, slo, shi, ext):
    lane = lax.broadcasted_iota(jnp.int32,(128,128),1)
    ext[0:256,:] = ph[0:256,:]
    ext[256:1024,:] = vlo[0:768,:]
    ext[1024:1792,:] = vhi[256:1024,:]
    ext[1792:2048,:] = ph[256:512,:]
    new = []
    for e in range(8):
        a, yr, pr = (alo,ylo,plo) if e<4 else (ahi,yhi,phi)
        hy = apply_row(a[e%4],[block(ext,local(pos,near,e if e<4 else 24+e,k)+(2 if e<4 else -18)) for k in range(5)])
        sl = slice(128*(e%4),128*(e%4)+128)
        new.append(recur(hy,yr[sl,:],pr[sl,:]))
        ye[128*e:128*e+128,:] = new[-1]
    for h in range(2):
        slo[128*h:128*h+128,:] = jnp.where(lane<64,new[2*h],new[2*h+1])
        shi[128*h:128*h+128,:] = jnp.where(lane<64,new[4+2*h],new[5+2*h])

def edge(pos, near, a2, p, ph, y, yp):
    B = pl.BlockSpec
    w = lambda shape,*idx: B(shape, lambda g,p,n: idx)
    ys = [w((512,128),0,0), w((512,128),7,0)]
    sds = jax.ShapeDtypeStruct
    return pl.pallas_call(edge_kernel, name="edge",
        grid_spec=pltpu.PrefetchScalarGridSpec(num_scalar_prefetch=2, grid=(1,),
            in_specs=[w((4,256,640),0,0,0), w((4,256,640),7,0,0), w((1024,128),0,0), w((1024,128),3,0), w((512,128),0,0)]+ys+ys,
            out_specs=[w((1024,128),0,0), w((256,128),0,0), w((256,128),0,0)],
            scratch_shapes=[pltpu.VMEM((2048,128),bf16)]),
        out_shape=[sds((1024,128),f32)]+[sds((256,128),f32)]*2,
        cost_estimate=pl.CostEstimate(flops=8*2*256*640*128,bytes_accessed=5*MB,transcendentals=0),
        compiler_params=pltpu.CompilerParams(vmem_limit_bytes=24*MB))(
            pos,near,a2,a2,p,p,ph,y,y,yp,yp)

def inner_kernel(pos, near, a2, p, ye, y, yp, yo, po):
    g = pl.program_id(0)
    @pl.when((g==0)|(g==7))
    def _():
        new = ye[...]
        yo[...] = new
        po[...] = dup_pack(new)
    @pl.when((g>0)&(g<7))
    def _():
        for r in range(4):
            hy = apply_row(a2[r],[block(p,local(pos,near,4*g+r,k)) for k in range(5)])
            sl = slice(128*r,128*r+128)
            new = recur(hy,y[sl,:],yp[sl,:])
            yo[sl,:] = new
            po[sl,:] = dup_pack(new)

def inner(pos, near, a2, p, ye, y, yp):
    B = pl.BlockSpec
    yb = B((512,128),lambda g,p,n:(g,0))
    sds = jax.ShapeDtypeStruct
    return pl.pallas_call(inner_kernel, name="inner",
        grid_spec=pltpu.PrefetchScalarGridSpec(num_scalar_prefetch=2, grid=(8,),
            in_specs=[B((4,256,640),lambda g,p,n:(g,0,0)), B((4096,128),lambda g,p,n:(0,0)), B((512,128),lambda g,p,n:(g//7,0)), yb, yb],
            out_specs=[yb,yb]),
        out_shape=[sds((4096,128),f32),sds((4096,128),bf16)],
        cost_estimate=pl.CostEstimate(flops=24*2*256*640*128*4,bytes_accessed=16*MB,transcendentals=0),
        compiler_params=pltpu.CompilerParams(vmem_limit_bytes=24*MB))(pos,near,a2,p,ye,y,yp)

NT = ((1,),(1,))
NN = ((1,),(0,))
NORB = 65536

def bdot(a, b, dims):
    return lax.dot_general(a,b,(dims,((),())),preferred_element_type=f32)

def params(mb):
    return pltpu.CompilerParams(vmem_limit_bytes=mb*MB)

SMEM = pl.BlockSpec(memory_space=pltpu.SMEM)
VMEM = pl.BlockSpec(memory_space=pltpu.VMEM)

def gram_kernel(pos, x_ref, o_ref, g_ref):
    half = pl.ds(pl.multiple_of(256*pos[1],256),256)
    xs = [split(x_ref[...]),split(o_ref[...])]
    hs = [split(x_ref[half,:]),split(o_ref[half,:])]
    for i in range(2):
        sl = slice(256*i,256*i+256)
        s = None
        for (xh,xl),(hh,hl) in zip(xs,hs):
            t = bdot(xh[sl],hh,NT)+bdot(xl[sl],hh,NT)+bdot(xh[sl],hl,NT)
            s = t if s is None else s+t
        g_ref[32*i:32*i+32] = s.reshape(32,8,256)

def gram(pos, x, o):
    return pl.pallas_call(gram_kernel, out_shape=jax.ShapeDtypeStruct((64,8,256),f32), name="gram",
        in_specs=[SMEM,VMEM,VMEM],
        cost_estimate=pl.CostEstimate(flops=3*2*512**3,bytes_accessed=3*MB,transcendentals=0),
        compiler_params=params(16))(pos,x,o)

def applied_kernel(pos, near, x_ref, hi_ref, a2, yt, xh, xl):
    for ref, at, w in ((x_ref,0,512),(hi_ref,512,256)):
        h, l = split(ref[...])
        xh[:,at:at+w] = h; xl[:,at:at+w] = l
    xh[:,512:768] = xh[:,512:768]*2; xl[:,512:768] = xl[:,512:768]*2
    xh[:,768:896] = jnp.zeros((512,128),bf16); xl[:,768:896] = jnp.zeros((512,128),bf16)
    for i in range(4):
        n = [local(pos,near,4*pos[2]+i,k)-4*pos[2] for k in range(5)]
        at = [pl.ds(pl.multiple_of(jnp.where(m<0,6,m)*128,128),128) for m in n]
        h = jnp.concatenate([xh[:,a] for a in at],axis=1)
        l = jnp.concatenate([xl[:,a] for a in at],axis=1)
        r = bdot(h,a2[i],NT)
        yt[:,128*i:128*i+128] = r[:,:128]+r[:,128:]+bdot(l,a2[i,:128,:],NT)

def applied(pos, near, x, hi, a2):
    B = pl.BlockSpec
    w = lambda shape: B(shape, lambda g,p,n: (0,)*len(shape))
    return pl.pallas_call(applied_kernel, name="applied",
        grid_spec=pltpu.PrefetchScalarGridSpec(num_scalar_prefetch=2, grid=(1,),
            in_specs=[w((512,512)),w((512,256)),w((4,256,640))],
            out_specs=w((512,512)),
            scratch_shapes=[pltpu.VMEM((512,896),bf16),pltpu.VMEM((512,896),bf16)]),
        out_shape=jax.ShapeDtypeStruct((512,512),f32),
        cost_estimate=pl.CostEstimate(flops=4*2*512*512*640,bytes_accessed=5*MB,transcendentals=0),
        compiler_params=params(24))(pos,near,x,hi,a2)

def moment_kernel(pos, x_ref, o_ref, yt_ref, ot_ref, g_ref, lo_ref, hi_ref, s_ref, acc):
    c = pos[1]
    xs = [split(x_ref[...]),split(o_ref[...])]
    tail = jnp.where(c==0,hi_ref[...],lo_ref[...])
    og = jnp.concatenate([tail[8*u+3:8*u+6,:] for u in range(4)],axis=1)
    for q in range(2):
        ws = []
        for x, y, g in ((x_ref,yt_ref,g_ref[...]),(o_ref,ot_ref,og)):
            places = (g+0.5)/32.0-1.0
            if q==0:
                w = jnp.where(c==0,y[...],x[...]*places[1:2,:])
            else:
                w = x[...]*jnp.where(c==0,places[0:1,:],places[2:3,:])
            ws.append(split(w))
        for i in range(2):
            sl = slice(256*i,256*i+256)
            s = None
            for (xh,xl),(yh,yl) in zip(xs,ws):
                t = bdot(xh[sl],yh,NT)+bdot(xl[sl],yh,NT)+bdot(xh[sl],yl,NT)
                s = t if s is None else s+t
            if q==0: acc[sl,:] = s
            else: s_ref[32*i:32*i+32,8:16,:] = s.reshape(32,8,512)
        if q==0:
            for i in range(4):
                sl = slice(128*i,128*i+128)
                s_ref[16*i:16*i+16,0:8,:] = (0.5*(acc[sl,:]+acc[:,sl].T)).reshape(16,8,512)

def moments(pos, x, o, yt, ot, g, lo, hi):
    B = pl.BlockSpec
    w = lambda shape,*idx: B(shape, lambda g: idx)
    full = w((512,512),0,0)
    return pl.pallas_call(moment_kernel, name="moments", grid=(1,),
        in_specs=[SMEM]+[full]*4+[w((3,512),0,0),w((32,128),48,0),w((32,128),48,0)],
        out_specs=w((64,16,512),0,0,0), scratch_shapes=[pltpu.VMEM((512,512),f32)],
        out_shape=jax.ShapeDtypeStruct((64,16,512),f32),
        cost_estimate=pl.CostEstimate(flops=12*2*512**3,bytes_accessed=8*MB,transcendentals=0),
        compiler_params=params(40))(pos,x,o,yt,ot,g,lo,hi)

def total_kernel(p_ref, o_ref):
    o_ref[...] = jnp.broadcast_to(jnp.sum(p_ref[...],axis=0)[None],o_ref.shape)

def total(part):
    return pl.pallas_call(total_kernel, out_shape=jax.ShapeDtypeStruct(part.shape,f32), name="total",
        cost_estimate=pl.CostEstimate(flops=200000,bytes_accessed=MB,transcendentals=0),
        compiler_params=params(16))(part)

def half_kernel(pos, s_ref, li_ref, out_ref, lt):
    lane = lax.broadcasted_iota(jnp.int32,(8,128),1)
    sub = lax.broadcasted_iota(jnp.int32,(8,128),0)
    z = hdot(jnp.sum(s_ref[...],axis=0),li_ref[...],NT)
    z0 = z[0:8]; z1 = z[8:16]
    k = 8*pos[0]+pos[2]
    lt[...] = li_ref[:,pl.ds(pl.multiple_of((k//16)*128,128),128)].T
    e = jnp.sum(z0*lt[pl.ds(pl.multiple_of(8*(k%16),8),8),:],axis=0,keepdims=True)
    ee = jnp.zeros((8,128),f32)
    for g in range(8):
        b = jnp.broadcast_to(e[:,128*(g//2):128*(g//2)+128],(8,128))
        if g%2==0: b = pltpu.roll(b,64,1)
        ee = jnp.where(sub==g,b,ee)
    for u in range(4):
        for v in range(4):
            a = z0[:,128*u:128*u+128]; b = z1[:,128*u:128*u+128]
            if v: a = pltpu.roll(a,128-32*v,1)
            if v!=1: b = pltpu.roll(b,(160-32*v)%128,1)
            t = jnp.where(lane<32,a,jnp.where(lane<64,b,ee))
            for y in range(8):
                out_ref[8*(4*u+v)+y] = t

def half(pos, s, li):
    return pl.pallas_call(half_kernel, name="half", in_specs=[SMEM,VMEM,VMEM],
        out_shape=jax.ShapeDtypeStruct((128,8,128),f32), scratch_shapes=[pltpu.VMEM((128,512),f32)],
        cost_estimate=pl.CostEstimate(flops=2*24*512*512*6,bytes_accessed=2*MB,transcendentals=0),
        compiler_params=params(16))(pos,s,li)

def tile_kernel(pos, r_ref, li_ref, p_ref, d_ref, w_ref, e_ref, acc):
    c = pos[1]; gx = 2*pos[0]+c; gy = pos[2]
    lane = lax.broadcasted_iota(jnp.int32,(64,128),1)
    lane8 = lax.broadcasted_iota(jnp.int32,(8,128),1)
    lb = li_ref[pl.ds(pl.multiple_of(64*gy,64),64),:]
    t0 = hdot(lb,r_ref[:,0].reshape(512,128),NN)
    t1 = hdot(lb,r_ref[:,1].reshape(512,128),NN)
    t = jnp.where(lane<64,t0,pltpu.roll(t1,64,1))
    tt = jnp.concatenate([t,t],axis=0).T
    p_ref[...] = tt[0:32,0:64]*(1.0/NORB)
    for q in range(3):
        d_ref[q] = tt[32*q+32:32*q+64,0:64]*(1.0/math.sqrt(NORB))
    e = jnp.sum(r_ref[:,0].reshape(64,8,128),axis=0)
    e_ref[...] = e*(1.0/NORB)
    ea = jnp.broadcast_to(e_ref[pl.ds(pos[0],1),:],(8,128))
    ea = pltpu.roll(ea,64-32*c,1)
    ea = jnp.where(lane8<32,ea,0.0)
    ea = ea+pltpu.roll(ea,32,1)+pltpu.roll(ea,64,1)+pltpu.roll(ea,96,1)
    eb = pltpu.roll(jnp.broadcast_to(e_ref[pl.ds(gy,1),:],(8,128)),64,1)
    eb = jnp.broadcast_to(eb[0:1,:],(128,128)).T[0:64,:]
    gap = eb-jnp.broadcast_to(ea[0:1,:],(64,128))
    dip = t*(1.0/math.sqrt(NORB))
    sq = jnp.where(lane>=32,dip*dip,0.0)
    st = (sq+pltpu.roll(sq,32,1)+pltpu.roll(sq,64,1)+pltpu.roll(sq,96,1))*(0.01/math.pi)
    base = (64*(lane8//32)).astype(f32)+0.5
    for w in range(64):
        om = -0.3+0.6*(base+float(w))/256.0
        tot = jnp.zeros((8,128),f32)
        for b in range(8):
            x = om-gap[8*b:8*b+8,:]
            tot = tot+st[8*b:8*b+8,:]/(x*x+0.0001)
        acc[w:w+1,:] = jnp.sum(tot,axis=0,keepdims=True)
    sel = (lane8//32==lax.broadcasted_iota(jnp.int32,(8,128),0)).astype(f32)
    m = hdot(sel,jnp.concatenate([acc[...],acc[...]],axis=0),NT)*(1.0/(512.0*512.0))
    m = jnp.concatenate([jnp.where(lane8[0:1]<64,m[0:1],m[1:2]),jnp.where(lane8[0:1]<64,m[2:3],m[3:4])],axis=0)
    w_ref[...] = jnp.broadcast_to(m[None],(128,2,128))

def tile(pos, r, li):
    sds = jax.ShapeDtypeStruct
    return pl.pallas_call(tile_kernel, name="tile", in_specs=[SMEM,VMEM,VMEM], out_specs=[VMEM]*3,
        out_shape=[sds((32,64),f32),sds((3,32,64),f32),sds((128,2,128),f32)],
        scratch_shapes=[pltpu.VMEM((8,128),f32),pltpu.VMEM((64,128),f32)],
        cost_estimate=pl.CostEstimate(flops=10000000,bytes_accessed=2*MB,transcendentals=0),
        compiler_params=params(16))(pos,r,li)

def rotate_kernel(x_ref, li_ref, o_ref):
    xh, xl = split(x_ref[...])
    for i in range(2):
        lh, ll = split(li_ref[256*i:256*i+256,:])
        o_ref[4*i:4*i+4] = (bdot(lh,xh,NN)+bdot(ll,xh,NN)+bdot(lh,xl,NN)).reshape(4,64,512)

def rotate(x, li):
    return pl.pallas_call(rotate_kernel, out_shape=jax.ShapeDtypeStruct((8,64,512),f32), name="rotate",
        cost_estimate=pl.CostEstimate(flops=3*2*512**3,bytes_accessed=3*MB,transcendentals=0),
        compiler_params=params(16))(x,li)

SLABS = ("gq","c")
PEERS = ("gq","gy")
ALL = ("gq","c","gy")

def swap(x, axis):
    return lax.all_to_all(x,axis,split_axis=0,concat_axis=0,tiled=True)

def chain(n):
    return [(i,i+1) for i in range(n-1)], [(i+1,i) for i in range(n-1)]

def shards(hopping_blocks, neighbors, orbital_grid, trial_block):
    gq = lax.axis_index("gq"); c = lax.axis_index("c"); gy = lax.axis_index("gy")
    pos = jnp.stack([gq,c,gy])
    near = neighbors
    up, down = chain(16)
    vt = trial_block.T
    sup, sdown, grid = payload(pos,near,hopping_blocks,vt,orbital_grid)
    plo = lax.ppermute(sup,SLABS,up)
    phi = lax.ppermute(sdown,SLABS,down)
    a2, y0, p0, own = prep(pos,hopping_blocks,vt)
    a2h, y0h, p0h = halo_prep(plo,phi)
    y1, p1, y1h, p1h = step(pos,near,a2,a2h,p0,p0h,y0,y0h,wide=True)
    ye, slo, shi = edge(pos,near,a2,p1,p1h,y1,y0)
    lo = lax.ppermute(shi,SLABS,up)
    hi = lax.ppermute(slo,SLABS,down)
    y2, p2 = inner(pos,near,a2,p1,ye,y1,y0)
    y2h, p2h = unpack(lo,hi)
    y3, p3, y3h, p3h = step(pos,near,a2,a2h,p2,p2h,y2,y2h,y1,y1h,wide=True)
    sent, = step(pos,near,a2,a2h,p3,p3h,y3,y3h,y2,y2h,last=True)

    x = swap(sent,"gy").reshape(512,512)
    pair = [(i,i^1) for i in range(16)]
    other = lax.ppermute(x,SLABS,pair)
    hi = lax.ppermute(x[:,:256],ALL,chain(128)[1])
    part = gram(pos,x,other)
    part, xa = lax.optimization_barrier((part,x))
    yt = applied(pos,near,xa,hi,own)
    summed, yt = lax.optimization_barrier((swap(part,PEERS),yt))
    ot = lax.ppermute(yt,SLABS,[(i+1,i) for i in range(0,16,2)])
    both, ot = lax.optimization_barrier((total(summed),ot))
    ga = swap(both,PEERS).reshape(512,256)
    s = moments(pos,x,other,yt,ot,grid,plo,phi)
    s, ga = lax.optimization_barrier((s,ga))
    gb = lax.ppermute(ga,SLABS,pair)
    s, gb = lax.optimization_barrier((s,gb))
    li = chol(pos,ga,gb,1.0/NORB)
    rows = swap(half(pos,swap(s,PEERS),li),ALL).reshape(8,2,64,128)
    projected, dipoles, spec = tile(pos,rows,li)
    q = swap(rotate(x,li),"gy")
    orthonormal = q.transpose(1,0,2).reshape(64,4096).T
    spectrum = jnp.sum(swap(spec,ALL),axis=0).reshape(256)
    return orthonormal, projected, dipoles, spectrum

def solution(mesh):
    P = jax.sharding.PartitionSpec
    fine = jax.sharding.Mesh(mesh.devices.reshape(8,2,8),ALL)
    return jax.shard_map(shards, mesh=fine,
        in_specs=(P(SLABS,None,None,None),P(SLABS,None),P(None,SLABS),P(SLABS,"gy")),
        out_specs=(P(SLABS,"gy"),P(SLABS,"gy"),P(None,SLABS,"gy"),P()),
        check_vma=False)
```

```python
import functools
import math

import jax
import jax.numpy as jnp
from jax import lax
from jax.experimental import pallas as pl
from jax.experimental.pallas import tpu as pltpu
f32=jnp.float32; bf16=jnp.bfloat16
MB=1<<20

def split(x):
    hi = x.astype(bf16)
    return hi, (x - hi.astype(f32)).astype(bf16)

def inv_chol_128(read, write):
    lane = lax.broadcasted_iota(jnp.int32,(8,128),1)
    sub = lax.broadcasted_iota(jnp.int32,(8,128),0)
    full = lambda v: jnp.broadcast_to(v,(8,128))
    m = [read(g) for g in range(16)]
    for p in range(16):
        j0 = 8*p
        d = m[p]
        c = [full(d[:,j0+l:j0+l+1]) for l in range(8)]
        s = {}; rp = []; rows = []; fin = d
        inpanel = (lane>=j0)&(lane<j0+8)
        for l in range(8):
            piv = full(c[l][l:l+1,:])
            r = 1.0/piv
            rp.append(r)
            mult = jnp.where(sub>l,c[l]*r,0.0)
            for q in range(l+1,8):
                s[l,q] = full(c[q][l:l+1,:])
                c[q] = c[q]-mult*s[l,q]
            row = jnp.where(lane==j0+l,1.0,full(d[l:l+1,:]))
            row = jnp.where(inpanel&(lane>j0+l),0.0,row)
            rows.append(row)
            d = jnp.where((lane==j0+l)&(sub>l),0.0,d)-mult*row
            fin = jnp.where(sub==l,row*lax.rsqrt(piv),fin)
        m[p] = fin
        for g in range(p+1,16):
            v = m[g]
            cg = [full(v[:,j0+l:j0+l+1]) for l in range(8)]
            v = jnp.where(inpanel,0.0,v)
            for l in range(8):
                mult = cg[l]*rp[l]
                for q in range(l+1,8):
                    cg[q] = cg[q]-mult*s[l,q]
                v = v-mult*rows[l]
            m[g] = v
    for g in range(16):
        write(g, jnp.where(lane<=sub+8*g, m[g], 0.0))

def hdot(a,b,dims):
    return lax.dot_general(a,b,(dims,((),())),precision=lax.Precision.HIGHEST,preferred_element_type=f32)

def chol_kernel(scale, pos, g_ref, o_ref, out_ref):
    c = pos[1]
    out_ref[:,pl.ds(pl.multiple_of(256*c,256),256)] = g_ref[...]*scale
    out_ref[:,pl.ds(pl.multiple_of(256-256*c,256),256)] = o_ref[...]*scale
    for k in range(4):
        k0 = 128*k
        def read(g): return out_ref[k0+8*g:k0+8*g+8,k0:k0+128]
        def write(g,v): out_ref[k0+8*g:k0+8*g+8,k0:k0+128] = v
        inv_chol_128(read,write)
        x = out_ref[128*k:128*k+128,128*k:128*k+128]
        for j in range(4):
            if j==k: continue
            out_ref[128*k:128*k+128,128*j:128*j+128] = hdot(x,out_ref[128*k:128*k+128,128*j:128*j+128],((1,),(0,)))
        bk = out_ref[128*k:128*k+128,:]
        for i in range(k+1,4):
            w = bk[:,128*i:128*i+128]
            upd = hdot(w,bk,((0,),(0,)))
            for j in range(4):
                if k<j<i: continue
                o = -upd[:,128*j:128*j+128] if j==k else out_ref[128*i:128*i+128,128*j:128*j+128]-upd[:,128*j:128*j+128]
                out_ref[128*i:128*i+128,128*j:128*j+128]=o
        for j in range(k+1,4):
            out_ref[128*k:128*k+128,128*j:128*j+128]=jnp.zeros((128,128),f32)

def call(kernel, name, args, outs, flops, scratch=(), vmem=56):
    whole = lambda v: pl.BlockSpec(v.shape, lambda g: (0,)*len(v.shape))
    single = not isinstance(outs,(list,tuple))
    return pl.pallas_call(kernel, name=name, grid=(1,),
        in_specs=[pl.BlockSpec(memory_space=pltpu.SMEM) if v.ndim==1 else whole(v) for v in args],
        out_specs=whole(outs) if single else [whole(v) for v in outs],
        out_shape=outs, scratch_shapes=list(scratch),
        cost_estimate=pl.CostEstimate(flops=flops,bytes_accessed=4*MB,transcendentals=0),
        compiler_params=pltpu.CompilerParams(vmem_limit_bytes=vmem*MB))(*args)

def sds(*shape, dtype=f32):
    return jax.ShapeDtypeStruct(shape,dtype)

def chol(pos, mine, other, scale):
    return call(functools.partial(chol_kernel,scale),"chol",(pos,mine,other),sds(512,512),8000000000)

def dup_pack(y):
    lane = lax.broadcasted_iota(jnp.int32,y.shape,1)
    hi = y.astype(bf16).astype(f32)
    return jnp.where(lane<64, hi, y-hi).astype(bf16)

def prep_kernel(pos, h_ref, v_ref, a2_ref, y_ref, p_ref, own_ref):
    for r in range(4):
        for k in range(5):
            hi, lo = split(h_ref[r,k])
            a2_ref[r,0:128,128*k:128*k+128] = hi
            a2_ref[r,128:256,128*k:128*k+128] = lo
    @pl.when(pl.program_id(0)==pos[2])
    def _():
        own_ref[...] = a2_ref[...]
    v = v_ref[...]
    y = jnp.concatenate([v,v],axis=0).T
    y_ref[...] = y
    p_ref[...] = dup_pack(y)

def prep(pos, h, vt):
    B = pl.BlockSpec
    yb = B((512,128),lambda g,n:(g,0))
    sds = jax.ShapeDtypeStruct
    return pl.pallas_call(prep_kernel, name="prep",
        grid_spec=pltpu.PrefetchScalarGridSpec(num_scalar_prefetch=1, grid=(8,),
            in_specs=[B((4,5,128,128),lambda g,n:(g,0,0,0)), B((64,512),lambda g,n:(0,g))],
            out_specs=[B((4,256,640),lambda g,n:(g,0,0)), yb, yb, B((4,256,640),lambda g,n:(0,0,0))]),
        out_shape=[sds((32,256,640),bf16), sds((4096,128),f32), sds((4096,128),bf16), sds((4,256,640),bf16)],
        cost_estimate=pl.CostEstimate(flops=1000000,bytes_accessed=25*MB,transcendentals=0),
        compiler_params=pltpu.CompilerParams(vmem_limit_bytes=24*MB))(pos,h,vt)

def payload_kernel(pos, near, ha, hb, va, vb, grid, up_ref, down_ref, g_ref):
    g = grid[...].astype(f32)
    g_ref[...] = g
    base = 32*(2*pos[0]+pos[1])
    for out, h, v, n in ((up_ref,ha,va,30),(down_ref,hb,vb,0)):
        for r in range(2):
            for k in range(5):
                o = near[k,n+r]-base-(n+r)+2
                out[pl.ds(pl.multiple_of(640*r+128*o,128),128),:] = h[r,k]
        for b in range(4):
            out[1280+64*b:1344+64*b,:] = v[:,128*b:128*b+128]
        out[1536:1568,:] = jnp.zeros((32,128),f32)
        for u in range(4):
            out[1539+8*u:1542+8*u,:] = g[:,128*u:128*u+128]

def payload(pos, near, h, vt, grid):
    B = pl.BlockSpec
    w = lambda shape,*idx: B(shape, lambda g,p,n: idx)
    sds = jax.ShapeDtypeStruct
    return pl.pallas_call(payload_kernel, name="payload",
        grid_spec=pltpu.PrefetchScalarGridSpec(num_scalar_prefetch=2, grid=(1,),
            in_specs=[w((2,5,128,128),15,0,0,0),w((2,5,128,128),0,0,0,0),w((64,512),0,7),w((64,512),0,0),B((3,512),lambda g,p,n:(0,p[2]))],
            out_specs=[w((1568,128),0,0)]*2+[w((3,512),0,0)]),
        out_shape=[sds((1568,128),f32)]*2+[sds((3,512),f32)],
        cost_estimate=pl.CostEstimate(flops=1000000,bytes_accessed=4*MB,transcendentals=0),
        compiler_params=pltpu.CompilerParams(vmem_limit_bytes=56*MB))(pos,near,h,h,vt,vt,grid)

def halo_prep_kernel(lo_ref, hi_ref, a2_ref, y_ref, p_ref):
    for s, ref in ((0,lo_ref),(1,hi_ref)):
        for r in range(2):
            for k in range(5):
                at = 128*(5*r+k)
                hi, lo = split(ref[at:at+128,:])
                a2_ref[2*s+r,0:128,128*k:128*k+128] = hi
                a2_ref[2*s+r,128:256,128*k:128*k+128] = lo
        for b in range(4):
            v = ref[1280+64*b:1344+64*b,:]
            y = jnp.concatenate([v,v],axis=0).T
            p_ref[512*s+128*b:512*s+128*b+128,:] = dup_pack(y)
            e = b-2 if s==0 else b
            if 0<=e<2: y_ref[256*s+128*e:256*s+128*e+128,:] = y

def halo_prep(lo, hi):
    return pl.pallas_call(halo_prep_kernel, name="halo_prep",
        out_shape=[jax.ShapeDtypeStruct((4,256,640),bf16), jax.ShapeDtypeStruct((512,128),f32), jax.ShapeDtypeStruct((1024,128),bf16)],
        cost_estimate=pl.CostEstimate(flops=1000000,bytes_accessed=4*MB,transcendentals=0),
        compiler_params=pltpu.CompilerParams(vmem_limit_bytes=16*MB))(lo,hi)

def unpack_kernel(lo_ref, hi_ref, y_ref, p_ref):
    lane = lax.broadcasted_iota(jnp.int32,(128,128),1)
    for s, ref in ((0,lo_ref),(1,hi_ref)):
        for h in range(2):
            x = ref[128*h:128*h+128,:]; xr = pltpu.roll(x,64,1)
            pair = (jnp.where(lane<64,x,xr),jnp.where(lane<64,xr,x))
            for w in range(2):
                b = 2*h+w
                p_ref[512*s+128*b:512*s+128*b+128,:] = dup_pack(pair[w])
                e = b-2 if s==0 else b
                if 0<=e<2: y_ref[256*s+128*e:256*s+128*e+128,:] = pair[w]

def unpack(lo, hi):
    return pl.pallas_call(unpack_kernel, name="unpack",
        out_shape=[jax.ShapeDtypeStruct((512,128),f32), jax.ShapeDtypeStruct((1024,128),bf16)],
        cost_estimate=pl.CostEstimate(flops=1000000,bytes_accessed=MB,transcendentals=0),
        compiler_params=pltpu.CompilerParams(vmem_limit_bytes=16*MB))(lo,hi)

C0, HALF = -0.3, 0.9

def apply_row(a2, pieces):
    rhs = jnp.concatenate(pieces,axis=0)
    res = jnp.dot(a2, rhs, preferred_element_type=f32)
    u = res[:128]+res[128:]
    return u + pltpu.roll(u, 64, 1)

def recur(hy, y, yp):
    t = (hy - C0*y)/HALF
    return t if yp is None else 2.0*t - yp

def local(pos, near, i, k):
    return near[k,i]-32*(2*pos[0]+pos[1])

def slot_of(n):
    return jnp.where(n<0,n+36,jnp.where(n>31,n+4,n))

HALO_SLOTS = ((32,33,34,35,0),(33,34,35,0,1),(30,31,36,37,38),(31,36,37,38,39))

def block(ref, slot):
    return ref[pl.ds(pl.multiple_of(slot*128,128),128),:]

def step_kernel(first, wide, last, pos, near, a2, a2h, p, ph, y, yh, *rest):
    rest = list(rest); ext = rest.pop()
    yp = yph = None
    if not first:
        yp = rest.pop(0); yph = rest.pop(0)
    outs = rest
    g = pl.program_id(0)
    @pl.when(g==0)
    def _():
        ext[0:4096,:] = p[...]
        if wide: ext[4096:5120,:] = ph[...]
        else: ext[4352:4864,:] = ph[...]
    @pl.when(g<8)
    def _():
        for r in range(4):
            hy = apply_row(a2[r],[block(ext,slot_of(local(pos,near,4*g+r,k))) for k in range(5)])
            sl = slice(128*r,128*r+128)
            new = recur(hy,y[sl,:],None if first else yp[sl,:])
            if last:
                outs[0][0,:,sl] = new.T[:64]
            else:
                outs[0][sl,:] = new
                outs[1][sl,:] = dup_pack(new)
    if wide:
        @pl.when(g==8)
        def _():
            for r in range(4):
                hy = apply_row(a2h[r],[ext[128*b:128*b+128,:] for b in HALO_SLOTS[r]])
                sl = slice(128*r,128*r+128)
                new = recur(hy,yh[sl,:],None if first else yph[sl,:])
                outs[2][sl,:] = new
                outs[3][sl,:] = dup_pack(new)

def step(pos, near, a2, a2h, p, ph, y, yh, yp=None, yph=None, wide=False, last=False):
    first = yp is None
    B = pl.BlockSpec
    at = lambda g: jnp.minimum(g,7)
    w = lambda *shape: B(shape, lambda g,p,n: (0,)*len(shape))
    yb = B((512,128),lambda g,p,n:(at(g),0))
    sds = jax.ShapeDtypeStruct
    if last:
        outs=[B((1,64,512),lambda g,p,n:(at(g),0,0))]; shapes=[sds((8,64,512),f32)]
    else:
        outs=[yb,yb]; shapes=[sds((4096,128),f32),sds((4096,128),bf16)]
    if wide:
        outs+=[w(512,128)]*2; shapes+=[sds((512,128),f32),sds((512,128),bf16)]
    return pl.pallas_call(functools.partial(step_kernel,first,wide,last), name="step",
        grid_spec=pltpu.PrefetchScalarGridSpec(num_scalar_prefetch=2, grid=(9 if wide else 8,),
            in_specs=[B((4,256,640),lambda g,p,n:(at(g),0,0)), w(4,256,640), w(4096,128), w(*ph.shape), yb, w(512,128)]+([] if first else [yb,w(512,128)]),
            out_specs=outs, scratch_shapes=[pltpu.VMEM((5120,128),bf16)]),
        out_shape=shapes,
        cost_estimate=pl.CostEstimate(flops=36*2*256*640*128*4,bytes_accessed=16*MB,transcendentals=0),
        compiler_params=pltpu.CompilerParams(vmem_limit_bytes=24*MB))(
            pos,near,a2,a2h,p,ph,y,yh,*([] if first else [yp,yph]))

def edge_kernel(pos, near, alo, ahi, vlo, vhi, ph, ylo, yhi, plo, phi, ye, slo, shi, ext):
    lane = lax.broadcasted_iota(jnp.int32,(128,128),1)
    ext[0:256,:] = ph[0:256,:]
    ext[256:1024,:] = vlo[0:768,:]
    ext[1024:1792,:] = vhi[256:1024,:]
    ext[1792:2048,:] = ph[256:512,:]
    new = []
    for e in range(8):
        a, yr, pr = (alo,ylo,plo) if e<4 else (ahi,yhi,phi)
        hy = apply_row(a[e%4],[block(ext,local(pos,near,e if e<4 else 24+e,k)+(2 if e<4 else -18)) for k in range(5)])
        sl = slice(128*(e%4),128*(e%4)+128)
        new.append(recur(hy,yr[sl,:],pr[sl,:]))
        ye[128*e:128*e+128,:] = new[-1]
    for h in range(2):
        slo[128*h:128*h+128,:] = jnp.where(lane<64,new[2*h],new[2*h+1])
        shi[128*h:128*h+128,:] = jnp.where(lane<64,new[4+2*h],new[5+2*h])

def edge(pos, near, a2, p, ph, y, yp):
    B = pl.BlockSpec
    w = lambda shape,*idx: B(shape, lambda g,p,n: idx)
    ys = [w((512,128),0,0), w((512,128),7,0)]
    sds = jax.ShapeDtypeStruct
    return pl.pallas_call(edge_kernel, name="edge",
        grid_spec=pltpu.PrefetchScalarGridSpec(num_scalar_prefetch=2, grid=(1,),
            in_specs=[w((4,256,640),0,0,0), w((4,256,640),7,0,0), w((1024,128),0,0), w((1024,128),3,0), w((512,128),0,0)]+ys+ys,
            out_specs=[w((1024,128),0,0), w((256,128),0,0), w((256,128),0,0)],
            scratch_shapes=[pltpu.VMEM((2048,128),bf16)]),
        out_shape=[sds((1024,128),f32)]+[sds((256,128),f32)]*2,
        cost_estimate=pl.CostEstimate(flops=8*2*256*640*128,bytes_accessed=5*MB,transcendentals=0),
        compiler_params=pltpu.CompilerParams(vmem_limit_bytes=24*MB))(
            pos,near,a2,a2,p,p,ph,y,y,yp,yp)

def inner_kernel(pos, near, a2, p, ye, y, yp, yo, po):
    g = pl.program_id(0)
    @pl.when((g==0)|(g==7))
    def _():
        new = ye[...]
        yo[...] = new
        po[...] = dup_pack(new)
    @pl.when((g>0)&(g<7))
    def _():
        for r in range(4):
            hy = apply_row(a2[r],[block(p,local(pos,near,4*g+r,k)) for k in range(5)])
            sl = slice(128*r,128*r+128)
            new = recur(hy,y[sl,:],yp[sl,:])
            yo[sl,:] = new
            po[sl,:] = dup_pack(new)

def inner(pos, near, a2, p, ye, y, yp):
    B = pl.BlockSpec
    yb = B((512,128),lambda g,p,n:(g,0))
    sds = jax.ShapeDtypeStruct
    return pl.pallas_call(inner_kernel, name="inner",
        grid_spec=pltpu.PrefetchScalarGridSpec(num_scalar_prefetch=2, grid=(8,),
            in_specs=[B((4,256,640),lambda g,p,n:(g,0,0)), B((4096,128),lambda g,p,n:(0,0)), B((512,128),lambda g,p,n:(g//7,0)), yb, yb],
            out_specs=[yb,yb]),
        out_shape=[sds((4096,128),f32),sds((4096,128),bf16)],
        cost_estimate=pl.CostEstimate(flops=24*2*256*640*128*4,bytes_accessed=16*MB,transcendentals=0),
        compiler_params=pltpu.CompilerParams(vmem_limit_bytes=24*MB))(pos,near,a2,p,ye,y,yp)

NT = ((1,),(1,))
NN = ((1,),(0,))
NORB = 65536

def bdot(a, b, dims):
    return lax.dot_general(a,b,(dims,((),())),preferred_element_type=f32)

def params(mb):
    return pltpu.CompilerParams(vmem_limit_bytes=mb*MB)

SMEM = pl.BlockSpec(memory_space=pltpu.SMEM)
VMEM = pl.BlockSpec(memory_space=pltpu.VMEM)

def gram_kernel(pos, x_ref, o_ref, g_ref):
    half = pl.ds(pl.multiple_of(256*pos[1],256),256)
    xs = [split(x_ref[...]),split(o_ref[...])]
    hs = [split(x_ref[half,:]),split(o_ref[half,:])]
    for i in range(2):
        sl = slice(256*i,256*i+256)
        s = None
        for (xh,xl),(hh,hl) in zip(xs,hs):
            t = bdot(xh[sl],hh,NT)+bdot(xl[sl],hh,NT)+bdot(xh[sl],hl,NT)
            s = t if s is None else s+t
        g_ref[32*i:32*i+32] = s.reshape(32,8,256)

def gram(pos, x, o):
    return call(gram_kernel,"gram",(pos,x,o),sds(64,8,256),3*2*512**3)

def applied_kernel(pos, near, x_ref, hi_ref, a2, yt, xh, xl):
    for ref, at, w in ((x_ref,0,512),(hi_ref,512,256)):
        h, l = split(ref[...])
        xh[:,at:at+w] = h; xl[:,at:at+w] = l
    xh[:,512:768] = xh[:,512:768]*2; xl[:,512:768] = xl[:,512:768]*2
    xh[:,768:896] = jnp.zeros((512,128),bf16); xl[:,768:896] = jnp.zeros((512,128),bf16)
    for i in range(4):
        n = [local(pos,near,4*pos[2]+i,k)-4*pos[2] for k in range(5)]
        at = [pl.ds(pl.multiple_of(jnp.where(m<0,6,m)*128,128),128) for m in n]
        h = jnp.concatenate([xh[:,a] for a in at],axis=1)
        l = jnp.concatenate([xl[:,a] for a in at],axis=1)
        r = bdot(h,a2[i],NT)
        yt[:,128*i:128*i+128] = r[:,:128]+r[:,128:]+bdot(l,a2[i,:128,:],NT)

def applied(pos, near, x, hi, a2):
    B = pl.BlockSpec
    w = lambda shape: B(shape, lambda g,p,n: (0,)*len(shape))
    return pl.pallas_call(applied_kernel, name="applied",
        grid_spec=pltpu.PrefetchScalarGridSpec(num_scalar_prefetch=2, grid=(1,),
            in_specs=[w((512,512)),w((512,256)),w((4,256,640))],
            out_specs=w((512,512)),
            scratch_shapes=[pltpu.VMEM((512,896),bf16),pltpu.VMEM((512,896),bf16)]),
        out_shape=jax.ShapeDtypeStruct((512,512),f32),
        cost_estimate=pl.CostEstimate(flops=4*2*512*512*640,bytes_accessed=5*MB,transcendentals=0),
        compiler_params=params(56))(pos,near,x,hi,a2)

def moment_kernel(pos, x_ref, o_ref, yt_ref, ot_ref, g_ref, lo_ref, hi_ref, s_ref, acc):
    c = pos[1]
    xs = [split(x_ref[...]),split(o_ref[...])]
    tail = jnp.where(c==0,hi_ref[...],lo_ref[...])
    og = jnp.concatenate([tail[8*u+3:8*u+6,:] for u in range(4)],axis=1)
    for q in range(2):
        ws = []
        for x, y, g in ((x_ref,yt_ref,g_ref[...]),(o_ref,ot_ref,og)):
            places = (g+0.5)/32.0-1.0
            if q==0:
                w = jnp.where(c==0,y[...],x[...]*places[1:2,:])
            else:
                w = x[...]*jnp.where(c==0,places[0:1,:],places[2:3,:])
            ws.append(split(w))
        for i in range(2):
            sl = slice(256*i,256*i+256)
            s = None
            for (xh,xl),(yh,yl) in zip(xs,ws):
                t = bdot(xh[sl],yh,NT)+bdot(xl[sl],yh,NT)+bdot(xh[sl],yl,NT)
                s = t if s is None else s+t
            if q==0: acc[sl,:] = s
            else: s_ref[32*i:32*i+32,8:16,:] = s.reshape(32,8,512)
        if q==0:
            for i in range(4):
                sl = slice(128*i,128*i+128)
                s_ref[16*i:16*i+16,0:8,:] = (0.5*(acc[sl,:]+acc[:,sl].T)).reshape(16,8,512)

def moments(pos, x, o, yt, ot, g, lo, hi):
    B = pl.BlockSpec
    w = lambda shape,*idx: B(shape, lambda g: idx)
    full = w((512,512),0,0)
    return pl.pallas_call(moment_kernel, name="moments", grid=(1,),
        in_specs=[SMEM]+[full]*4+[w((3,512),0,0),w((32,128),48,0),w((32,128),48,0)],
        out_specs=w((64,16,512),0,0,0), scratch_shapes=[pltpu.VMEM((512,512),f32)],
        out_shape=jax.ShapeDtypeStruct((64,16,512),f32),
        cost_estimate=pl.CostEstimate(flops=12*2*512**3,bytes_accessed=8*MB,transcendentals=0),
        compiler_params=params(56))(pos,x,o,yt,ot,g,lo,hi)

def total_kernel(p_ref, o_ref):
    o_ref[...] = jnp.broadcast_to(jnp.sum(p_ref[...],axis=0)[None],o_ref.shape)

def total(part):
    return call(total_kernel,"total",(part,),sds(*part.shape),200000)

def half_kernel(pos, s_ref, li_ref, out_ref, lt):
    lane = lax.broadcasted_iota(jnp.int32,(8,128),1)
    sub = lax.broadcasted_iota(jnp.int32,(8,128),0)
    z = hdot(jnp.sum(s_ref[...],axis=0),li_ref[...],NT)
    z0 = z[0:8]; z1 = z[8:16]
    k = 8*pos[0]+pos[2]
    lt[...] = li_ref[:,pl.ds(pl.multiple_of((k//16)*128,128),128)].T
    e = jnp.sum(z0*lt[pl.ds(pl.multiple_of(8*(k%16),8),8),:],axis=0,keepdims=True)
    ee = jnp.zeros((8,128),f32)
    for g in range(8):
        b = jnp.broadcast_to(e[:,128*(g//2):128*(g//2)+128],(8,128))
        if g%2==0: b = pltpu.roll(b,64,1)
        ee = jnp.where(sub==g,b,ee)
    for u in range(4):
        for v in range(4):
            a = z0[:,128*u:128*u+128]; b = z1[:,128*u:128*u+128]
            if v: a = pltpu.roll(a,128-32*v,1)
            if v!=1: b = pltpu.roll(b,(160-32*v)%128,1)
            t = jnp.where(lane<32,a,jnp.where(lane<64,b,ee))
            for y in range(8):
                out_ref[8*(4*u+v)+y] = t

def half(pos, s, li):
    return call(half_kernel,"half",(pos,s,li),sds(128,8,128),2*24*512*512*6,[pltpu.VMEM((128,512),f32)],vmem=24)

def tile_kernel(pos, r_ref, li_ref, p_ref, d_ref, w_ref, e_ref, acc):
    c = pos[1]; gx = 2*pos[0]+c; gy = pos[2]
    lane = lax.broadcasted_iota(jnp.int32,(64,128),1)
    lane8 = lax.broadcasted_iota(jnp.int32,(8,128),1)
    lb = li_ref[pl.ds(pl.multiple_of(64*gy,64),64),:]
    t0 = hdot(lb,r_ref[:,0].reshape(512,128),NN)
    t1 = hdot(lb,r_ref[:,1].reshape(512,128),NN)
    t = jnp.where(lane<64,t0,pltpu.roll(t1,64,1))
    tt = jnp.concatenate([t,t],axis=0).T
    p_ref[...] = tt[0:32,0:64]*(1.0/NORB)
    for q in range(3):
        d_ref[q] = tt[32*q+32:32*q+64,0:64]*(1.0/math.sqrt(NORB))
    e = jnp.sum(r_ref[:,0].reshape(64,8,128),axis=0)
    e_ref[...] = e*(1.0/NORB)
    ea = jnp.broadcast_to(e_ref[pl.ds(pos[0],1),:],(8,128))
    ea = pltpu.roll(ea,64-32*c,1)
    ea = jnp.where(lane8<32,ea,0.0)
    ea = ea+pltpu.roll(ea,32,1)+pltpu.roll(ea,64,1)+pltpu.roll(ea,96,1)
    eb = pltpu.roll(jnp.broadcast_to(e_ref[pl.ds(gy,1),:],(8,128)),64,1)
    eb = jnp.broadcast_to(eb[0:1,:],(128,128)).T[0:64,:]
    gap = eb-jnp.broadcast_to(ea[0:1,:],(64,128))
    dip = t*(1.0/math.sqrt(NORB))
    sq = jnp.where(lane>=32,dip*dip,0.0)
    st = (sq+pltpu.roll(sq,32,1)+pltpu.roll(sq,64,1)+pltpu.roll(sq,96,1))*(0.01/math.pi)
    base = (64*(lane8//32)).astype(f32)+0.5
    for w in range(64):
        om = -0.3+0.6*(base+float(w))/256.0
        tot = jnp.zeros((8,128),f32)
        for b in range(8):
            x = om-gap[8*b:8*b+8,:]
            tot = tot+st[8*b:8*b+8,:]/(x*x+0.0001)
        acc[w:w+1,:] = jnp.sum(tot,axis=0,keepdims=True)
    sel = (lane8//32==lax.broadcasted_iota(jnp.int32,(8,128),0)).astype(f32)
    m = hdot(sel,jnp.concatenate([acc[...],acc[...]],axis=0),NT)*(1.0/(512.0*512.0))
    m = jnp.concatenate([jnp.where(lane8[0:1]<64,m[0:1],m[1:2]),jnp.where(lane8[0:1]<64,m[2:3],m[3:4])],axis=0)
    w_ref[...] = jnp.broadcast_to(m[None],(128,2,128))

def tile(pos, r, li):
    return call(tile_kernel,"tile",(pos,r,li),[sds(32,64),sds(3,32,64),sds(128,2,128)],10000000,[pltpu.VMEM((8,128),f32),pltpu.VMEM((64,128),f32)],vmem=24)

def rotate_kernel(pos, x_ref, li_ref, *o_refs):
    xh, xl = split(x_ref[...])
    for i in range(4):
        at = [pl.ds(pl.multiple_of(64*jnp.bitwise_xor(pos[2],2*i+j),64),64) for j in range(2)]
        lh, ll = split(jnp.concatenate([li_ref[a,:] for a in at],axis=0))
        o = bdot(lh,xh,NN)+bdot(ll,xh,NN)+bdot(lh,xl,NN)
        o_refs[2*i][...] = o[0:64]; o_refs[2*i+1][...] = o[64:128]

def rotate(pos, x, li):
    return call(rotate_kernel,"rotate",(pos,x,li),[sds(64,512)]*8,3*2*512**3)

def gather_kernel(pos, *refs):
    for r in range(8):
        refs[8][:,pl.ds(pl.multiple_of(512*jnp.bitwise_xor(pos[2],r),512),512)] = refs[r][...]

def gather(pos, pieces):
    return call(gather_kernel,"gather",(pos,*pieces),sds(64,4096),1000)

SLABS = ("gq","c")
PEERS = ("gq","gy")
ALL = ("gq","c","gy")

def swap(x, axis):
    return lax.all_to_all(x,axis,split_axis=0,concat_axis=0,tiled=True)

def chain(n):
    return [(i,i+1) for i in range(n-1)], [(i+1,i) for i in range(n-1)]

def shards(hopping_blocks, neighbors, orbital_grid, trial_block):
    gq = lax.axis_index("gq"); c = lax.axis_index("c"); gy = lax.axis_index("gy")
    pos = jnp.stack([gq,c,gy])
    near = neighbors.T
    up, down = chain(16)
    vt = trial_block.T
    sup, sdown, grid = payload(pos,near,hopping_blocks,vt,orbital_grid)
    plo = lax.ppermute(sup,SLABS,up)
    phi = lax.ppermute(sdown,SLABS,down)
    a2, y0, p0, own = prep(pos,hopping_blocks,vt)
    a2h, y0h, p0h = halo_prep(plo,phi)
    y1, p1, y1h, p1h = step(pos,near,a2,a2h,p0,p0h,y0,y0h,wide=True)
    ye, slo, shi = edge(pos,near,a2,p1,p1h,y1,y0)
    lo = lax.ppermute(shi,SLABS,up)
    hi = lax.ppermute(slo,SLABS,down)
    y2, p2 = inner(pos,near,a2,p1,ye,y1,y0)
    y2h, p2h = unpack(lo,hi)
    y3, p3, y3h, p3h = step(pos,near,a2,a2h,p2,p2h,y2,y2h,y1,y1h,wide=True)
    sent, = step(pos,near,a2,a2h,p3,p3h,y3,y3h,y2,y2h,last=True)

    x = swap(sent,"gy").reshape(512,512)
    pair = [(i,i^1) for i in range(16)]
    other = lax.ppermute(x,SLABS,pair)
    hi = lax.ppermute(x[:,:256],ALL,chain(128)[1])
    part = gram(pos,x,other)
    part, xa = lax.optimization_barrier((part,x))
    yt = applied(pos,near,xa,hi,own)
    summed, yt = lax.optimization_barrier((swap(part,PEERS),yt))
    ot = lax.ppermute(yt,SLABS,[(i+1,i) for i in range(0,16,2)])
    both, ot = lax.optimization_barrier((total(summed),ot))
    ga = swap(both,PEERS).reshape(512,256)
    s = moments(pos,x,other,yt,ot,grid,plo,phi)
    s, ga = lax.optimization_barrier((s,ga))
    gb = lax.ppermute(ga,SLABS,pair)
    s, gb = lax.optimization_barrier((s,gb))
    li = chol(pos,ga,gb,1.0/NORB)
    rows = swap(half(pos,swap(s,PEERS),li),ALL).reshape(8,2,64,128)
    projected, dipoles, spec = tile(pos,rows,li)
    q = rotate(pos,x,li)
    q = [q[0]]+[lax.ppermute(q[r],"gy",[(i,i^r) for i in range(8)]) for r in range(1,8)]
    orthonormal = gather(pos,q).T
    spectrum = jnp.sum(swap(spec,ALL),axis=0).reshape(256)
    return orthonormal, projected, dipoles, spectrum

def solution(mesh):
    P = jax.sharding.PartitionSpec
    fine = jax.sharding.Mesh(mesh.devices.reshape(8,2,8),ALL)
    return jax.shard_map(shards, mesh=fine,
        in_specs=(P(SLABS,None,None,None),P(SLABS,None),P(None,SLABS),P(SLABS,"gy")),
        out_specs=(P(SLABS,"gy"),P(SLABS,"gy"),P(None,SLABS,"gy"),P()),
        check_vma=False)
```

```python
import functools
import math

import jax
import jax.numpy as jnp
from jax import lax
from jax.experimental import pallas as pl
from jax.experimental.pallas import tpu as pltpu
f32=jnp.float32; bf16=jnp.bfloat16
MB=1<<20

def split(x):
    hi = x.astype(bf16)
    return hi, (x - hi.astype(f32)).astype(bf16)

def inv_chol_128(read, write):
    lane = lax.broadcasted_iota(jnp.int32,(8,128),1)
    sub = lax.broadcasted_iota(jnp.int32,(8,128),0)
    full = lambda v: jnp.broadcast_to(v,(8,128))
    m = [read(g) for g in range(16)]
    for p in range(16):
        j0 = 8*p
        d = m[p]
        c = [full(d[:,j0+l:j0+l+1]) for l in range(8)]
        s = {}; rp = []; rows = []; fin = d
        inpanel = (lane>=j0)&(lane<j0+8)
        for l in range(8):
            piv = full(c[l][l:l+1,:])
            r = 1.0/piv
            rp.append(r)
            mult = jnp.where(sub>l,c[l]*r,0.0)
            for q in range(l+1,8):
                s[l,q] = full(c[q][l:l+1,:])
                c[q] = c[q]-mult*s[l,q]
            row = jnp.where(lane==j0+l,1.0,full(d[l:l+1,:]))
            row = jnp.where(inpanel&(lane>j0+l),0.0,row)
            rows.append(row)
            d = jnp.where((lane==j0+l)&(sub>l),0.0,d)-mult*row
            fin = jnp.where(sub==l,row*lax.rsqrt(piv),fin)
        m[p] = fin
        for g in range(p+1,16):
            v = m[g]
            cg = [full(v[:,j0+l:j0+l+1]) for l in range(8)]
            v = jnp.where(inpanel,0.0,v)
            for l in range(8):
                mult = cg[l]*rp[l]
                for q in range(l+1,8):
                    cg[q] = cg[q]-mult*s[l,q]
                v = v-mult*rows[l]
            m[g] = v
    for g in range(16):
        write(g, jnp.where(lane<=sub+8*g, m[g], 0.0))

def hdot(a,b,dims):
    return lax.dot_general(a,b,(dims,((),())),precision=lax.Precision.HIGHEST,preferred_element_type=f32)

def chol_kernel(scale, pos, g_ref, o_ref, out_ref):
    c = pos[1]
    out_ref[:,pl.ds(pl.multiple_of(256*c,256),256)] = g_ref[...]*scale
    out_ref[:,pl.ds(pl.multiple_of(256-256*c,256),256)] = o_ref[...]*scale
    for k in range(4):
        k0 = 128*k
        def read(g): return out_ref[k0+8*g:k0+8*g+8,k0:k0+128]
        def write(g,v): out_ref[k0+8*g:k0+8*g+8,k0:k0+128] = v
        inv_chol_128(read,write)
        x = out_ref[128*k:128*k+128,128*k:128*k+128]
        for j in range(4):
            if j==k: continue
            out_ref[128*k:128*k+128,128*j:128*j+128] = hdot(x,out_ref[128*k:128*k+128,128*j:128*j+128],((1,),(0,)))
        bk = out_ref[128*k:128*k+128,:]
        for i in range(k+1,4):
            w = bk[:,128*i:128*i+128]
            upd = hdot(w,bk,((0,),(0,)))
            for j in range(4):
                if k<j<i: continue
                o = -upd[:,128*j:128*j+128] if j==k else out_ref[128*i:128*i+128,128*j:128*j+128]-upd[:,128*j:128*j+128]
                out_ref[128*i:128*i+128,128*j:128*j+128]=o
        for j in range(k+1,4):
            out_ref[128*k:128*k+128,128*j:128*j+128]=jnp.zeros((128,128),f32)

def call(kernel, name, args, outs, flops, scratch=(), vmem=16):
    single = not isinstance(outs,(list,tuple))
    if vmem < 56:
        whole = lambda v: pl.BlockSpec(memory_space=pltpu.VMEM)
        grid = {}
    else:
        whole = lambda v: pl.BlockSpec(v.shape, lambda g: (0,)*len(v.shape))
        grid = dict(grid=(1,))
    return pl.pallas_call(kernel, name=name, **grid,
        in_specs=[pl.BlockSpec(memory_space=pltpu.SMEM) if v.ndim==1 else whole(v) for v in args],
        out_specs=whole(outs) if single else [whole(v) for v in outs],
        out_shape=outs, scratch_shapes=list(scratch),
        cost_estimate=pl.CostEstimate(flops=flops,bytes_accessed=4*MB,transcendentals=0),
        compiler_params=pltpu.CompilerParams(vmem_limit_bytes=vmem*MB))(*args)

def sds(*shape, dtype=f32):
    return jax.ShapeDtypeStruct(shape,dtype)

def chol(pos, mine, other, scale):
    return call(functools.partial(chol_kernel,scale),"chol",(pos,mine,other),sds(512,512),8000000000,vmem=56)

def dup_pack(y):
    lane = lax.broadcasted_iota(jnp.int32,y.shape,1)
    hi = y.astype(bf16).astype(f32)
    return jnp.where(lane<64, hi, y-hi).astype(bf16)

def prep_kernel(pos, h_ref, v_ref, a2_ref, y_ref, p_ref, own_ref):
    for r in range(4):
        for k in range(5):
            hi, lo = split(h_ref[r,k])
            a2_ref[r,0:128,128*k:128*k+128] = hi
            a2_ref[r,128:256,128*k:128*k+128] = lo
    @pl.when(pl.program_id(0)==pos[2])
    def _():
        own_ref[...] = a2_ref[...]
    v = v_ref[...]
    y = jnp.concatenate([v,v],axis=0).T
    y_ref[...] = y
    p_ref[...] = dup_pack(y)

def prep(pos, h, vt):
    B = pl.BlockSpec
    yb = B((512,128),lambda g,n:(g,0))
    sds = jax.ShapeDtypeStruct
    return pl.pallas_call(prep_kernel, name="prep",
        grid_spec=pltpu.PrefetchScalarGridSpec(num_scalar_prefetch=1, grid=(8,),
            in_specs=[B((4,5,128,128),lambda g,n:(g,0,0,0)), B((64,512),lambda g,n:(0,g))],
            out_specs=[B((4,256,640),lambda g,n:(g,0,0)), yb, yb, B((4,256,640),lambda g,n:(0,0,0))]),
        out_shape=[sds((32,256,640),bf16), sds((4096,128),f32), sds((4096,128),bf16), sds((4,256,640),bf16)],
        cost_estimate=pl.CostEstimate(flops=1000000,bytes_accessed=25*MB,transcendentals=0),
        compiler_params=pltpu.CompilerParams(vmem_limit_bytes=24*MB))(pos,h,vt)

def payload_kernel(pos, near, ha, hb, va, vb, grid, up_ref, down_ref, g_ref):
    g = grid[...].astype(f32)
    g_ref[...] = g
    base = 32*(2*pos[0]+pos[1])
    for out, h, v, n in ((up_ref,ha,va,30),(down_ref,hb,vb,0)):
        for r in range(2):
            for k in range(5):
                o = near[k,n+r]-base-(n+r)+2
                out[pl.ds(pl.multiple_of(640*r+128*o,128),128),:] = h[r,k]
        for b in range(4):
            out[1280+64*b:1344+64*b,:] = v[:,128*b:128*b+128]
        out[1536:1568,:] = jnp.zeros((32,128),f32)
        for u in range(4):
            out[1539+8*u:1542+8*u,:] = g[:,128*u:128*u+128]

def payload(pos, near, h, vt, grid):
    B = pl.BlockSpec
    w = lambda shape,*idx: B(shape, lambda g,p,n: idx)
    sds = jax.ShapeDtypeStruct
    return pl.pallas_call(payload_kernel, name="payload",
        grid_spec=pltpu.PrefetchScalarGridSpec(num_scalar_prefetch=2, grid=(1,),
            in_specs=[w((2,5,128,128),15,0,0,0),w((2,5,128,128),0,0,0,0),w((64,512),0,7),w((64,512),0,0),B((3,512),lambda g,p,n:(0,p[2]))],
            out_specs=[w((1568,128),0,0)]*2+[w((3,512),0,0)]),
        out_shape=[sds((1568,128),f32)]*2+[sds((3,512),f32)],
        cost_estimate=pl.CostEstimate(flops=1000000,bytes_accessed=4*MB,transcendentals=0),
        compiler_params=pltpu.CompilerParams(vmem_limit_bytes=56*MB))(pos,near,h,h,vt,vt,grid)

def halo_prep_kernel(lo_ref, hi_ref, a2_ref, y_ref, p_ref):
    for s, ref in ((0,lo_ref),(1,hi_ref)):
        for r in range(2):
            for k in range(5):
                at = 128*(5*r+k)
                hi, lo = split(ref[at:at+128,:])
                a2_ref[2*s+r,0:128,128*k:128*k+128] = hi
                a2_ref[2*s+r,128:256,128*k:128*k+128] = lo
        for b in range(4):
            v = ref[1280+64*b:1344+64*b,:]
            y = jnp.concatenate([v,v],axis=0).T
            p_ref[512*s+128*b:512*s+128*b+128,:] = dup_pack(y)
            e = b-2 if s==0 else b
            if 0<=e<2: y_ref[256*s+128*e:256*s+128*e+128,:] = y

def halo_prep(lo, hi):
    return pl.pallas_call(halo_prep_kernel, name="halo_prep",
        out_shape=[jax.ShapeDtypeStruct((4,256,640),bf16), jax.ShapeDtypeStruct((512,128),f32), jax.ShapeDtypeStruct((1024,128),bf16)],
        cost_estimate=pl.CostEstimate(flops=1000000,bytes_accessed=4*MB,transcendentals=0),
        compiler_params=pltpu.CompilerParams(vmem_limit_bytes=16*MB))(lo,hi)

def unpack_kernel(lo_ref, hi_ref, y_ref, p_ref):
    lane = lax.broadcasted_iota(jnp.int32,(128,128),1)
    for s, ref in ((0,lo_ref),(1,hi_ref)):
        for h in range(2):
            x = ref[128*h:128*h+128,:]; xr = pltpu.roll(x,64,1)
            pair = (jnp.where(lane<64,x,xr),jnp.where(lane<64,xr,x))
            for w in range(2):
                b = 2*h+w
                p_ref[512*s+128*b:512*s+128*b+128,:] = dup_pack(pair[w])
                e = b-2 if s==0 else b
                if 0<=e<2: y_ref[256*s+128*e:256*s+128*e+128,:] = pair[w]

def unpack(lo, hi):
    return pl.pallas_call(unpack_kernel, name="unpack",
        out_shape=[jax.ShapeDtypeStruct((512,128),f32), jax.ShapeDtypeStruct((1024,128),bf16)],
        cost_estimate=pl.CostEstimate(flops=1000000,bytes_accessed=MB,transcendentals=0),
        compiler_params=pltpu.CompilerParams(vmem_limit_bytes=16*MB))(lo,hi)

C0, HALF = -0.3, 0.9

def apply_row(a2, pieces):
    rhs = jnp.concatenate(pieces,axis=0)
    res = jnp.dot(a2, rhs, preferred_element_type=f32)
    u = res[:128]+res[128:]
    return u + pltpu.roll(u, 64, 1)

def recur(hy, y, yp):
    t = (hy - C0*y)/HALF
    return t if yp is None else 2.0*t - yp

def local(pos, near, i, k):
    return near[k,i]-32*(2*pos[0]+pos[1])

def slot_of(n):
    return jnp.where(n<0,n+36,jnp.where(n>31,n+4,n))

HALO_SLOTS = ((32,33,34,35,0),(33,34,35,0,1),(30,31,36,37,38),(31,36,37,38,39))

def block(ref, slot):
    return ref[pl.ds(pl.multiple_of(slot*128,128),128),:]

def step_kernel(first, wide, last, pos, near, a2, a2h, p, ph, y, yh, *rest):
    rest = list(rest); ext = rest.pop()
    yp = yph = None
    if not first:
        yp = rest.pop(0); yph = rest.pop(0)
    outs = rest
    g = pl.program_id(0)
    @pl.when(g==0)
    def _():
        ext[0:4096,:] = p[...]
        if wide: ext[4096:5120,:] = ph[...]
        else: ext[4352:4864,:] = ph[...]
    @pl.when(g<8)
    def _():
        for r in range(4):
            hy = apply_row(a2[r],[block(ext,slot_of(local(pos,near,4*g+r,k))) for k in range(5)])
            sl = slice(128*r,128*r+128)
            new = recur(hy,y[sl,:],None if first else yp[sl,:])
            if last:
                outs[0][0,:,sl] = new.T[:64]
            else:
                outs[0][sl,:] = new
                outs[1][sl,:] = dup_pack(new)
    if wide:
        @pl.when(g==8)
        def _():
            for r in range(4):
                hy = apply_row(a2h[r],[ext[128*b:128*b+128,:] for b in HALO_SLOTS[r]])
                sl = slice(128*r,128*r+128)
                new = recur(hy,yh[sl,:],None if first else yph[sl,:])
                outs[2][sl,:] = new
                outs[3][sl,:] = dup_pack(new)

def step(pos, near, a2, a2h, p, ph, y, yh, yp=None, yph=None, wide=False, last=False):
    first = yp is None
    B = pl.BlockSpec
    at = lambda g: jnp.minimum(g,7)
    w = lambda *shape: B(shape, lambda g,p,n: (0,)*len(shape))
    yb = B((512,128),lambda g,p,n:(at(g),0))
    sds = jax.ShapeDtypeStruct
    if last:
        outs=[B((1,64,512),lambda g,p,n:(at(g),0,0))]; shapes=[sds((8,64,512),f32)]
    else:
        outs=[yb,yb]; shapes=[sds((4096,128),f32),sds((4096,128),bf16)]
    if wide:
        outs+=[w(512,128)]*2; shapes+=[sds((512,128),f32),sds((512,128),bf16)]
    return pl.pallas_call(functools.partial(step_kernel,first,wide,last), name="step",
        grid_spec=pltpu.PrefetchScalarGridSpec(num_scalar_prefetch=2, grid=(9 if wide else 8,),
            in_specs=[B((4,256,640),lambda g,p,n:(at(g),0,0)), w(4,256,640), w(4096,128), w(*ph.shape), yb, w(512,128)]+([] if first else [yb,w(512,128)]),
            out_specs=outs, scratch_shapes=[pltpu.VMEM((5120,128),bf16)]),
        out_shape=shapes,
        cost_estimate=pl.CostEstimate(flops=36*2*256*640*128*4,bytes_accessed=16*MB,transcendentals=0),
        compiler_params=pltpu.CompilerParams(vmem_limit_bytes=24*MB))(
            pos,near,a2,a2h,p,ph,y,yh,*([] if first else [yp,yph]))

def edge_kernel(pos, near, alo, ahi, vlo, vhi, ph, ylo, yhi, plo, phi, ye, slo, shi, ext):
    lane = lax.broadcasted_iota(jnp.int32,(128,128),1)
    ext[0:256,:] = ph[0:256,:]
    ext[256:1024,:] = vlo[0:768,:]
    ext[1024:1792,:] = vhi[256:1024,:]
    ext[1792:2048,:] = ph[256:512,:]
    new = []
    for e in range(8):
        a, yr, pr = (alo,ylo,plo) if e<4 else (ahi,yhi,phi)
        hy = apply_row(a[e%4],[block(ext,local(pos,near,e if e<4 else 24+e,k)+(2 if e<4 else -18)) for k in range(5)])
        sl = slice(128*(e%4),128*(e%4)+128)
        new.append(recur(hy,yr[sl,:],pr[sl,:]))
        ye[128*e:128*e+128,:] = new[-1]
    for h in range(2):
        slo[128*h:128*h+128,:] = jnp.where(lane<64,new[2*h],new[2*h+1])
        shi[128*h:128*h+128,:] = jnp.where(lane<64,new[4+2*h],new[5+2*h])

def edge(pos, near, a2, p, ph, y, yp):
    B = pl.BlockSpec
    w = lambda shape,*idx: B(shape, lambda g,p,n: idx)
    ys = [w((512,128),0,0), w((512,128),7,0)]
    sds = jax.ShapeDtypeStruct
    return pl.pallas_call(edge_kernel, name="edge",
        grid_spec=pltpu.PrefetchScalarGridSpec(num_scalar_prefetch=2, grid=(1,),
            in_specs=[w((4,256,640),0,0,0), w((4,256,640),7,0,0), w((1024,128),0,0), w((1024,128),3,0), w((512,128),0,0)]+ys+ys,
            out_specs=[w((1024,128),0,0), w((256,128),0,0), w((256,128),0,0)],
            scratch_shapes=[pltpu.VMEM((2048,128),bf16)]),
        out_shape=[sds((1024,128),f32)]+[sds((256,128),f32)]*2,
        cost_estimate=pl.CostEstimate(flops=8*2*256*640*128,bytes_accessed=5*MB,transcendentals=0),
        compiler_params=pltpu.CompilerParams(vmem_limit_bytes=24*MB))(
            pos,near,a2,a2,p,p,ph,y,y,yp,yp)

def inner_kernel(pos, near, a2, p, ye, y, yp, yo, po):
    g = pl.program_id(0)
    @pl.when((g==0)|(g==7))
    def _():
        new = ye[...]
        yo[...] = new
        po[...] = dup_pack(new)
    @pl.when((g>0)&(g<7))
    def _():
        for r in range(4):
            hy = apply_row(a2[r],[block(p,local(pos,near,4*g+r,k)) for k in range(5)])
            sl = slice(128*r,128*r+128)
            new = recur(hy,y[sl,:],yp[sl,:])
            yo[sl,:] = new
            po[sl,:] = dup_pack(new)

def inner(pos, near, a2, p, ye, y, yp):
    B = pl.BlockSpec
    yb = B((512,128),lambda g,p,n:(g,0))
    sds = jax.ShapeDtypeStruct
    return pl.pallas_call(inner_kernel, name="inner",
        grid_spec=pltpu.PrefetchScalarGridSpec(num_scalar_prefetch=2, grid=(8,),
            in_specs=[B((4,256,640),lambda g,p,n:(g,0,0)), B((4096,128),lambda g,p,n:(0,0)), B((512,128),lambda g,p,n:(g//7,0)), yb, yb],
            out_specs=[yb,yb]),
        out_shape=[sds((4096,128),f32),sds((4096,128),bf16)],
        cost_estimate=pl.CostEstimate(flops=24*2*256*640*128*4,bytes_accessed=16*MB,transcendentals=0),
        compiler_params=pltpu.CompilerParams(vmem_limit_bytes=24*MB))(pos,near,a2,p,ye,y,yp)

NT = ((1,),(1,))
NN = ((1,),(0,))
NORB = 65536

def bdot(a, b, dims):
    return lax.dot_general(a,b,(dims,((),())),preferred_element_type=f32)

def params(mb):
    return pltpu.CompilerParams(vmem_limit_bytes=mb*MB)

SMEM = pl.BlockSpec(memory_space=pltpu.SMEM)
VMEM = pl.BlockSpec(memory_space=pltpu.VMEM)

def gram_kernel(pos, x_ref, o_ref, g_ref):
    half = pl.ds(pl.multiple_of(256*pos[1],256),256)
    xs = [split(x_ref[...]),split(o_ref[...])]
    hs = [split(x_ref[half,:]),split(o_ref[half,:])]
    for i in range(2):
        sl = slice(256*i,256*i+256)
        s = None
        for (xh,xl),(hh,hl) in zip(xs,hs):
            t = bdot(xh[sl],hh,NT)+bdot(xl[sl],hh,NT)+bdot(xh[sl],hl,NT)
            s = t if s is None else s+t
        g_ref[32*i:32*i+32] = s.reshape(32,8,256)

def gram(pos, x, o):
    return call(gram_kernel,"gram",(pos,x,o),sds(64,8,256),3*2*512**3)

def applied_kernel(pos, near, x_ref, hi_ref, a2, yt, xh, xl):
    for ref, at, w in ((x_ref,0,512),(hi_ref,512,256)):
        h, l = split(ref[...])
        xh[:,at:at+w] = h; xl[:,at:at+w] = l
    xh[:,512:768] = xh[:,512:768]*2; xl[:,512:768] = xl[:,512:768]*2
    xh[:,768:896] = jnp.zeros((512,128),bf16); xl[:,768:896] = jnp.zeros((512,128),bf16)
    for i in range(4):
        n = [local(pos,near,4*pos[2]+i,k)-4*pos[2] for k in range(5)]
        at = [pl.ds(pl.multiple_of(jnp.where(m<0,6,m)*128,128),128) for m in n]
        h = jnp.concatenate([xh[:,a] for a in at],axis=1)
        l = jnp.concatenate([xl[:,a] for a in at],axis=1)
        r = bdot(h,a2[i],NT)
        yt[:,128*i:128*i+128] = r[:,:128]+r[:,128:]+bdot(l,a2[i,:128,:],NT)

def applied(pos, near, x, hi, a2):
    B = pl.BlockSpec
    w = lambda shape: B(shape, lambda g,p,n: (0,)*len(shape))
    return pl.pallas_call(applied_kernel, name="applied",
        grid_spec=pltpu.PrefetchScalarGridSpec(num_scalar_prefetch=2, grid=(1,),
            in_specs=[w((512,512)),w((512,256)),w((4,256,640))],
            out_specs=w((512,512)),
            scratch_shapes=[pltpu.VMEM((512,896),bf16),pltpu.VMEM((512,896),bf16)]),
        out_shape=jax.ShapeDtypeStruct((512,512),f32),
        cost_estimate=pl.CostEstimate(flops=4*2*512*512*640,bytes_accessed=5*MB,transcendentals=0),
        compiler_params=params(24))(pos,near,x,hi,a2)

def moment_kernel(pos, x_ref, o_ref, yt_ref, ot_ref, g_ref, lo_ref, hi_ref, s_ref, acc):
    c = pos[1]
    xs = [split(x_ref[...]),split(o_ref[...])]
    tail = jnp.where(c==0,hi_ref[...],lo_ref[...])
    og = jnp.concatenate([tail[8*u+3:8*u+6,:] for u in range(4)],axis=1)
    for q in range(2):
        ws = []
        for x, y, g in ((x_ref,yt_ref,g_ref[...]),(o_ref,ot_ref,og)):
            places = (g+0.5)/32.0-1.0
            if q==0:
                w = jnp.where(c==0,y[...],x[...]*places[1:2,:])
            else:
                w = x[...]*jnp.where(c==0,places[0:1,:],places[2:3,:])
            ws.append(split(w))
        for i in range(2):
            sl = slice(256*i,256*i+256)
            s = None
            for (xh,xl),(yh,yl) in zip(xs,ws):
                t = bdot(xh[sl],yh,NT)+bdot(xl[sl],yh,NT)+bdot(xh[sl],yl,NT)
                s = t if s is None else s+t
            if q==0: acc[sl,:] = s
            else: s_ref[32*i:32*i+32,8:16,:] = s.reshape(32,8,512)
        if q==0:
            for i in range(4):
                sl = slice(128*i,128*i+128)
                s_ref[16*i:16*i+16,0:8,:] = (0.5*(acc[sl,:]+acc[:,sl].T)).reshape(16,8,512)

def moments(pos, x, o, yt, ot, g, lo, hi):
    B = pl.BlockSpec
    w = lambda shape,*idx: B(shape, lambda g: idx)
    full = w((512,512),0,0)
    return pl.pallas_call(moment_kernel, name="moments", grid=(1,),
        in_specs=[SMEM]+[full]*4+[w((3,512),0,0),w((32,128),48,0),w((32,128),48,0)],
        out_specs=w((64,16,512),0,0,0), scratch_shapes=[pltpu.VMEM((512,512),f32)],
        out_shape=jax.ShapeDtypeStruct((64,16,512),f32),
        cost_estimate=pl.CostEstimate(flops=12*2*512**3,bytes_accessed=8*MB,transcendentals=0),
        compiler_params=params(40))(pos,x,o,yt,ot,g,lo,hi)

def total_kernel(p_ref, o_ref):
    o_ref[...] = jnp.broadcast_to(jnp.sum(p_ref[...],axis=0)[None],o_ref.shape)

def total(part):
    return call(total_kernel,"total",(part,),sds(*part.shape),200000)

def half_kernel(pos, s_ref, li_ref, out_ref, lt):
    lane = lax.broadcasted_iota(jnp.int32,(8,128),1)
    sub = lax.broadcasted_iota(jnp.int32,(8,128),0)
    z = hdot(jnp.sum(s_ref[...],axis=0),li_ref[...],NT)
    z0 = z[0:8]; z1 = z[8:16]
    k = 8*pos[0]+pos[2]
    lt[...] = li_ref[:,pl.ds(pl.multiple_of((k//16)*128,128),128)].T
    e = jnp.sum(z0*lt[pl.ds(pl.multiple_of(8*(k%16),8),8),:],axis=0,keepdims=True)
    ee = jnp.zeros((8,128),f32)
    for g in range(8):
        b = jnp.broadcast_to(e[:,128*(g//2):128*(g//2)+128],(8,128))
        if g%2==0: b = pltpu.roll(b,64,1)
        ee = jnp.where(sub==g,b,ee)
    for u in range(4):
        for v in range(4):
            a = z0[:,128*u:128*u+128]; b = z1[:,128*u:128*u+128]
            if v: a = pltpu.roll(a,128-32*v,1)
            if v!=1: b = pltpu.roll(b,(160-32*v)%128,1)
            t = jnp.where(lane<32,a,jnp.where(lane<64,b,ee))
            for y in range(8):
                out_ref[8*(4*u+v)+y] = t

def half(pos, s, li):
    return call(half_kernel,"half",(pos,s,li),sds(128,8,128),2*24*512*512*6,[pltpu.VMEM((128,512),f32)],vmem=24)

def tile_kernel(pos, r_ref, li_ref, p_ref, d_ref, w_ref, e_ref, acc):
    c = pos[1]; gx = 2*pos[0]+c; gy = pos[2]
    lane = lax.broadcasted_iota(jnp.int32,(64,128),1)
    lane8 = lax.broadcasted_iota(jnp.int32,(8,128),1)
    lb = li_ref[pl.ds(pl.multiple_of(64*gy,64),64),:]
    t0 = hdot(lb,r_ref[:,0].reshape(512,128),NN)
    t1 = hdot(lb,r_ref[:,1].reshape(512,128),NN)
    t = jnp.where(lane<64,t0,pltpu.roll(t1,64,1))
    tt = jnp.concatenate([t,t],axis=0).T
    p_ref[...] = tt[0:32,0:64]*(1.0/NORB)
    for q in range(3):
        d_ref[q] = tt[32*q+32:32*q+64,0:64]*(1.0/math.sqrt(NORB))
    e = jnp.sum(r_ref[:,0].reshape(64,8,128),axis=0)
    e_ref[...] = e*(1.0/NORB)
    ea = jnp.broadcast_to(e_ref[pl.ds(pos[0],1),:],(8,128))
    ea = pltpu.roll(ea,64-32*c,1)
    ea = jnp.where(lane8<32,ea,0.0)
    ea = ea+pltpu.roll(ea,32,1)+pltpu.roll(ea,64,1)+pltpu.roll(ea,96,1)
    eb = pltpu.roll(jnp.broadcast_to(e_ref[pl.ds(gy,1),:],(8,128)),64,1)
    eb = jnp.broadcast_to(eb[0:1,:],(128,128)).T[0:64,:]
    gap = eb-jnp.broadcast_to(ea[0:1,:],(64,128))
    dip = t*(1.0/math.sqrt(NORB))
    sq = jnp.where(lane>=32,dip*dip,0.0)
    st = (sq+pltpu.roll(sq,32,1)+pltpu.roll(sq,64,1)+pltpu.roll(sq,96,1))*(0.01/math.pi)
    base = (64*(lane8//32)).astype(f32)+0.5
    for w in range(64):
        om = -0.3+0.6*(base+float(w))/256.0
        tot = jnp.zeros((8,128),f32)
        for b in range(8):
            x = om-gap[8*b:8*b+8,:]
            tot = tot+st[8*b:8*b+8,:]/(x*x+0.0001)
        acc[w:w+1,:] = jnp.sum(tot,axis=0,keepdims=True)
    sel = (lane8//32==lax.broadcasted_iota(jnp.int32,(8,128),0)).astype(f32)
    m = hdot(sel,jnp.concatenate([acc[...],acc[...]],axis=0),NT)*(1.0/(512.0*512.0))
    m = jnp.concatenate([jnp.where(lane8[0:1]<64,m[0:1],m[1:2]),jnp.where(lane8[0:1]<64,m[2:3],m[3:4])],axis=0)
    w_ref[...] = jnp.broadcast_to(m[None],(128,2,128))

def tile(pos, r, li):
    return call(tile_kernel,"tile",(pos,r,li),[sds(32,64),sds(3,32,64),sds(128,2,128)],10000000,[pltpu.VMEM((8,128),f32),pltpu.VMEM((64,128),f32)],vmem=24)

def rotate_kernel(first, pos, x_ref, li_ref, *o_refs):
    xh, xl = split(x_ref[...])
    at = [pl.ds(pl.multiple_of(64*jnp.bitwise_xor(pos[2],first+j),64),64) for j in range(4)]
    lh, ll = split(jnp.concatenate([li_ref[a,:] for a in at],axis=0))
    o = bdot(lh,xh,NN)+bdot(ll,xh,NN)+bdot(lh,xl,NN)
    for j in range(4):
        o_refs[j][...] = o[64*j:64*j+64]

def rotate(pos, x, li, first):
    return call(functools.partial(rotate_kernel,first),"rotate",(pos,x,li),[sds(64,512)]*4,3*512**3,vmem=56)

def gather_kernel(pos, *refs):
    for r in range(8):
        refs[8][:,pl.ds(pl.multiple_of(512*jnp.bitwise_xor(pos[2],r),512),512)] = refs[r][...]

def gather(pos, pieces):
    return call(gather_kernel,"gather",(pos,*pieces),sds(64,4096),1000)

SLABS = ("gq","c")
PEERS = ("gq","gy")
ALL = ("gq","c","gy")

def swap(x, axis):
    return lax.all_to_all(x,axis,split_axis=0,concat_axis=0,tiled=True)

def chain(n):
    return [(i,i+1) for i in range(n-1)], [(i+1,i) for i in range(n-1)]

def shards(hopping_blocks, neighbors, orbital_grid, trial_block):
    gq = lax.axis_index("gq"); c = lax.axis_index("c"); gy = lax.axis_index("gy")
    pos = jnp.stack([gq,c,gy])
    near = neighbors.T
    up, down = chain(16)
    vt = trial_block.T
    sup, sdown, grid = payload(pos,near,hopping_blocks,vt,orbital_grid)
    plo = lax.ppermute(sup,SLABS,up)
    phi = lax.ppermute(sdown,SLABS,down)
    a2, y0, p0, own = prep(pos,hopping_blocks,vt)
    a2h, y0h, p0h = halo_prep(plo,phi)
    y1, p1, y1h, p1h = step(pos,near,a2,a2h,p0,p0h,y0,y0h,wide=True)
    ye, slo, shi = edge(pos,near,a2,p1,p1h,y1,y0)
    lo = lax.ppermute(shi,SLABS,up)
    hi = lax.ppermute(slo,SLABS,down)
    y2, p2 = inner(pos,near,a2,p1,ye,y1,y0)
    y2h, p2h = unpack(lo,hi)
    y3, p3, y3h, p3h = step(pos,near,a2,a2h,p2,p2h,y2,y2h,y1,y1h,wide=True)
    sent, = step(pos,near,a2,a2h,p3,p3h,y3,y3h,y2,y2h,last=True)

    x = swap(sent,"gy").reshape(512,512)
    pair = [(i,i^1) for i in range(16)]
    other = lax.ppermute(x,SLABS,pair)
    hi = lax.ppermute(x[:,:256],ALL,chain(128)[1])
    part = gram(pos,x,other)
    part, xa = lax.optimization_barrier((part,x))
    yt = applied(pos,near,xa,hi,own)
    summed, yt = lax.optimization_barrier((swap(part,PEERS),yt))
    ot = lax.ppermute(yt,SLABS,[(i+1,i) for i in range(0,16,2)])
    both, ot = lax.optimization_barrier((total(summed),ot))
    ga = swap(both,PEERS).reshape(512,256)
    s = moments(pos,x,other,yt,ot,grid,plo,phi)
    s, ga = lax.optimization_barrier((s,ga))
    gb = lax.ppermute(ga,SLABS,pair)
    s, gb = lax.optimization_barrier((s,gb))
    li = chol(pos,ga,gb,1.0/NORB)
    near_q = rotate(pos,x,li,0)
    s, _ = lax.optimization_barrier((swap(s,PEERS),near_q[0]))
    rows = swap(half(pos,s,li),ALL).reshape(8,2,64,128)
    far_q = rotate(pos,x,li,4)
    projected, dipoles, spec = tile(pos,rows,li)
    spectrum = jnp.sum(swap(spec,ALL),axis=0).reshape(256)
    q = [*near_q,*far_q]
    q = [q[0]]+[lax.ppermute(q[r],"gy",[(i,i^r) for i in range(8)]) for r in range(1,8)]
    orthonormal = gather(pos,q).T
    return orthonormal, projected, dipoles, spectrum

def solution(mesh):
    P = jax.sharding.PartitionSpec
    fine = jax.sharding.Mesh(mesh.devices.reshape(8,2,8),ALL)
    return jax.shard_map(shards, mesh=fine,
        in_specs=(P(SLABS,None,None,None),P(SLABS,None),P(None,SLABS),P(SLABS,"gy")),
        out_specs=(P(SLABS,"gy"),P(SLABS,"gy"),P(None,SLABS,"gy"),P()),
        check_vma=False)
```

```python
import functools
import math

import jax
import jax.numpy as jnp
from jax import lax
from jax.experimental import pallas as pl
from jax.experimental.pallas import tpu as pltpu
f32=jnp.float32; bf16=jnp.bfloat16
MB=1<<20

def split(x):
    hi = x.astype(bf16)
    return hi, (x - hi.astype(f32)).astype(bf16)

def inv_chol_128(read, write):
    lane = lax.broadcasted_iota(jnp.int32,(8,128),1)
    sub = lax.broadcasted_iota(jnp.int32,(8,128),0)
    full = lambda v: jnp.broadcast_to(v,(8,128))
    m = [read(g) for g in range(16)]
    for p in range(16):
        j0 = 8*p
        d = m[p]
        c = [full(d[:,j0+l:j0+l+1]) for l in range(8)]
        s = {}; rp = []; rows = []; fin = d
        inpanel = (lane>=j0)&(lane<j0+8)
        for l in range(8):
            piv = full(c[l][l:l+1,:])
            r = 1.0/piv
            rp.append(r)
            mult = jnp.where(sub>l,c[l]*r,0.0)
            for q in range(l+1,8):
                s[l,q] = full(c[q][l:l+1,:])
                c[q] = c[q]-mult*s[l,q]
            row = jnp.where(lane==j0+l,1.0,full(d[l:l+1,:]))
            row = jnp.where(inpanel&(lane>j0+l),0.0,row)
            rows.append(row)
            d = jnp.where((lane==j0+l)&(sub>l),0.0,d)-mult*row
            fin = jnp.where(sub==l,row*lax.rsqrt(piv),fin)
        m[p] = fin
        for g in range(p+1,16):
            v = m[g]
            cg = [full(v[:,j0+l:j0+l+1]) for l in range(8)]
            v = jnp.where(inpanel,0.0,v)
            for l in range(8):
                mult = cg[l]*rp[l]
                for q in range(l+1,8):
                    cg[q] = cg[q]-mult*s[l,q]
                v = v-mult*rows[l]
            m[g] = v
    for g in range(16):
        write(g, jnp.where(lane<=sub+8*g, m[g], 0.0))

def hdot(a,b,dims):
    return lax.dot_general(a,b,(dims,((),())),precision=lax.Precision.HIGHEST,preferred_element_type=f32)

def chol_kernel(scale, g_ref, out_ref):
    for c in range(2):
        out_ref[:,256*c:256*c+256] = g_ref[:,c].reshape(512,256)*scale
    for k in range(4):
        k0 = 128*k
        def read(g): return out_ref[k0+8*g:k0+8*g+8,k0:k0+128]
        def write(g,v): out_ref[k0+8*g:k0+8*g+8,k0:k0+128] = v
        inv_chol_128(read,write)
        x = out_ref[128*k:128*k+128,128*k:128*k+128]
        for j in range(4):
            if j==k: continue
            out_ref[128*k:128*k+128,128*j:128*j+128] = hdot(x,out_ref[128*k:128*k+128,128*j:128*j+128],((1,),(0,)))
        bk = out_ref[128*k:128*k+128,:]
        for i in range(k+1,4):
            w = bk[:,128*i:128*i+128]
            upd = hdot(w,bk,((0,),(0,)))
            for j in range(4):
                if k<j<i: continue
                o = -upd[:,128*j:128*j+128] if j==k else out_ref[128*i:128*i+128,128*j:128*j+128]-upd[:,128*j:128*j+128]
                out_ref[128*i:128*i+128,128*j:128*j+128]=o
        for j in range(k+1,4):
            out_ref[128*k:128*k+128,128*j:128*j+128]=jnp.zeros((128,128),f32)

def call(kernel, name, args, outs, flops, scratch=(), vmem=16):
    single = not isinstance(outs,(list,tuple))
    if vmem < 56:
        whole = lambda v: pl.BlockSpec(memory_space=pltpu.VMEM)
        grid = {}
    else:
        whole = lambda v: pl.BlockSpec(v.shape, lambda g: (0,)*len(v.shape))
        grid = dict(grid=(1,))
    return pl.pallas_call(kernel, name=name, **grid,
        in_specs=[pl.BlockSpec(memory_space=pltpu.SMEM) if v.ndim==1 else whole(v) for v in args],
        out_specs=whole(outs) if single else [whole(v) for v in outs],
        out_shape=outs, scratch_shapes=list(scratch),
        cost_estimate=pl.CostEstimate(flops=flops,bytes_accessed=4*MB,transcendentals=0),
        compiler_params=pltpu.CompilerParams(vmem_limit_bytes=vmem*MB))(*args)

def sds(*shape, dtype=f32):
    return jax.ShapeDtypeStruct(shape,dtype)

def chol(g, scale):
    return call(functools.partial(chol_kernel,scale),"chol",(g,),sds(512,512),8000000000,vmem=56)

def dup_pack(y):
    lane = lax.broadcasted_iota(jnp.int32,y.shape,1)
    hi = y.astype(bf16).astype(f32)
    return jnp.where(lane<64, hi, y-hi).astype(bf16)

def prep_kernel(pos, h_ref, v_ref, a2_ref, y_ref, p_ref, own_ref):
    for r in range(4):
        for k in range(5):
            hi, lo = split(h_ref[r,k])
            a2_ref[r,0:128,128*k:128*k+128] = hi
            a2_ref[r,128:256,128*k:128*k+128] = lo
    @pl.when(pl.program_id(0)==pos[2])
    def _():
        own_ref[...] = a2_ref[...]
    v = v_ref[...]
    y = jnp.concatenate([v,v],axis=0).T
    y_ref[...] = y
    p_ref[...] = dup_pack(y)

def prep(pos, h, vt):
    B = pl.BlockSpec
    yb = B((512,128),lambda g,n:(g,0))
    sds = jax.ShapeDtypeStruct
    return pl.pallas_call(prep_kernel, name="prep",
        grid_spec=pltpu.PrefetchScalarGridSpec(num_scalar_prefetch=1, grid=(8,),
            in_specs=[B((4,5,128,128),lambda g,n:(g,0,0,0)), B((64,512),lambda g,n:(0,g))],
            out_specs=[B((4,256,640),lambda g,n:(g,0,0)), yb, yb, B((4,256,640),lambda g,n:(0,0,0))]),
        out_shape=[sds((32,256,640),bf16), sds((4096,128),f32), sds((4096,128),bf16), sds((4,256,640),bf16)],
        cost_estimate=pl.CostEstimate(flops=1000000,bytes_accessed=25*MB,transcendentals=0),
        compiler_params=pltpu.CompilerParams(vmem_limit_bytes=24*MB))(pos,h,vt)

def payload_kernel(pos, near, ha, hb, va, vb, grid, up_ref, down_ref, g_ref):
    g = grid[...].astype(f32)
    g_ref[...] = g
    base = 32*(2*pos[0]+pos[1])
    for out, h, v, n in ((up_ref,ha,va,30),(down_ref,hb,vb,0)):
        for r in range(2):
            for k in range(5):
                o = near[k,n+r]-base-(n+r)+2
                out[pl.ds(pl.multiple_of(640*r+128*o,128),128),:] = h[r,k]
        for b in range(4):
            out[1280+64*b:1344+64*b,:] = v[:,128*b:128*b+128]
        out[1536:1568,:] = jnp.zeros((32,128),f32)
        for u in range(4):
            out[1539+8*u:1542+8*u,:] = g[:,128*u:128*u+128]

def payload(pos, near, h, vt, grid):
    B = pl.BlockSpec
    w = lambda shape,*idx: B(shape, lambda g,p,n: idx)
    sds = jax.ShapeDtypeStruct
    return pl.pallas_call(payload_kernel, name="payload",
        grid_spec=pltpu.PrefetchScalarGridSpec(num_scalar_prefetch=2, grid=(1,),
            in_specs=[w((2,5,128,128),15,0,0,0),w((2,5,128,128),0,0,0,0),w((64,512),0,7),w((64,512),0,0),B((3,512),lambda g,p,n:(0,p[2]))],
            out_specs=[w((1568,128),0,0)]*2+[w((3,512),0,0)]),
        out_shape=[sds((1568,128),f32)]*2+[sds((3,512),f32)],
        cost_estimate=pl.CostEstimate(flops=1000000,bytes_accessed=4*MB,transcendentals=0),
        compiler_params=pltpu.CompilerParams(vmem_limit_bytes=56*MB))(pos,near,h,h,vt,vt,grid)

def halo_prep_kernel(lo_ref, hi_ref, a2_ref, y_ref, p_ref):
    for s, ref in ((0,lo_ref),(1,hi_ref)):
        for r in range(2):
            for k in range(5):
                at = 128*(5*r+k)
                hi, lo = split(ref[at:at+128,:])
                a2_ref[2*s+r,0:128,128*k:128*k+128] = hi
                a2_ref[2*s+r,128:256,128*k:128*k+128] = lo
        for b in range(4):
            v = ref[1280+64*b:1344+64*b,:]
            y = jnp.concatenate([v,v],axis=0).T
            p_ref[512*s+128*b:512*s+128*b+128,:] = dup_pack(y)
            e = b-2 if s==0 else b
            if 0<=e<2: y_ref[256*s+128*e:256*s+128*e+128,:] = y

def halo_prep(lo, hi):
    return pl.pallas_call(halo_prep_kernel, name="halo_prep",
        out_shape=[jax.ShapeDtypeStruct((4,256,640),bf16), jax.ShapeDtypeStruct((512,128),f32), jax.ShapeDtypeStruct((1024,128),bf16)],
        cost_estimate=pl.CostEstimate(flops=1000000,bytes_accessed=4*MB,transcendentals=0),
        compiler_params=pltpu.CompilerParams(vmem_limit_bytes=16*MB))(lo,hi)

def unpack_kernel(lo_ref, hi_ref, y_ref, p_ref):
    lane = lax.broadcasted_iota(jnp.int32,(128,128),1)
    for s, ref in ((0,lo_ref),(1,hi_ref)):
        for h in range(2):
            x = ref[128*h:128*h+128,:]; xr = pltpu.roll(x,64,1)
            pair = (jnp.where(lane<64,x,xr),jnp.where(lane<64,xr,x))
            for w in range(2):
                b = 2*h+w
                p_ref[512*s+128*b:512*s+128*b+128,:] = dup_pack(pair[w])
                e = b-2 if s==0 else b
                if 0<=e<2: y_ref[256*s+128*e:256*s+128*e+128,:] = pair[w]

def unpack(lo, hi):
    return pl.pallas_call(unpack_kernel, name="unpack",
        out_shape=[jax.ShapeDtypeStruct((512,128),f32), jax.ShapeDtypeStruct((1024,128),bf16)],
        cost_estimate=pl.CostEstimate(flops=1000000,bytes_accessed=MB,transcendentals=0),
        compiler_params=pltpu.CompilerParams(vmem_limit_bytes=16*MB))(lo,hi)

C0, HALF = -0.3, 0.9

def apply_row(a2, pieces):
    rhs = jnp.concatenate(pieces,axis=0)
    res = jnp.dot(a2, rhs, preferred_element_type=f32)
    u = res[:128]+res[128:]
    return u + pltpu.roll(u, 64, 1)

def recur(hy, y, yp):
    t = (hy - C0*y)/HALF
    return t if yp is None else 2.0*t - yp

def local(pos, near, i, k):
    return near[k,i]-32*(2*pos[0]+pos[1])

def slot_of(n):
    return jnp.where(n<0,n+36,jnp.where(n>31,n+4,n))

HALO_SLOTS = ((32,33,34,35,0),(33,34,35,0,1),(30,31,36,37,38),(31,36,37,38,39))

def block(ref, slot):
    return ref[pl.ds(pl.multiple_of(slot*128,128),128),:]

def step_kernel(first, wide, last, pos, near, a2, a2h, p, ph, y, yh, *rest):
    rest = list(rest); ext = rest.pop()
    yp = yph = None
    if not first:
        yp = rest.pop(0); yph = rest.pop(0)
    outs = rest
    g = pl.program_id(0)
    @pl.when(g==0)
    def _():
        ext[0:4096,:] = p[...]
        if wide: ext[4096:5120,:] = ph[...]
        else: ext[4352:4864,:] = ph[...]
    @pl.when(g<8)
    def _():
        for r in range(4):
            hy = apply_row(a2[r],[block(ext,slot_of(local(pos,near,4*g+r,k))) for k in range(5)])
            sl = slice(128*r,128*r+128)
            new = recur(hy,y[sl,:],None if first else yp[sl,:])
            if last:
                outs[0][0,:,sl] = new.T[:64]
            else:
                outs[0][sl,:] = new
                outs[1][sl,:] = dup_pack(new)
    if wide:
        @pl.when(g==8)
        def _():
            for r in range(4):
                hy = apply_row(a2h[r],[ext[128*b:128*b+128,:] for b in HALO_SLOTS[r]])
                sl = slice(128*r,128*r+128)
                new = recur(hy,yh[sl,:],None if first else yph[sl,:])
                outs[2][sl,:] = new
                outs[3][sl,:] = dup_pack(new)

def step(pos, near, a2, a2h, p, ph, y, yh, yp=None, yph=None, wide=False, last=False):
    first = yp is None
    B = pl.BlockSpec
    at = lambda g: jnp.minimum(g,7)
    w = lambda *shape: B(shape, lambda g,p,n: (0,)*len(shape))
    yb = B((512,128),lambda g,p,n:(at(g),0))
    sds = jax.ShapeDtypeStruct
    if last:
        outs=[B((1,64,512),lambda g,p,n:(at(g),0,0))]; shapes=[sds((8,64,512),f32)]
    else:
        outs=[yb,yb]; shapes=[sds((4096,128),f32),sds((4096,128),bf16)]
    if wide:
        outs+=[w(512,128)]*2; shapes+=[sds((512,128),f32),sds((512,128),bf16)]
    return pl.pallas_call(functools.partial(step_kernel,first,wide,last), name="step",
        grid_spec=pltpu.PrefetchScalarGridSpec(num_scalar_prefetch=2, grid=(9 if wide else 8,),
            in_specs=[B((4,256,640),lambda g,p,n:(at(g),0,0)), w(4,256,640), w(4096,128), w(*ph.shape), yb, w(512,128)]+([] if first else [yb,w(512,128)]),
            out_specs=outs, scratch_shapes=[pltpu.VMEM((5120,128),bf16)]),
        out_shape=shapes,
        cost_estimate=pl.CostEstimate(flops=36*2*256*640*128*4,bytes_accessed=16*MB,transcendentals=0),
        compiler_params=pltpu.CompilerParams(vmem_limit_bytes=24*MB))(
            pos,near,a2,a2h,p,ph,y,yh,*([] if first else [yp,yph]))

def edge_kernel(pos, near, alo, ahi, vlo, vhi, ph, ylo, yhi, plo, phi, ye, slo, shi, ext):
    lane = lax.broadcasted_iota(jnp.int32,(128,128),1)
    ext[0:256,:] = ph[0:256,:]
    ext[256:1024,:] = vlo[0:768,:]
    ext[1024:1792,:] = vhi[256:1024,:]
    ext[1792:2048,:] = ph[256:512,:]
    new = []
    for e in range(8):
        a, yr, pr = (alo,ylo,plo) if e<4 else (ahi,yhi,phi)
        hy = apply_row(a[e%4],[block(ext,local(pos,near,e if e<4 else 24+e,k)+(2 if e<4 else -18)) for k in range(5)])
        sl = slice(128*(e%4),128*(e%4)+128)
        new.append(recur(hy,yr[sl,:],pr[sl,:]))
        ye[128*e:128*e+128,:] = new[-1]
    for h in range(2):
        slo[128*h:128*h+128,:] = jnp.where(lane<64,new[2*h],new[2*h+1])
        shi[128*h:128*h+128,:] = jnp.where(lane<64,new[4+2*h],new[5+2*h])

def edge(pos, near, a2, p, ph, y, yp):
    B = pl.BlockSpec
    w = lambda shape,*idx: B(shape, lambda g,p,n: idx)
    ys = [w((512,128),0,0), w((512,128),7,0)]
    sds = jax.ShapeDtypeStruct
    return pl.pallas_call(edge_kernel, name="edge",
        grid_spec=pltpu.PrefetchScalarGridSpec(num_scalar_prefetch=2, grid=(1,),
            in_specs=[w((4,256,640),0,0,0), w((4,256,640),7,0,0), w((1024,128),0,0), w((1024,128),3,0), w((512,128),0,0)]+ys+ys,
            out_specs=[w((1024,128),0,0), w((256,128),0,0), w((256,128),0,0)],
            scratch_shapes=[pltpu.VMEM((2048,128),bf16)]),
        out_shape=[sds((1024,128),f32)]+[sds((256,128),f32)]*2,
        cost_estimate=pl.CostEstimate(flops=8*2*256*640*128,bytes_accessed=5*MB,transcendentals=0),
        compiler_params=pltpu.CompilerParams(vmem_limit_bytes=24*MB))(
            pos,near,a2,a2,p,p,ph,y,y,yp,yp)

def inner_kernel(pos, near, a2, p, ye, y, yp, yo, po):
    g = pl.program_id(0)
    @pl.when((g==0)|(g==7))
    def _():
        new = ye[...]
        yo[...] = new
        po[...] = dup_pack(new)
    @pl.when((g>0)&(g<7))
    def _():
        for r in range(4):
            hy = apply_row(a2[r],[block(p,local(pos,near,4*g+r,k)) for k in range(5)])
            sl = slice(128*r,128*r+128)
            new = recur(hy,y[sl,:],yp[sl,:])
            yo[sl,:] = new
            po[sl,:] = dup_pack(new)

def inner(pos, near, a2, p, ye, y, yp):
    B = pl.BlockSpec
    yb = B((512,128),lambda g,p,n:(g,0))
    sds = jax.ShapeDtypeStruct
    return pl.pallas_call(inner_kernel, name="inner",
        grid_spec=pltpu.PrefetchScalarGridSpec(num_scalar_prefetch=2, grid=(8,),
            in_specs=[B((4,256,640),lambda g,p,n:(g,0,0)), B((4096,128),lambda g,p,n:(0,0)), B((512,128),lambda g,p,n:(g//7,0)), yb, yb],
            out_specs=[yb,yb]),
        out_shape=[sds((4096,128),f32),sds((4096,128),bf16)],
        cost_estimate=pl.CostEstimate(flops=24*2*256*640*128*4,bytes_accessed=16*MB,transcendentals=0),
        compiler_params=pltpu.CompilerParams(vmem_limit_bytes=24*MB))(pos,near,a2,p,ye,y,yp)

NT = ((1,),(1,))
NN = ((1,),(0,))
NORB = 65536

def bdot(a, b, dims):
    return lax.dot_general(a,b,(dims,((),())),preferred_element_type=f32)

def params(mb):
    return pltpu.CompilerParams(vmem_limit_bytes=mb*MB)

SMEM = pl.BlockSpec(memory_space=pltpu.SMEM)
VMEM = pl.BlockSpec(memory_space=pltpu.VMEM)

def gram_kernel(pos, x_ref, o_ref, g_ref):
    half = pl.ds(pl.multiple_of(256*pos[1],256),256)
    xs = [split(x_ref[...]),split(o_ref[...])]
    hs = [split(x_ref[half,:]),split(o_ref[half,:])]
    for i in range(2):
        sl = slice(256*i,256*i+256)
        s = None
        for (xh,xl),(hh,hl) in zip(xs,hs):
            t = bdot(xh[sl],hh,NT)+bdot(xl[sl],hh,NT)+bdot(xh[sl],hl,NT)
            s = t if s is None else s+t
        g_ref[32*i:32*i+32] = s.reshape(32,8,256)

def gram(pos, x, o):
    return call(gram_kernel,"gram",(pos,x,o),sds(64,8,256),3*2*512**3)

def applied_kernel(pos, near, x_ref, hi_ref, a2, yt, xh, xl):
    for ref, at, w in ((x_ref,0,512),(hi_ref,512,256)):
        h, l = split(ref[...])
        xh[:,at:at+w] = h; xl[:,at:at+w] = l
    xh[:,512:768] = xh[:,512:768]*2; xl[:,512:768] = xl[:,512:768]*2
    xh[:,768:896] = jnp.zeros((512,128),bf16); xl[:,768:896] = jnp.zeros((512,128),bf16)
    for i in range(4):
        n = [local(pos,near,4*pos[2]+i,k)-4*pos[2] for k in range(5)]
        at = [pl.ds(pl.multiple_of(jnp.where(m<0,6,m)*128,128),128) for m in n]
        h = jnp.concatenate([xh[:,a] for a in at],axis=1)
        l = jnp.concatenate([xl[:,a] for a in at],axis=1)
        r = bdot(h,a2[i],NT)
        yt[:,128*i:128*i+128] = r[:,:128]+r[:,128:]+bdot(l,a2[i,:128,:],NT)

def applied(pos, near, x, hi, a2):
    B = pl.BlockSpec
    w = lambda shape: B(shape, lambda g,p,n: (0,)*len(shape))
    return pl.pallas_call(applied_kernel, name="applied",
        grid_spec=pltpu.PrefetchScalarGridSpec(num_scalar_prefetch=2, grid=(1,),
            in_specs=[w((512,512)),w((512,256)),w((4,256,640))],
            out_specs=w((512,512)),
            scratch_shapes=[pltpu.VMEM((512,896),bf16),pltpu.VMEM((512,896),bf16)]),
        out_shape=jax.ShapeDtypeStruct((512,512),f32),
        cost_estimate=pl.CostEstimate(flops=4*2*512*512*640,bytes_accessed=5*MB,transcendentals=0),
        compiler_params=params(24))(pos,near,x,hi,a2)

def moment_kernel(pos, x_ref, o_ref, yt_ref, ot_ref, g_ref, lo_ref, hi_ref, s_ref, acc):
    c = pos[1]
    xs = [split(x_ref[...]),split(o_ref[...])]
    tail = jnp.where(c==0,hi_ref[...],lo_ref[...])
    og = jnp.concatenate([tail[8*u+3:8*u+6,:] for u in range(4)],axis=1)
    for q in range(2):
        ws = []
        for x, y, g in ((x_ref,yt_ref,g_ref[...]),(o_ref,ot_ref,og)):
            places = (g+0.5)/32.0-1.0
            if q==0:
                w = jnp.where(c==0,y[...],x[...]*places[1:2,:])
            else:
                w = x[...]*jnp.where(c==0,places[0:1,:],places[2:3,:])
            ws.append(split(w))
        for i in range(2):
            sl = slice(256*i,256*i+256)
            s = None
            for (xh,xl),(yh,yl) in zip(xs,ws):
                t = bdot(xh[sl],yh,NT)+bdot(xl[sl],yh,NT)+bdot(xh[sl],yl,NT)
                s = t if s is None else s+t
            if q==0: acc[sl,:] = s
            else: s_ref[32*i:32*i+32,8:16,:] = s.reshape(32,8,512)
        if q==0:
            for i in range(4):
                sl = slice(128*i,128*i+128)
                s_ref[16*i:16*i+16,0:8,:] = (0.5*(acc[sl,:]+acc[:,sl].T)).reshape(16,8,512)

def moments(pos, x, o, yt, ot, g, lo, hi):
    B = pl.BlockSpec
    w = lambda shape,*idx: B(shape, lambda g: idx)
    full = w((512,512),0,0)
    return pl.pallas_call(moment_kernel, name="moments", grid=(1,),
        in_specs=[SMEM]+[full]*4+[w((3,512),0,0),w((32,128),48,0),w((32,128),48,0)],
        out_specs=w((64,16,512),0,0,0), scratch_shapes=[pltpu.VMEM((512,512),f32)],
        out_shape=jax.ShapeDtypeStruct((64,16,512),f32),
        cost_estimate=pl.CostEstimate(flops=12*2*512**3,bytes_accessed=8*MB,transcendentals=0),
        compiler_params=params(40))(pos,x,o,yt,ot,g,lo,hi)

def total_kernel(p_ref, o_ref):
    o_ref[...] = jnp.broadcast_to(jnp.sum(p_ref[...],axis=0)[None],o_ref.shape)

def total(part):
    return call(total_kernel,"total",(part,),sds(128,8,256),200000)

def half_kernel(pos, s_ref, li_ref, out_ref, lt):
    lane = lax.broadcasted_iota(jnp.int32,(8,128),1)
    sub = lax.broadcasted_iota(jnp.int32,(8,128),0)
    z = hdot(jnp.sum(s_ref[...],axis=0),li_ref[...],NT)
    z0 = z[0:8]; z1 = z[8:16]
    k = 8*pos[0]+pos[2]
    lt[...] = li_ref[:,pl.ds(pl.multiple_of((k//16)*128,128),128)].T
    e = jnp.sum(z0*lt[pl.ds(pl.multiple_of(8*(k%16),8),8),:],axis=0,keepdims=True)
    ee = jnp.zeros((8,128),f32)
    for g in range(8):
        b = jnp.broadcast_to(e[:,128*(g//2):128*(g//2)+128],(8,128))
        if g%2==0: b = pltpu.roll(b,64,1)
        ee = jnp.where(sub==g,b,ee)
    for u in range(4):
        for v in range(4):
            a = z0[:,128*u:128*u+128]; b = z1[:,128*u:128*u+128]
            if v: a = pltpu.roll(a,128-32*v,1)
            if v!=1: b = pltpu.roll(b,(160-32*v)%128,1)
            t = jnp.where(lane<32,a,jnp.where(lane<64,b,ee))
            for y in range(8):
                out_ref[8*(4*u+v)+y] = t

def half(pos, s, li):
    return call(half_kernel,"half",(pos,s,li),sds(128,8,128),2*24*512*512*6,[pltpu.VMEM((128,512),f32)],vmem=24)

def tile_kernel(pos, r_ref, li_ref, p_ref, d_ref, w_ref, e_ref, acc):
    c = pos[1]; gx = 2*pos[0]+c; gy = pos[2]
    lane = lax.broadcasted_iota(jnp.int32,(64,128),1)
    lane8 = lax.broadcasted_iota(jnp.int32,(8,128),1)
    lb = li_ref[pl.ds(pl.multiple_of(64*gy,64),64),:]
    t0 = hdot(lb,r_ref[:,0].reshape(512,128),NN)
    t1 = hdot(lb,r_ref[:,1].reshape(512,128),NN)
    t = jnp.where(lane<64,t0,pltpu.roll(t1,64,1))
    tt = jnp.concatenate([t,t],axis=0).T
    p_ref[...] = tt[0:32,0:64]*(1.0/NORB)
    for q in range(3):
        d_ref[q] = tt[32*q+32:32*q+64,0:64]*(1.0/math.sqrt(NORB))
    e = jnp.sum(r_ref[:,0].reshape(64,8,128),axis=0)
    e_ref[...] = e*(1.0/NORB)
    ea = jnp.broadcast_to(e_ref[pl.ds(pos[0],1),:],(8,128))
    ea = pltpu.roll(ea,64-32*c,1)
    ea = jnp.where(lane8<32,ea,0.0)
    ea = ea+pltpu.roll(ea,32,1)+pltpu.roll(ea,64,1)+pltpu.roll(ea,96,1)
    eb = pltpu.roll(jnp.broadcast_to(e_ref[pl.ds(gy,1),:],(8,128)),64,1)
    eb = jnp.broadcast_to(eb[0:1,:],(128,128)).T[0:64,:]
    gap = eb-jnp.broadcast_to(ea[0:1,:],(64,128))
    dip = t*(1.0/math.sqrt(NORB))
    sq = jnp.where(lane>=32,dip*dip,0.0)
    st = (sq+pltpu.roll(sq,32,1)+pltpu.roll(sq,64,1)+pltpu.roll(sq,96,1))*(0.01/math.pi)
    base = (64*(lane8//32)).astype(f32)+0.5
    for w in range(64):
        om = -0.3+0.6*(base+float(w))/256.0
        tot = jnp.zeros((8,128),f32)
        for b in range(8):
            x = om-gap[8*b:8*b+8,:]
            tot = tot+st[8*b:8*b+8,:]/(x*x+0.0001)
        acc[w:w+1,:] = jnp.sum(tot,axis=0,keepdims=True)
    sel = (lane8//32==lax.broadcasted_iota(jnp.int32,(8,128),0)).astype(f32)
    m = hdot(sel,jnp.concatenate([acc[...],acc[...]],axis=0),NT)*(1.0/(512.0*512.0))
    m = jnp.concatenate([jnp.where(lane8[0:1]<64,m[0:1],m[1:2]),jnp.where(lane8[0:1]<64,m[2:3],m[3:4])],axis=0)
    w_ref[...] = jnp.broadcast_to(m[None],(128,2,128))

def tile(pos, r, li):
    return call(tile_kernel,"tile",(pos,r,li),[sds(32,64),sds(3,32,64),sds(128,2,128)],10000000,[pltpu.VMEM((8,128),f32),pltpu.VMEM((64,128),f32)],vmem=24)

def rotate_kernel(pos, x_ref, li_ref, *o_refs):
    xh, xl = split(x_ref[...])
    for i in range(4):
        at = [pl.ds(pl.multiple_of(64*jnp.bitwise_xor(pos[2],2*i+j),64),64) for j in range(2)]
        lh, ll = split(jnp.concatenate([li_ref[a,:] for a in at],axis=0))
        o = bdot(lh,xh,NN)+bdot(ll,xh,NN)+bdot(lh,xl,NN)
        o_refs[2*i][...] = o[0:64]; o_refs[2*i+1][...] = o[64:128]

def rotate(pos, x, li):
    return call(rotate_kernel,"rotate",(pos,x,li),[sds(64,512)]*8,3*2*512**3,vmem=56)

def gather_kernel(pos, *refs):
    for r in range(8):
        refs[8][:,pl.ds(pl.multiple_of(512*jnp.bitwise_xor(pos[2],r),512),512)] = refs[r][...]

def gather(pos, pieces):
    return call(gather_kernel,"gather",(pos,*pieces),sds(64,4096),1000)

SLABS = ("gq","c")
PEERS = ("gq","gy")
ALL = ("gq","c","gy")

def swap(x, axis):
    return lax.all_to_all(x,axis,split_axis=0,concat_axis=0,tiled=True)

def chain(n):
    return [(i,i+1) for i in range(n-1)], [(i+1,i) for i in range(n-1)]

def shards(hopping_blocks, neighbors, orbital_grid, trial_block):
    gq = lax.axis_index("gq"); c = lax.axis_index("c"); gy = lax.axis_index("gy")
    pos = jnp.stack([gq,c,gy])
    near = neighbors.T
    up, down = chain(16)
    vt = trial_block.T
    sup, sdown, grid = payload(pos,near,hopping_blocks,vt,orbital_grid)
    plo = lax.ppermute(sup,SLABS,up)
    phi = lax.ppermute(sdown,SLABS,down)
    a2, y0, p0, own = prep(pos,hopping_blocks,vt)
    a2h, y0h, p0h = halo_prep(plo,phi)
    y1, p1, y1h, p1h = step(pos,near,a2,a2h,p0,p0h,y0,y0h,wide=True)
    ye, slo, shi = edge(pos,near,a2,p1,p1h,y1,y0)
    lo = lax.ppermute(shi,SLABS,up)
    hi = lax.ppermute(slo,SLABS,down)
    y2, p2 = inner(pos,near,a2,p1,ye,y1,y0)
    y2h, p2h = unpack(lo,hi)
    y3, p3, y3h, p3h = step(pos,near,a2,a2h,p2,p2h,y2,y2h,y1,y1h,wide=True)
    sent, = step(pos,near,a2,a2h,p3,p3h,y3,y3h,y2,y2h,last=True)

    x = swap(sent,"gy").reshape(512,512)
    pair = [(i,i^1) for i in range(16)]
    other = lax.ppermute(x,SLABS,pair)
    hi = lax.ppermute(x[:,:256],ALL,chain(128)[1])
    part = gram(pos,x,other)
    part, xa = lax.optimization_barrier((part,x))
    yt = applied(pos,near,xa,hi,own)
    summed, yt = lax.optimization_barrier((swap(part,PEERS),yt))
    ot = lax.ppermute(yt,SLABS,[(i+1,i) for i in range(0,16,2)])
    both, ot = lax.optimization_barrier((total(summed),ot))
    g = swap(both,ALL).reshape(8,2,64,256)
    s = moments(pos,x,other,yt,ot,grid,plo,phi)
    s, g = lax.optimization_barrier((s,g))
    li = chol(g,1.0/NORB)
    rows = swap(half(pos,swap(s,PEERS),li),ALL).reshape(8,2,64,128)
    projected, dipoles, spec = tile(pos,rows,li)
    q = rotate(pos,x,li)
    q = [q[0]]+[lax.ppermute(q[r],"gy",[(i,i^r) for i in range(8)]) for r in range(1,8)]
    orthonormal = gather(pos,q).T
    spectrum = jnp.sum(swap(spec,ALL),axis=0).reshape(256)
    return orthonormal, projected, dipoles, spectrum

def solution(mesh):
    P = jax.sharding.PartitionSpec
    fine = jax.sharding.Mesh(mesh.devices.reshape(8,2,8),ALL)
    return jax.shard_map(shards, mesh=fine,
        in_specs=(P(SLABS,None,None,None),P(SLABS,None),P(None,SLABS),P(SLABS,"gy")),
        out_specs=(P(SLABS,"gy"),P(SLABS,"gy"),P(None,SLABS,"gy"),P()),
        check_vma=False)
```

```python
import functools
import math

import jax
import jax.numpy as jnp
from jax import lax
from jax.experimental import pallas as pl
from jax.experimental.pallas import tpu as pltpu
f32=jnp.float32; bf16=jnp.bfloat16
MB=1<<20

def split(x):
    hi = x.astype(bf16)
    return hi, (x - hi.astype(f32)).astype(bf16)

def inv_chol_128(read, write):
    lane = lax.broadcasted_iota(jnp.int32,(8,128),1)
    sub = lax.broadcasted_iota(jnp.int32,(8,128),0)
    full = lambda v: jnp.broadcast_to(v,(8,128))
    m = [read(g) for g in range(16)]
    for p in range(16):
        j0 = 8*p
        d = m[p]
        c = [full(d[:,j0+l:j0+l+1]) for l in range(8)]
        s = {}; rp = []; rows = []; fin = d
        inpanel = (lane>=j0)&(lane<j0+8)
        for l in range(8):
            piv = full(c[l][l:l+1,:])
            r = 1.0/piv
            rp.append(r)
            mult = jnp.where(sub>l,c[l]*r,0.0)
            for q in range(l+1,8):
                s[l,q] = full(c[q][l:l+1,:])
                c[q] = c[q]-mult*s[l,q]
            row = jnp.where(lane==j0+l,1.0,full(d[l:l+1,:]))
            row = jnp.where(inpanel&(lane>j0+l),0.0,row)
            rows.append(row)
            d = jnp.where((lane==j0+l)&(sub>l),0.0,d)-mult*row
            fin = jnp.where(sub==l,row*lax.rsqrt(piv),fin)
        m[p] = fin
        for g in range(p+1,16):
            v = m[g]
            cg = [full(v[:,j0+l:j0+l+1]) for l in range(8)]
            v = jnp.where(inpanel,0.0,v)
            for l in range(8):
                mult = cg[l]*rp[l]
                for q in range(l+1,8):
                    cg[q] = cg[q]-mult*s[l,q]
                v = v-mult*rows[l]
            m[g] = v
    for g in range(16):
        write(g, jnp.where(lane<=sub+8*g, m[g], 0.0))

def hdot(a,b,dims):
    return lax.dot_general(a,b,(dims,((),())),precision=lax.Precision.HIGHEST,preferred_element_type=f32)

def chol_kernel(scale, g_ref, out_ref):
    for c in range(2):
        out_ref[:,256*c:256*c+256] = g_ref[:,c].reshape(512,256)*scale
    column = lax.broadcasted_iota(jnp.int32,(128,512),1)//128
    def outer(k, carry):
        k0 = pl.multiple_of(k*128,128)
        rows = pl.ds(k0,128)
        def read(g): return out_ref[pl.ds(k0+8*g,8),rows]
        def write(g,v): out_ref[pl.ds(k0+8*g,8),rows] = v
        inv_chol_128(read,write)
        x = out_ref[rows,rows]
        bk = jnp.where(column==k,jnp.concatenate([x]*4,axis=1),hdot(x,out_ref[rows,:],((1,),(0,))))
        out_ref[rows,:] = bk
        for i in range(1,4):
            @pl.when(k<i)
            def _():
                at = slice(128*i,128*i+128)
                upd = hdot(bk[:,at],bk,((0,),(0,)))
                out_ref[at,:] = jnp.where(column==k,0.0,out_ref[at,:])-upd
        out_ref[rows,:] = jnp.where(column<=k,bk,0.0)
        return carry
    lax.fori_loop(0,4,outer,0)

def call(kernel, name, args, outs, flops, scratch=(), vmem=16):
    single = not isinstance(outs,(list,tuple))
    if vmem < 56:
        whole = lambda v: pl.BlockSpec(memory_space=pltpu.VMEM)
        grid = {}
    else:
        whole = lambda v: pl.BlockSpec(v.shape, lambda g: (0,)*len(v.shape))
        grid = dict(grid=(1,))
    return pl.pallas_call(kernel, name=name, **grid,
        in_specs=[pl.BlockSpec(memory_space=pltpu.SMEM) if v.ndim==1 else whole(v) for v in args],
        out_specs=whole(outs) if single else [whole(v) for v in outs],
        out_shape=outs, scratch_shapes=list(scratch),
        cost_estimate=pl.CostEstimate(flops=flops,bytes_accessed=4*MB,transcendentals=0),
        compiler_params=pltpu.CompilerParams(vmem_limit_bytes=vmem*MB))(*args)

def sds(*shape, dtype=f32):
    return jax.ShapeDtypeStruct(shape,dtype)

def chol(g, scale):
    return call(functools.partial(chol_kernel,scale),"chol",(g,),sds(512,512),8000000000,vmem=56)

def dup_pack(y):
    lane = lax.broadcasted_iota(jnp.int32,y.shape,1)
    hi = y.astype(bf16).astype(f32)
    return jnp.where(lane<64, hi, y-hi).astype(bf16)

def prep_kernel(pos, h_ref, v_ref, a2_ref, y_ref, p_ref, own_ref):
    for r in range(4):
        for k in range(5):
            hi, lo = split(h_ref[r,k])
            a2_ref[r,0:128,128*k:128*k+128] = hi
            a2_ref[r,128:256,128*k:128*k+128] = lo
    @pl.when(pl.program_id(0)==pos[2])
    def _():
        own_ref[...] = a2_ref[...]
    v = v_ref[...]
    y = jnp.concatenate([v,v],axis=0).T
    y_ref[...] = y
    p_ref[...] = dup_pack(y)

def prep(pos, h, vt):
    B = pl.BlockSpec
    yb = B((512,128),lambda g,n:(g,0))
    sds = jax.ShapeDtypeStruct
    return pl.pallas_call(prep_kernel, name="prep",
        grid_spec=pltpu.PrefetchScalarGridSpec(num_scalar_prefetch=1, grid=(8,),
            in_specs=[B((4,5,128,128),lambda g,n:(g,0,0,0)), B((64,512),lambda g,n:(0,g))],
            out_specs=[B((4,256,640),lambda g,n:(g,0,0)), yb, yb, B((4,256,640),lambda g,n:(0,0,0))]),
        out_shape=[sds((32,256,640),bf16), sds((4096,128),f32), sds((4096,128),bf16), sds((4,256,640),bf16)],
        cost_estimate=pl.CostEstimate(flops=1000000,bytes_accessed=25*MB,transcendentals=0),
        compiler_params=pltpu.CompilerParams(vmem_limit_bytes=24*MB))(pos,h,vt)

def payload_kernel(pos, near, ha, hb, va, vb, grid, up_ref, down_ref, g_ref):
    g = grid[...].astype(f32)
    g_ref[...] = g
    base = 32*(2*pos[0]+pos[1])
    for out, h, v, n in ((up_ref,ha,va,30),(down_ref,hb,vb,0)):
        for r in range(2):
            for k in range(5):
                o = near[k,n+r]-base-(n+r)+2
                out[pl.ds(pl.multiple_of(640*r+128*o,128),128),:] = h[r,k]
        for b in range(4):
            out[1280+64*b:1344+64*b,:] = v[:,128*b:128*b+128]
        out[1536:1568,:] = jnp.zeros((32,128),f32)
        for u in range(4):
            out[1539+8*u:1542+8*u,:] = g[:,128*u:128*u+128]

def payload(pos, near, h, vt, grid):
    B = pl.BlockSpec
    w = lambda shape,*idx: B(shape, lambda g,p,n: idx)
    sds = jax.ShapeDtypeStruct
    return pl.pallas_call(payload_kernel, name="payload",
        grid_spec=pltpu.PrefetchScalarGridSpec(num_scalar_prefetch=2, grid=(1,),
            in_specs=[w((2,5,128,128),15,0,0,0),w((2,5,128,128),0,0,0,0),w((64,512),0,7),w((64,512),0,0),B((3,512),lambda g,p,n:(0,p[2]))],
            out_specs=[w((1568,128),0,0)]*2+[w((3,512),0,0)]),
        out_shape=[sds((1568,128),f32)]*2+[sds((3,512),f32)],
        cost_estimate=pl.CostEstimate(flops=1000000,bytes_accessed=4*MB,transcendentals=0),
        compiler_params=pltpu.CompilerParams(vmem_limit_bytes=56*MB))(pos,near,h,h,vt,vt,grid)

def halo_prep_kernel(lo_ref, hi_ref, a2_ref, y_ref, p_ref):
    for s, ref in ((0,lo_ref),(1,hi_ref)):
        for r in range(2):
            for k in range(5):
                at = 128*(5*r+k)
                hi, lo = split(ref[at:at+128,:])
                a2_ref[2*s+r,0:128,128*k:128*k+128] = hi
                a2_ref[2*s+r,128:256,128*k:128*k+128] = lo
        for b in range(4):
            v = ref[1280+64*b:1344+64*b,:]
            y = jnp.concatenate([v,v],axis=0).T
            p_ref[512*s+128*b:512*s+128*b+128,:] = dup_pack(y)
            e = b-2 if s==0 else b
            if 0<=e<2: y_ref[256*s+128*e:256*s+128*e+128,:] = y

def halo_prep(lo, hi):
    return pl.pallas_call(halo_prep_kernel, name="halo_prep",
        out_shape=[jax.ShapeDtypeStruct((4,256,640),bf16), jax.ShapeDtypeStruct((512,128),f32), jax.ShapeDtypeStruct((1024,128),bf16)],
        cost_estimate=pl.CostEstimate(flops=1000000,bytes_accessed=4*MB,transcendentals=0),
        compiler_params=pltpu.CompilerParams(vmem_limit_bytes=16*MB))(lo,hi)

def unpack_kernel(lo_ref, hi_ref, y_ref, p_ref):
    lane = lax.broadcasted_iota(jnp.int32,(128,128),1)
    for s, ref in ((0,lo_ref),(1,hi_ref)):
        for h in range(2):
            x = ref[128*h:128*h+128,:]; xr = pltpu.roll(x,64,1)
            pair = (jnp.where(lane<64,x,xr),jnp.where(lane<64,xr,x))
            for w in range(2):
                b = 2*h+w
                p_ref[512*s+128*b:512*s+128*b+128,:] = dup_pack(pair[w])
                e = b-2 if s==0 else b
                if 0<=e<2: y_ref[256*s+128*e:256*s+128*e+128,:] = pair[w]

def unpack(lo, hi):
    return pl.pallas_call(unpack_kernel, name="unpack",
        out_shape=[jax.ShapeDtypeStruct((512,128),f32), jax.ShapeDtypeStruct((1024,128),bf16)],
        cost_estimate=pl.CostEstimate(flops=1000000,bytes_accessed=MB,transcendentals=0),
        compiler_params=pltpu.CompilerParams(vmem_limit_bytes=16*MB))(lo,hi)

C0, HALF = -0.3, 0.9

def apply_row(a2, pieces):
    rhs = jnp.concatenate(pieces,axis=0)
    res = jnp.dot(a2, rhs, preferred_element_type=f32)
    u = res[:128]+res[128:]
    return u + pltpu.roll(u, 64, 1)

def recur(hy, y, yp):
    t = (hy - C0*y)/HALF
    return t if yp is None else 2.0*t - yp

def local(pos, near, i, k):
    return near[k,i]-32*(2*pos[0]+pos[1])

def slot_of(n):
    return jnp.where(n<0,n+36,jnp.where(n>31,n+4,n))

HALO_SLOTS = ((32,33,34,35,0),(33,34,35,0,1),(30,31,36,37,38),(31,36,37,38,39))

def block(ref, slot):
    return ref[pl.ds(pl.multiple_of(slot*128,128),128),:]

def step_kernel(first, wide, last, pos, near, a2, a2h, p, ph, y, yh, *rest):
    rest = list(rest); ext = rest.pop()
    yp = yph = None
    if not first:
        yp = rest.pop(0); yph = rest.pop(0)
    outs = rest
    g = pl.program_id(0)
    @pl.when(g==0)
    def _():
        ext[0:4096,:] = p[...]
        if wide: ext[4096:5120,:] = ph[...]
        else: ext[4352:4864,:] = ph[...]
    @pl.when(g<8)
    def _():
        for r in range(4):
            hy = apply_row(a2[r],[block(ext,slot_of(local(pos,near,4*g+r,k))) for k in range(5)])
            sl = slice(128*r,128*r+128)
            new = recur(hy,y[sl,:],None if first else yp[sl,:])
            if last:
                outs[0][0,:,sl] = new.T[:64]
            else:
                outs[0][sl,:] = new
                outs[1][sl,:] = dup_pack(new)
    if wide:
        @pl.when(g==8)
        def _():
            for r in range(4):
                hy = apply_row(a2h[r],[ext[128*b:128*b+128,:] for b in HALO_SLOTS[r]])
                sl = slice(128*r,128*r+128)
                new = recur(hy,yh[sl,:],None if first else yph[sl,:])
                outs[2][sl,:] = new
                outs[3][sl,:] = dup_pack(new)

def step(pos, near, a2, a2h, p, ph, y, yh, yp=None, yph=None, wide=False, last=False):
    first = yp is None
    B = pl.BlockSpec
    at = lambda g: jnp.minimum(g,7)
    w = lambda *shape: B(shape, lambda g,p,n: (0,)*len(shape))
    yb = B((512,128),lambda g,p,n:(at(g),0))
    sds = jax.ShapeDtypeStruct
    if last:
        outs=[B((1,64,512),lambda g,p,n:(at(g),0,0))]; shapes=[sds((8,64,512),f32)]
    else:
        outs=[yb,yb]; shapes=[sds((4096,128),f32),sds((4096,128),bf16)]
    if wide:
        outs+=[w(512,128)]*2; shapes+=[sds((512,128),f32),sds((512,128),bf16)]
    return pl.pallas_call(functools.partial(step_kernel,first,wide,last), name="step",
        grid_spec=pltpu.PrefetchScalarGridSpec(num_scalar_prefetch=2, grid=(9 if wide else 8,),
            in_specs=[B((4,256,640),lambda g,p,n:(at(g),0,0)), w(4,256,640), w(4096,128), w(*ph.shape), yb, w(512,128)]+([] if first else [yb,w(512,128)]),
            out_specs=outs, scratch_shapes=[pltpu.VMEM((5120,128),bf16)]),
        out_shape=shapes,
        cost_estimate=pl.CostEstimate(flops=36*2*256*640*128*4,bytes_accessed=16*MB,transcendentals=0),
        compiler_params=pltpu.CompilerParams(vmem_limit_bytes=24*MB))(
            pos,near,a2,a2h,p,ph,y,yh,*([] if first else [yp,yph]))

def edge_kernel(pos, near, alo, ahi, vlo, vhi, ph, ylo, yhi, plo, phi, ye, slo, shi, ext):
    lane = lax.broadcasted_iota(jnp.int32,(128,128),1)
    ext[0:256,:] = ph[0:256,:]
    ext[256:1024,:] = vlo[0:768,:]
    ext[1024:1792,:] = vhi[256:1024,:]
    ext[1792:2048,:] = ph[256:512,:]
    new = []
    for e in range(8):
        a, yr, pr = (alo,ylo,plo) if e<4 else (ahi,yhi,phi)
        hy = apply_row(a[e%4],[block(ext,local(pos,near,e if e<4 else 24+e,k)+(2 if e<4 else -18)) for k in range(5)])
        sl = slice(128*(e%4),128*(e%4)+128)
        new.append(recur(hy,yr[sl,:],pr[sl,:]))
        ye[128*e:128*e+128,:] = new[-1]
    for h in range(2):
        slo[128*h:128*h+128,:] = jnp.where(lane<64,new[2*h],new[2*h+1])
        shi[128*h:128*h+128,:] = jnp.where(lane<64,new[4+2*h],new[5+2*h])

def edge(pos, near, a2, p, ph, y, yp):
    B = pl.BlockSpec
    w = lambda shape,*idx: B(shape, lambda g,p,n: idx)
    ys = [w((512,128),0,0), w((512,128),7,0)]
    sds = jax.ShapeDtypeStruct
    return pl.pallas_call(edge_kernel, name="edge",
        grid_spec=pltpu.PrefetchScalarGridSpec(num_scalar_prefetch=2, grid=(1,),
            in_specs=[w((4,256,640),0,0,0), w((4,256,640),7,0,0), w((1024,128),0,0), w((1024,128),3,0), w((512,128),0,0)]+ys+ys,
            out_specs=[w((1024,128),0,0), w((256,128),0,0), w((256,128),0,0)],
            scratch_shapes=[pltpu.VMEM((2048,128),bf16)]),
        out_shape=[sds((1024,128),f32)]+[sds((256,128),f32)]*2,
        cost_estimate=pl.CostEstimate(flops=8*2*256*640*128,bytes_accessed=5*MB,transcendentals=0),
        compiler_params=pltpu.CompilerParams(vmem_limit_bytes=24*MB))(
            pos,near,a2,a2,p,p,ph,y,y,yp,yp)

def inner_kernel(pos, near, a2, p, ye, y, yp, yo, po):
    g = pl.program_id(0)
    @pl.when((g==0)|(g==7))
    def _():
        new = ye[...]
        yo[...] = new
        po[...] = dup_pack(new)
    @pl.when((g>0)&(g<7))
    def _():
        for r in range(4):
            hy = apply_row(a2[r],[block(p,local(pos,near,4*g+r,k)) for k in range(5)])
            sl = slice(128*r,128*r+128)
            new = recur(hy,y[sl,:],yp[sl,:])
            yo[sl,:] = new
            po[sl,:] = dup_pack(new)

def inner(pos, near, a2, p, ye, y, yp):
    B = pl.BlockSpec
    yb = B((512,128),lambda g,p,n:(g,0))
    sds = jax.ShapeDtypeStruct
    return pl.pallas_call(inner_kernel, name="inner",
        grid_spec=pltpu.PrefetchScalarGridSpec(num_scalar_prefetch=2, grid=(8,),
            in_specs=[B((4,256,640),lambda g,p,n:(g,0,0)), B((4096,128),lambda g,p,n:(0,0)), B((512,128),lambda g,p,n:(g//7,0)), yb, yb],
            out_specs=[yb,yb]),
        out_shape=[sds((4096,128),f32),sds((4096,128),bf16)],
        cost_estimate=pl.CostEstimate(flops=24*2*256*640*128*4,bytes_accessed=16*MB,transcendentals=0),
        compiler_params=pltpu.CompilerParams(vmem_limit_bytes=24*MB))(pos,near,a2,p,ye,y,yp)

NT = ((1,),(1,))
NN = ((1,),(0,))
NORB = 65536

def bdot(a, b, dims):
    return lax.dot_general(a,b,(dims,((),())),preferred_element_type=f32)

def params(mb):
    return pltpu.CompilerParams(vmem_limit_bytes=mb*MB)

SMEM = pl.BlockSpec(memory_space=pltpu.SMEM)
VMEM = pl.BlockSpec(memory_space=pltpu.VMEM)

def gram_kernel(pos, x_ref, o_ref, g_ref):
    half = pl.ds(pl.multiple_of(256*pos[1],256),256)
    xs = [split(x_ref[...]),split(o_ref[...])]
    hs = [split(x_ref[half,:]),split(o_ref[half,:])]
    for i in range(2):
        sl = slice(256*i,256*i+256)
        s = None
        for (xh,xl),(hh,hl) in zip(xs,hs):
            t = bdot(xh[sl],hh,NT)+bdot(xl[sl],hh,NT)+bdot(xh[sl],hl,NT)
            s = t if s is None else s+t
        g_ref[32*i:32*i+32] = s.reshape(32,8,256)

def gram(pos, x, o):
    return call(gram_kernel,"gram",(pos,x,o),sds(64,8,256),3*2*512**3)

def applied_kernel(pos, near, x_ref, hi_ref, a2, yt, xh, xl):
    for ref, at, w in ((x_ref,0,512),(hi_ref,512,256)):
        h, l = split(ref[...])
        xh[:,at:at+w] = h; xl[:,at:at+w] = l
    xh[:,512:768] = xh[:,512:768]*2; xl[:,512:768] = xl[:,512:768]*2
    xh[:,768:896] = jnp.zeros((512,128),bf16); xl[:,768:896] = jnp.zeros((512,128),bf16)
    for i in range(4):
        n = [local(pos,near,4*pos[2]+i,k)-4*pos[2] for k in range(5)]
        at = [pl.ds(pl.multiple_of(jnp.where(m<0,6,m)*128,128),128) for m in n]
        h = jnp.concatenate([xh[:,a] for a in at],axis=1)
        l = jnp.concatenate([xl[:,a] for a in at],axis=1)
        r = bdot(h,a2[i],NT)
        yt[:,128*i:128*i+128] = r[:,:128]+r[:,128:]+bdot(l,a2[i,:128,:],NT)

def applied(pos, near, x, hi, a2):
    B = pl.BlockSpec
    w = lambda shape: B(shape, lambda g,p,n: (0,)*len(shape))
    return pl.pallas_call(applied_kernel, name="applied",
        grid_spec=pltpu.PrefetchScalarGridSpec(num_scalar_prefetch=2, grid=(1,),
            in_specs=[w((512,512)),w((512,256)),w((4,256,640))],
            out_specs=w((512,512)),
            scratch_shapes=[pltpu.VMEM((512,896),bf16),pltpu.VMEM((512,896),bf16)]),
        out_shape=jax.ShapeDtypeStruct((512,512),f32),
        cost_estimate=pl.CostEstimate(flops=4*2*512*512*640,bytes_accessed=5*MB,transcendentals=0),
        compiler_params=params(24))(pos,near,x,hi,a2)

def moment_kernel(pos, x_ref, o_ref, yt_ref, ot_ref, g_ref, lo_ref, hi_ref, s_ref, acc):
    c = pos[1]
    xs = [split(x_ref[...]),split(o_ref[...])]
    tail = jnp.where(c==0,hi_ref[...],lo_ref[...])
    og = jnp.concatenate([tail[8*u+3:8*u+6,:] for u in range(4)],axis=1)
    for q in range(2):
        ws = []
        for x, y, g in ((x_ref,yt_ref,g_ref[...]),(o_ref,ot_ref,og)):
            places = (g+0.5)/32.0-1.0
            if q==0:
                w = jnp.where(c==0,y[...],x[...]*places[1:2,:])
            else:
                w = x[...]*jnp.where(c==0,places[0:1,:],places[2:3,:])
            ws.append(split(w))
        for i in range(2):
            sl = slice(256*i,256*i+256)
            s = None
            for (xh,xl),(yh,yl) in zip(xs,ws):
                t = bdot(xh[sl],yh,NT)+bdot(xl[sl],yh,NT)+bdot(xh[sl],yl,NT)
                s = t if s is None else s+t
            if q==0: acc[sl,:] = s
            else: s_ref[32*i:32*i+32,8:16,:] = s.reshape(32,8,512)
        if q==0:
            for i in range(4):
                sl = slice(128*i,128*i+128)
                s_ref[16*i:16*i+16,0:8,:] = (0.5*(acc[sl,:]+acc[:,sl].T)).reshape(16,8,512)

def moments(pos, x, o, yt, ot, g, lo, hi):
    B = pl.BlockSpec
    w = lambda shape,*idx: B(shape, lambda g: idx)
    full = w((512,512),0,0)
    return pl.pallas_call(moment_kernel, name="moments", grid=(1,),
        in_specs=[SMEM]+[full]*4+[w((3,512),0,0),w((32,128),48,0),w((32,128),48,0)],
        out_specs=w((64,16,512),0,0,0), scratch_shapes=[pltpu.VMEM((512,512),f32)],
        out_shape=jax.ShapeDtypeStruct((64,16,512),f32),
        cost_estimate=pl.CostEstimate(flops=12*2*512**3,bytes_accessed=8*MB,transcendentals=0),
        compiler_params=params(40))(pos,x,o,yt,ot,g,lo,hi)

def total_kernel(p_ref, o_ref):
    o_ref[...] = jnp.broadcast_to(jnp.sum(p_ref[...],axis=0)[None],o_ref.shape)

def total(part):
    return call(total_kernel,"total",(part,),sds(128,8,256),200000)

def half_kernel(pos, s_ref, li_ref, out_ref, lt):
    lane = lax.broadcasted_iota(jnp.int32,(8,128),1)
    sub = lax.broadcasted_iota(jnp.int32,(8,128),0)
    z = hdot(jnp.sum(s_ref[...],axis=0),li_ref[...],NT)
    z0 = z[0:8]; z1 = z[8:16]
    k = 8*pos[0]+pos[2]
    lt[...] = li_ref[:,pl.ds(pl.multiple_of((k//16)*128,128),128)].T
    e = jnp.sum(z0*lt[pl.ds(pl.multiple_of(8*(k%16),8),8),:],axis=0,keepdims=True)
    ee = jnp.zeros((8,128),f32)
    for g in range(8):
        b = jnp.broadcast_to(e[:,128*(g//2):128*(g//2)+128],(8,128))
        if g%2==0: b = pltpu.roll(b,64,1)
        ee = jnp.where(sub==g,b,ee)
    for u in range(4):
        for v in range(4):
            a = z0[:,128*u:128*u+128]; b = z1[:,128*u:128*u+128]
            if v: a = pltpu.roll(a,128-32*v,1)
            if v!=1: b = pltpu.roll(b,(160-32*v)%128,1)
            t = jnp.where(lane<32,a,jnp.where(lane<64,b,ee))
            for y in range(8):
                out_ref[8*(4*u+v)+y] = t

def half(pos, s, li):
    return call(half_kernel,"half",(pos,s,li),sds(128,8,128),2*24*512*512*6,[pltpu.VMEM((128,512),f32)],vmem=24)

def tile_kernel(pos, r_ref, li_ref, p_ref, d_ref, w_ref, e_ref, acc):
    c = pos[1]; gx = 2*pos[0]+c; gy = pos[2]
    lane = lax.broadcasted_iota(jnp.int32,(64,128),1)
    lane8 = lax.broadcasted_iota(jnp.int32,(8,128),1)
    lb = li_ref[pl.ds(pl.multiple_of(64*gy,64),64),:]
    t0 = hdot(lb,r_ref[:,0].reshape(512,128),NN)
    t1 = hdot(lb,r_ref[:,1].reshape(512,128),NN)
    t = jnp.where(lane<64,t0,pltpu.roll(t1,64,1))
    tt = jnp.concatenate([t,t],axis=0).T
    p_ref[...] = tt[0:32,0:64]*(1.0/NORB)
    for q in range(3):
        d_ref[q] = tt[32*q+32:32*q+64,0:64]*(1.0/math.sqrt(NORB))
    e = jnp.sum(r_ref[:,0].reshape(64,8,128),axis=0)
    e_ref[...] = e*(1.0/NORB)
    ea = jnp.broadcast_to(e_ref[pl.ds(pos[0],1),:],(8,128))
    ea = pltpu.roll(ea,64-32*c,1)
    ea = jnp.where(lane8<32,ea,0.0)
    ea = ea+pltpu.roll(ea,32,1)+pltpu.roll(ea,64,1)+pltpu.roll(ea,96,1)
    eb = pltpu.roll(jnp.broadcast_to(e_ref[pl.ds(gy,1),:],(8,128)),64,1)
    eb = jnp.broadcast_to(eb[0:1,:],(128,128)).T[0:64,:]
    gap = eb-jnp.broadcast_to(ea[0:1,:],(64,128))
    dip = t*(1.0/math.sqrt(NORB))
    sq = jnp.where(lane>=32,dip*dip,0.0)
    st = (sq+pltpu.roll(sq,32,1)+pltpu.roll(sq,64,1)+pltpu.roll(sq,96,1))*(0.01/math.pi)
    base = (64*(lane8//32)).astype(f32)+0.5
    for w in range(64):
        om = -0.3+0.6*(base+float(w))/256.0
        tot = jnp.zeros((8,128),f32)
        for b in range(8):
            x = om-gap[8*b:8*b+8,:]
            tot = tot+st[8*b:8*b+8,:]/(x*x+0.0001)
        acc[w:w+1,:] = jnp.sum(tot,axis=0,keepdims=True)
    sel = (lane8//32==lax.broadcasted_iota(jnp.int32,(8,128),0)).astype(f32)
    m = hdot(sel,jnp.concatenate([acc[...],acc[...]],axis=0),NT)*(1.0/(512.0*512.0))
    m = jnp.concatenate([jnp.where(lane8[0:1]<64,m[0:1],m[1:2]),jnp.where(lane8[0:1]<64,m[2:3],m[3:4])],axis=0)
    w_ref[...] = jnp.broadcast_to(m[None],(128,2,128))

def tile(pos, r, li):
    return call(tile_kernel,"tile",(pos,r,li),[sds(32,64),sds(3,32,64),sds(128,2,128)],10000000,[pltpu.VMEM((8,128),f32),pltpu.VMEM((64,128),f32)],vmem=24)

def rotate_kernel(pos, x_ref, li_ref, *o_refs):
    xh, xl = split(x_ref[...])
    for i in range(4):
        at = [pl.ds(pl.multiple_of(64*jnp.bitwise_xor(pos[2],2*i+j),64),64) for j in range(2)]
        lh, ll = split(jnp.concatenate([li_ref[a,:] for a in at],axis=0))
        o = bdot(lh,xh,NN)+bdot(ll,xh,NN)+bdot(lh,xl,NN)
        o_refs[2*i][...] = o[0:64]; o_refs[2*i+1][...] = o[64:128]

def rotate(pos, x, li):
    return call(rotate_kernel,"rotate",(pos,x,li),[sds(64,512)]*8,3*2*512**3,vmem=56)

def gather_kernel(pos, *refs):
    for r in range(8):
        refs[8][:,pl.ds(pl.multiple_of(512*jnp.bitwise_xor(pos[2],r),512),512)] = refs[r][...]

def gather(pos, pieces):
    return call(gather_kernel,"gather",(pos,*pieces),sds(64,4096),1000)

SLABS = ("gq","c")
PEERS = ("gq","gy")
ALL = ("gq","c","gy")

def swap(x, axis):
    return lax.all_to_all(x,axis,split_axis=0,concat_axis=0,tiled=True)

def chain(n):
    return [(i,i+1) for i in range(n-1)], [(i+1,i) for i in range(n-1)]

def shards(hopping_blocks, neighbors, orbital_grid, trial_block):
    gq = lax.axis_index("gq"); c = lax.axis_index("c"); gy = lax.axis_index("gy")
    pos = jnp.stack([gq,c,gy])
    near = neighbors.T
    up, down = chain(16)
    vt = trial_block.T
    sup, sdown, grid = payload(pos,near,hopping_blocks,vt,orbital_grid)
    plo = lax.ppermute(sup,SLABS,up)
    phi = lax.ppermute(sdown,SLABS,down)
    a2, y0, p0, own = prep(pos,hopping_blocks,vt)
    a2h, y0h, p0h = halo_prep(plo,phi)
    y1, p1, y1h, p1h = step(pos,near,a2,a2h,p0,p0h,y0,y0h,wide=True)
    ye, slo, shi = edge(pos,near,a2,p1,p1h,y1,y0)
    lo = lax.ppermute(shi,SLABS,up)
    hi = lax.ppermute(slo,SLABS,down)
    y2, p2 = inner(pos,near,a2,p1,ye,y1,y0)
    y2h, p2h = unpack(lo,hi)
    y3, p3, y3h, p3h = step(pos,near,a2,a2h,p2,p2h,y2,y2h,y1,y1h,wide=True)
    sent, = step(pos,near,a2,a2h,p3,p3h,y3,y3h,y2,y2h,last=True)

    x = swap(sent,"gy").reshape(512,512)
    pair = [(i,i^1) for i in range(16)]
    other = lax.ppermute(x,SLABS,pair)
    hi = lax.ppermute(x[:,:256],ALL,chain(128)[1])
    part = gram(pos,x,other)
    part, xa = lax.optimization_barrier((part,x))
    yt = applied(pos,near,xa,hi,own)
    summed, yt = lax.optimization_barrier((swap(part,PEERS),yt))
    ot = lax.ppermute(yt,SLABS,[(i+1,i) for i in range(0,16,2)])
    both, ot = lax.optimization_barrier((total(summed),ot))
    g = swap(both,ALL).reshape(8,2,64,256)
    s = moments(pos,x,other,yt,ot,grid,plo,phi)
    s, g = lax.optimization_barrier((s,g))
    li = chol(g,1.0/NORB)
    rows = swap(half(pos,swap(s,PEERS),li),ALL).reshape(8,2,64,128)
    projected, dipoles, spec = tile(pos,rows,li)
    q = rotate(pos,x,li)
    q = [q[0]]+[lax.ppermute(q[r],"gy",[(i,i^r) for i in range(8)]) for r in range(1,8)]
    orthonormal = gather(pos,q).T
    spectrum = jnp.sum(swap(spec,ALL),axis=0).reshape(256)
    return orthonormal, projected, dipoles, spectrum

def solution(mesh):
    P = jax.sharding.PartitionSpec
    fine = jax.sharding.Mesh(mesh.devices.reshape(8,2,8),ALL)
    return jax.shard_map(shards, mesh=fine,
        in_specs=(P(SLABS,None,None,None),P(SLABS,None),P(None,SLABS),P(SLABS,"gy")),
        out_specs=(P(SLABS,"gy"),P(SLABS,"gy"),P(None,SLABS,"gy"),P()),
        check_vma=False)
```

```python
import functools
import math

import jax
import jax.numpy as jnp
from jax import lax
from jax.experimental import pallas as pl
from jax.experimental.pallas import tpu as pltpu
f32=jnp.float32; bf16=jnp.bfloat16
MB=1<<20

def split(x):
    hi = x.astype(bf16)
    return hi, (x - hi.astype(f32)).astype(bf16)

def inv_chol_128(read, write):
    lane = lax.broadcasted_iota(jnp.int32,(8,128),1)
    sub = lax.broadcasted_iota(jnp.int32,(8,128),0)
    full = lambda v: jnp.broadcast_to(v,(8,128))
    m = [read(g) for g in range(16)]
    for p in range(16):
        j0 = 8*p
        d = m[p]
        c = [full(d[:,j0+l:j0+l+1]) for l in range(8)]
        s = {}; rp = []; rows = []; fin = d
        inpanel = (lane>=j0)&(lane<j0+8)
        for l in range(8):
            piv = full(c[l][l:l+1,:])
            r = 1.0/piv
            rp.append(r)
            mult = jnp.where(sub>l,c[l]*r,0.0)
            for q in range(l+1,8):
                s[l,q] = full(c[q][l:l+1,:])
                c[q] = c[q]-mult*s[l,q]
            row = jnp.where(lane==j0+l,1.0,full(d[l:l+1,:]))
            row = jnp.where(inpanel&(lane>j0+l),0.0,row)
            rows.append(row)
            d = jnp.where((lane==j0+l)&(sub>l),0.0,d)-mult*row
            fin = jnp.where(sub==l,row*lax.rsqrt(piv),fin)
        m[p] = fin
        for g in range(p+1,16):
            v = m[g]
            cg = [full(v[:,j0+l:j0+l+1]) for l in range(8)]
            v = jnp.where(inpanel,0.0,v)
            for l in range(8):
                mult = cg[l]*rp[l]
                for q in range(l+1,8):
                    cg[q] = cg[q]-mult*s[l,q]
                v = v-mult*rows[l]
            m[g] = v
    for g in range(16):
        write(g, jnp.where(lane<=sub+8*g, m[g], 0.0))

def hdot(a,b,dims):
    return lax.dot_general(a,b,(dims,((),())),precision=lax.Precision.HIGHEST,preferred_element_type=f32)

def chol_kernel(scale, g_ref, out_ref):
    for c in range(2):
        out_ref[:,256*c:256*c+256] = g_ref[:,c].reshape(512,256)*scale
    column = lax.broadcasted_iota(jnp.int32,(128,512),1)//128
    def outer(k, carry):
        k0 = pl.multiple_of(k*128,128)
        rows = pl.ds(k0,128)
        def read(g): return out_ref[pl.ds(k0+8*g,8),rows]
        def write(g,v): out_ref[pl.ds(k0+8*g,8),rows] = v
        inv_chol_128(read,write)
        x = out_ref[rows,rows]
        bk = jnp.where(column==k,jnp.concatenate([x]*4,axis=1),hdot(x,out_ref[rows,:],((1,),(0,))))
        out_ref[rows,:] = bk
        for i in range(1,4):
            @pl.when(k<i)
            def _():
                at = slice(128*i,128*i+128)
                upd = hdot(bk[:,at],bk,((0,),(0,)))
                out_ref[at,:] = jnp.where(column==k,0.0,out_ref[at,:])-upd
        out_ref[rows,:] = jnp.where(column<=k,bk,0.0)
        return carry
    lax.fori_loop(0,4,outer,0)

def call(kernel, name, args, outs, flops, scratch=(), vmem=16):
    single = not isinstance(outs,(list,tuple))
    if vmem < 56:
        whole = lambda v: pl.BlockSpec(memory_space=pltpu.VMEM)
        grid = {}
    else:
        whole = lambda v: pl.BlockSpec(v.shape, lambda g: (0,)*len(v.shape))
        grid = dict(grid=(1,))
    return pl.pallas_call(kernel, name=name, **grid,
        in_specs=[pl.BlockSpec(memory_space=pltpu.SMEM) if v.ndim==1 else whole(v) for v in args],
        out_specs=whole(outs) if single else [whole(v) for v in outs],
        out_shape=outs, scratch_shapes=list(scratch),
        cost_estimate=pl.CostEstimate(flops=flops,bytes_accessed=4*MB,transcendentals=0),
        compiler_params=pltpu.CompilerParams(vmem_limit_bytes=vmem*MB))(*args)

def sds(*shape, dtype=f32):
    return jax.ShapeDtypeStruct(shape,dtype)

def chol(g, scale):
    return call(functools.partial(chol_kernel,scale),"chol",(g,),sds(512,512),8000000000,vmem=56)

def dup_pack(y):
    lane = lax.broadcasted_iota(jnp.int32,y.shape,1)
    hi = y.astype(bf16).astype(f32)
    return jnp.where(lane<64, hi, y-hi).astype(bf16)

def prep_kernel(pos, h_ref, v_ref, a2_ref, y_ref, p_ref, own_ref):
    for r in range(4):
        for k in range(5):
            hi, lo = split(h_ref[r,k])
            a2_ref[r,0:128,128*k:128*k+128] = hi
            a2_ref[r,128:256,128*k:128*k+128] = lo
    @pl.when(pl.program_id(0)==pos[2])
    def _():
        own_ref[...] = a2_ref[...]
    v = v_ref[...]
    y = jnp.concatenate([v,v],axis=0).T
    y_ref[...] = y
    p_ref[...] = dup_pack(y)

def prep(pos, h, vt):
    B = pl.BlockSpec
    yb = B((512,128),lambda g,n:(g,0))
    sds = jax.ShapeDtypeStruct
    return pl.pallas_call(prep_kernel, name="prep",
        grid_spec=pltpu.PrefetchScalarGridSpec(num_scalar_prefetch=1, grid=(8,),
            in_specs=[B((4,5,128,128),lambda g,n:(g,0,0,0)), B((64,512),lambda g,n:(0,g))],
            out_specs=[B((4,256,640),lambda g,n:(g,0,0)), yb, yb, B((4,256,640),lambda g,n:(0,0,0))]),
        out_shape=[sds((32,256,640),bf16), sds((4096,128),f32), sds((4096,128),bf16), sds((4,256,640),bf16)],
        cost_estimate=pl.CostEstimate(flops=1000000,bytes_accessed=25*MB,transcendentals=0),
        compiler_params=pltpu.CompilerParams(vmem_limit_bytes=24*MB))(pos,h,vt)

def payload_kernel(pos, near, ha, hb, va, vb, grid, up_ref, down_ref, g_ref):
    g = grid[...].astype(f32)
    g_ref[...] = g
    base = 32*(2*pos[0]+pos[1])
    for out, h, v, n in ((up_ref,ha,va,30),(down_ref,hb,vb,0)):
        for r in range(2):
            for k in range(5):
                o = near[k,n+r]-base-(n+r)+2
                out[pl.ds(pl.multiple_of(640*r+128*o,128),128),:] = h[r,k]
        for b in range(4):
            out[1280+64*b:1344+64*b,:] = v[:,128*b:128*b+128]
        out[1536:1568,:] = jnp.zeros((32,128),f32)
        for u in range(4):
            out[1539+8*u:1542+8*u,:] = g[:,128*u:128*u+128]

def payload(pos, near, h, vt, grid):
    B = pl.BlockSpec
    w = lambda shape,*idx: B(shape, lambda g,p,n: idx)
    sds = jax.ShapeDtypeStruct
    return pl.pallas_call(payload_kernel, name="payload",
        grid_spec=pltpu.PrefetchScalarGridSpec(num_scalar_prefetch=2, grid=(1,),
            in_specs=[w((2,5,128,128),15,0,0,0),w((2,5,128,128),0,0,0,0),w((64,512),0,7),w((64,512),0,0),B((3,512),lambda g,p,n:(0,p[2]))],
            out_specs=[w((1568,128),0,0)]*2+[w((3,512),0,0)]),
        out_shape=[sds((1568,128),f32)]*2+[sds((3,512),f32)],
        cost_estimate=pl.CostEstimate(flops=1000000,bytes_accessed=4*MB,transcendentals=0),
        compiler_params=pltpu.CompilerParams(vmem_limit_bytes=56*MB))(pos,near,h,h,vt,vt,grid)

def halo_prep_kernel(lo_ref, hi_ref, a2_ref, y_ref, p_ref):
    for s, ref in ((0,lo_ref),(1,hi_ref)):
        for r in range(2):
            for k in range(5):
                at = 128*(5*r+k)
                hi, lo = split(ref[at:at+128,:])
                a2_ref[2*s+r,0:128,128*k:128*k+128] = hi
                a2_ref[2*s+r,128:256,128*k:128*k+128] = lo
        for b in range(4):
            v = ref[1280+64*b:1344+64*b,:]
            y = jnp.concatenate([v,v],axis=0).T
            p_ref[512*s+128*b:512*s+128*b+128,:] = dup_pack(y)
            e = b-2 if s==0 else b
            if 0<=e<2: y_ref[256*s+128*e:256*s+128*e+128,:] = y

def halo_prep(lo, hi):
    return pl.pallas_call(halo_prep_kernel, name="halo_prep",
        out_shape=[jax.ShapeDtypeStruct((4,256,640),bf16), jax.ShapeDtypeStruct((512,128),f32), jax.ShapeDtypeStruct((1024,128),bf16)],
        cost_estimate=pl.CostEstimate(flops=1000000,bytes_accessed=4*MB,transcendentals=0),
        compiler_params=pltpu.CompilerParams(vmem_limit_bytes=16*MB))(lo,hi)

def unpack_kernel(lo_ref, hi_ref, y_ref, p_ref):
    lane = lax.broadcasted_iota(jnp.int32,(128,128),1)
    for s, ref in ((0,lo_ref),(1,hi_ref)):
        for h in range(2):
            x = ref[128*h:128*h+128,:]; xr = pltpu.roll(x,64,1)
            pair = (jnp.where(lane<64,x,xr),jnp.where(lane<64,xr,x))
            for w in range(2):
                b = 2*h+w
                p_ref[512*s+128*b:512*s+128*b+128,:] = dup_pack(pair[w])
                e = b-2 if s==0 else b
                if 0<=e<2: y_ref[256*s+128*e:256*s+128*e+128,:] = pair[w]

def unpack(lo, hi):
    return pl.pallas_call(unpack_kernel, name="unpack",
        out_shape=[jax.ShapeDtypeStruct((512,128),f32), jax.ShapeDtypeStruct((1024,128),bf16)],
        cost_estimate=pl.CostEstimate(flops=1000000,bytes_accessed=MB,transcendentals=0),
        compiler_params=pltpu.CompilerParams(vmem_limit_bytes=16*MB))(lo,hi)

C0, HALF = -0.3, 0.9

def apply_row(a2, pieces):
    rhs = jnp.concatenate(pieces,axis=0)
    res = jnp.dot(a2, rhs, preferred_element_type=f32)
    u = res[:128]+res[128:]
    return u + pltpu.roll(u, 64, 1)

def recur(hy, y, yp):
    t = (hy - C0*y)/HALF
    return t if yp is None else 2.0*t - yp

def local(pos, near, i, k):
    return near[k,i]-32*(2*pos[0]+pos[1])

def slot_of(n):
    return jnp.where(n<0,n+36,jnp.where(n>31,n+4,n))

HALO_SLOTS = ((32,33,34,35,0),(33,34,35,0,1),(30,31,36,37,38),(31,36,37,38,39))

def block(ref, slot):
    return ref[pl.ds(pl.multiple_of(slot*128,128),128),:]

def step_kernel(first, wide, last, pos, near, a2, a2h, p, ph, y, yh, *rest):
    rest = list(rest); ext = rest.pop()
    yp = yph = None
    if not first:
        yp = rest.pop(0); yph = rest.pop(0)
    outs = rest
    g = pl.program_id(0)
    @pl.when(g==0)
    def _():
        ext[0:4096,:] = p[...]
        if wide: ext[4096:5120,:] = ph[...]
        else: ext[4352:4864,:] = ph[...]
    @pl.when(g<8)
    def _():
        for r in range(4):
            hy = apply_row(a2[r],[block(ext,slot_of(local(pos,near,4*g+r,k))) for k in range(5)])
            sl = slice(128*r,128*r+128)
            new = recur(hy,y[sl,:],None if first else yp[sl,:])
            if last:
                outs[0][0,:,sl] = new.T[:64]
            else:
                outs[0][sl,:] = new
                outs[1][sl,:] = dup_pack(new)
    if wide:
        @pl.when(g==8)
        def _():
            for r in range(4):
                hy = apply_row(a2h[r],[ext[128*b:128*b+128,:] for b in HALO_SLOTS[r]])
                sl = slice(128*r,128*r+128)
                new = recur(hy,yh[sl,:],None if first else yph[sl,:])
                outs[2][sl,:] = new
                outs[3][sl,:] = dup_pack(new)

def step(pos, near, a2, a2h, p, ph, y, yh, yp=None, yph=None, wide=False, last=False):
    first = yp is None
    B = pl.BlockSpec
    at = lambda g: jnp.minimum(g,7)
    w = lambda *shape: B(shape, lambda g,p,n: (0,)*len(shape))
    yb = B((512,128),lambda g,p,n:(at(g),0))
    sds = jax.ShapeDtypeStruct
    if last:
        outs=[B((1,64,512),lambda g,p,n:(at(g),0,0))]; shapes=[sds((8,64,512),f32)]
    else:
        outs=[yb,yb]; shapes=[sds((4096,128),f32),sds((4096,128),bf16)]
    if wide:
        outs+=[w(512,128)]*2; shapes+=[sds((512,128),f32),sds((512,128),bf16)]
    return pl.pallas_call(functools.partial(step_kernel,first,wide,last), name="step",
        grid_spec=pltpu.PrefetchScalarGridSpec(num_scalar_prefetch=2, grid=(9 if wide else 8,),
            in_specs=[B((4,256,640),lambda g,p,n:(at(g),0,0)), w(4,256,640), w(4096,128), w(*ph.shape), yb, w(512,128)]+([] if first else [yb,w(512,128)]),
            out_specs=outs, scratch_shapes=[pltpu.VMEM((5120,128),bf16)]),
        out_shape=shapes,
        cost_estimate=pl.CostEstimate(flops=36*2*256*640*128*4,bytes_accessed=16*MB,transcendentals=0),
        compiler_params=pltpu.CompilerParams(vmem_limit_bytes=24*MB))(
            pos,near,a2,a2h,p,ph,y,yh,*([] if first else [yp,yph]))

def edge_kernel(pos, near, alo, ahi, vlo, vhi, ph, ylo, yhi, plo, phi, ye, slo, shi, ext):
    lane = lax.broadcasted_iota(jnp.int32,(128,128),1)
    ext[0:256,:] = ph[0:256,:]
    ext[256:1024,:] = vlo[0:768,:]
    ext[1024:1792,:] = vhi[256:1024,:]
    ext[1792:2048,:] = ph[256:512,:]
    new = []
    for e in range(8):
        a, yr, pr = (alo,ylo,plo) if e<4 else (ahi,yhi,phi)
        hy = apply_row(a[e%4],[block(ext,local(pos,near,e if e<4 else 24+e,k)+(2 if e<4 else -18)) for k in range(5)])
        sl = slice(128*(e%4),128*(e%4)+128)
        new.append(recur(hy,yr[sl,:],pr[sl,:]))
        ye[128*e:128*e+128,:] = new[-1]
    for h in range(2):
        slo[128*h:128*h+128,:] = jnp.where(lane<64,new[2*h],new[2*h+1])
        shi[128*h:128*h+128,:] = jnp.where(lane<64,new[4+2*h],new[5+2*h])

def edge(pos, near, a2, p, ph, y, yp):
    B = pl.BlockSpec
    w = lambda shape,*idx: B(shape, lambda g,p,n: idx)
    ys = [w((512,128),0,0), w((512,128),7,0)]
    sds = jax.ShapeDtypeStruct
    return pl.pallas_call(edge_kernel, name="edge",
        grid_spec=pltpu.PrefetchScalarGridSpec(num_scalar_prefetch=2, grid=(1,),
            in_specs=[w((4,256,640),0,0,0), w((4,256,640),7,0,0), w((1024,128),0,0), w((1024,128),3,0), w((512,128),0,0)]+ys+ys,
            out_specs=[w((1024,128),0,0), w((256,128),0,0), w((256,128),0,0)],
            scratch_shapes=[pltpu.VMEM((2048,128),bf16)]),
        out_shape=[sds((1024,128),f32)]+[sds((256,128),f32)]*2,
        cost_estimate=pl.CostEstimate(flops=8*2*256*640*128,bytes_accessed=5*MB,transcendentals=0),
        compiler_params=pltpu.CompilerParams(vmem_limit_bytes=24*MB))(
            pos,near,a2,a2,p,p,ph,y,y,yp,yp)

def inner_kernel(pos, near, a2, p, ye, y, yp, yo, po):
    g = pl.program_id(0)
    @pl.when((g==0)|(g==7))
    def _():
        new = ye[...]
        yo[...] = new
        po[...] = dup_pack(new)
    @pl.when((g>0)&(g<7))
    def _():
        for r in range(4):
            hy = apply_row(a2[r],[block(p,local(pos,near,4*g+r,k)) for k in range(5)])
            sl = slice(128*r,128*r+128)
            new = recur(hy,y[sl,:],yp[sl,:])
            yo[sl,:] = new
            po[sl,:] = dup_pack(new)

def inner(pos, near, a2, p, ye, y, yp):
    B = pl.BlockSpec
    yb = B((512,128),lambda g,p,n:(g,0))
    sds = jax.ShapeDtypeStruct
    return pl.pallas_call(inner_kernel, name="inner",
        grid_spec=pltpu.PrefetchScalarGridSpec(num_scalar_prefetch=2, grid=(8,),
            in_specs=[B((4,256,640),lambda g,p,n:(g,0,0)), B((4096,128),lambda g,p,n:(0,0)), B((512,128),lambda g,p,n:(g//7,0)), yb, yb],
            out_specs=[yb,yb]),
        out_shape=[sds((4096,128),f32),sds((4096,128),bf16)],
        cost_estimate=pl.CostEstimate(flops=24*2*256*640*128*4,bytes_accessed=16*MB,transcendentals=0),
        compiler_params=pltpu.CompilerParams(vmem_limit_bytes=24*MB))(pos,near,a2,p,ye,y,yp)

NT = ((1,),(1,))
NN = ((1,),(0,))
NORB = 65536

def bdot(a, b, dims):
    return lax.dot_general(a,b,(dims,((),())),preferred_element_type=f32)

def params(mb):
    return pltpu.CompilerParams(vmem_limit_bytes=mb*MB)

SMEM = pl.BlockSpec(memory_space=pltpu.SMEM)
VMEM = pl.BlockSpec(memory_space=pltpu.VMEM)

def gram_kernel(pos, x_ref, o_ref, g_ref):
    half = pl.ds(pl.multiple_of(256*pos[1],256),256)
    xs = [split(x_ref[...]),split(o_ref[...])]
    hs = [split(x_ref[half,:]),split(o_ref[half,:])]
    for i in range(2):
        sl = slice(256*i,256*i+256)
        s = None
        for (xh,xl),(hh,hl) in zip(xs,hs):
            t = bdot(xh[sl],hh,NT)+bdot(xl[sl],hh,NT)+bdot(xh[sl],hl,NT)
            s = t if s is None else s+t
        g_ref[32*i:32*i+32] = s.reshape(32,8,256)

def gram(pos, x, o):
    return call(gram_kernel,"gram",(pos,x,o),sds(64,8,256),3*2*512**3)

def applied_kernel(pos, near, x_ref, hi_ref, a2, yt, xh, xl):
    for ref, at, w in ((x_ref,0,512),(hi_ref,512,256)):
        h, l = split(ref[...])
        xh[:,at:at+w] = h; xl[:,at:at+w] = l
    xh[:,512:768] = xh[:,512:768]*2; xl[:,512:768] = xl[:,512:768]*2
    xh[:,768:896] = jnp.zeros((512,128),bf16); xl[:,768:896] = jnp.zeros((512,128),bf16)
    for i in range(4):
        n = [local(pos,near,4*pos[2]+i,k)-4*pos[2] for k in range(5)]
        at = [pl.ds(pl.multiple_of(jnp.where(m<0,6,m)*128,128),128) for m in n]
        h = jnp.concatenate([xh[:,a] for a in at],axis=1)
        l = jnp.concatenate([xl[:,a] for a in at],axis=1)
        r = bdot(h,a2[i],NT)
        yt[:,128*i:128*i+128] = r[:,:128]+r[:,128:]+bdot(l,a2[i,:128,:],NT)

def applied(pos, near, x, hi, a2):
    B = pl.BlockSpec
    w = lambda shape: B(shape, lambda g,p,n: (0,)*len(shape))
    return pl.pallas_call(applied_kernel, name="applied",
        grid_spec=pltpu.PrefetchScalarGridSpec(num_scalar_prefetch=2, grid=(1,),
            in_specs=[w((512,512)),w((512,256)),w((4,256,640))],
            out_specs=w((512,512)),
            scratch_shapes=[pltpu.VMEM((512,896),bf16),pltpu.VMEM((512,896),bf16)]),
        out_shape=jax.ShapeDtypeStruct((512,512),f32),
        cost_estimate=pl.CostEstimate(flops=4*2*512*512*640,bytes_accessed=5*MB,transcendentals=0),
        compiler_params=params(24))(pos,near,x,hi,a2)

def moment_kernel(pos, x_ref, o_ref, yt_ref, ot_ref, g_ref, lo_ref, hi_ref, s_ref, acc):
    c = pos[1]
    xs = [split(x_ref[...]),split(o_ref[...])]
    tail = jnp.where(c==0,hi_ref[...],lo_ref[...])
    og = jnp.concatenate([tail[8*u+3:8*u+6,:] for u in range(4)],axis=1)
    for q in range(2):
        ws = []
        for x, y, g in ((x_ref,yt_ref,g_ref[...]),(o_ref,ot_ref,og)):
            places = (g+0.5)/32.0-1.0
            if q==0:
                w = jnp.where(c==0,y[...],x[...]*places[1:2,:])
            else:
                w = x[...]*jnp.where(c==0,places[0:1,:],places[2:3,:])
            ws.append(split(w))
        for i in range(2):
            sl = slice(256*i,256*i+256)
            s = None
            for (xh,xl),(yh,yl) in zip(xs,ws):
                t = bdot(xh[sl],yh,NT)+bdot(xl[sl],yh,NT)+bdot(xh[sl],yl,NT)
                s = t if s is None else s+t
            if q==0: acc[sl,:] = s
            else: s_ref[32*i:32*i+32,8:16,:] = s.reshape(32,8,512)
        if q==0:
            for i in range(4):
                sl = slice(128*i,128*i+128)
                s_ref[16*i:16*i+16,0:8,:] = (0.5*(acc[sl,:]+acc[:,sl].T)).reshape(16,8,512)

def moments(pos, x, o, yt, ot, g, lo, hi):
    B = pl.BlockSpec
    w = lambda shape,*idx: B(shape, lambda g: idx)
    full = w((512,512),0,0)
    return pl.pallas_call(moment_kernel, name="moments", grid=(1,),
        in_specs=[SMEM]+[full]*4+[w((3,512),0,0),w((32,128),48,0),w((32,128),48,0)],
        out_specs=w((64,16,512),0,0,0), scratch_shapes=[pltpu.VMEM((512,512),f32)],
        out_shape=jax.ShapeDtypeStruct((64,16,512),f32),
        cost_estimate=pl.CostEstimate(flops=12*2*512**3,bytes_accessed=8*MB,transcendentals=0),
        compiler_params=params(40))(pos,x,o,yt,ot,g,lo,hi)

def total_kernel(p_ref, o_ref):
    o_ref[...] = jnp.broadcast_to(jnp.sum(p_ref[...],axis=0)[None],o_ref.shape)

def total(part):
    return call(total_kernel,"total",(part,),sds(128,8,256),200000)

def half_kernel(pos, s_ref, li_ref, out_ref, lt):
    lane = lax.broadcasted_iota(jnp.int32,(8,128),1)
    sub = lax.broadcasted_iota(jnp.int32,(8,128),0)
    z = hdot(jnp.sum(s_ref[...],axis=0),li_ref[...],NT)
    z0 = z[0:8]; z1 = z[8:16]
    k = 8*pos[0]+pos[2]
    lt[...] = li_ref[:,pl.ds(pl.multiple_of((k//16)*128,128),128)].T
    e = jnp.sum(z0*lt[pl.ds(pl.multiple_of(8*(k%16),8),8),:],axis=0,keepdims=True)
    ee = jnp.zeros((8,128),f32)
    for g in range(8):
        b = jnp.broadcast_to(e[:,128*(g//2):128*(g//2)+128],(8,128))
        if g%2==0: b = pltpu.roll(b,64,1)
        ee = jnp.where(sub==g,b,ee)
    for u in range(4):
        for v in range(4):
            a = z0[:,128*u:128*u+128]; b = z1[:,128*u:128*u+128]
            if v: a = pltpu.roll(a,128-32*v,1)
            if v!=1: b = pltpu.roll(b,(160-32*v)%128,1)
            t = jnp.where(lane<32,a,jnp.where(lane<64,b,ee))
            for y in range(8):
                out_ref[8*(4*u+v)+y] = t

def half(pos, s, li):
    return call(half_kernel,"half",(pos,s,li),sds(128,8,128),2*24*512*512*6,[pltpu.VMEM((128,512),f32)],vmem=24)

def tile_kernel(pos, r_ref, li_ref, p_ref, d_ref, w_ref, e_ref, acc):
    c = pos[1]; gx = 2*pos[0]+c; gy = pos[2]
    lane = lax.broadcasted_iota(jnp.int32,(64,128),1)
    lane8 = lax.broadcasted_iota(jnp.int32,(8,128),1)
    lb = li_ref[pl.ds(pl.multiple_of(64*gy,64),64),:]
    t0 = hdot(lb,r_ref[:,0].reshape(512,128),NN)
    t1 = hdot(lb,r_ref[:,1].reshape(512,128),NN)
    t = jnp.where(lane<64,t0,pltpu.roll(t1,64,1))
    tt = jnp.concatenate([t,t],axis=0).T
    p_ref[...] = tt[0:32,0:64]*(1.0/NORB)
    for q in range(3):
        d_ref[q] = tt[32*q+32:32*q+64,0:64]*(1.0/math.sqrt(NORB))
    e = jnp.sum(r_ref[:,0].reshape(64,8,128),axis=0)
    e_ref[...] = e*(1.0/NORB)
    ea = jnp.broadcast_to(e_ref[pl.ds(pos[0],1),:],(8,128))
    ea = pltpu.roll(ea,64-32*c,1)
    ea = jnp.where(lane8<32,ea,0.0)
    ea = ea+pltpu.roll(ea,32,1)+pltpu.roll(ea,64,1)+pltpu.roll(ea,96,1)
    eb = pltpu.roll(jnp.broadcast_to(e_ref[pl.ds(gy,1),:],(8,128)),64,1)
    eb = jnp.broadcast_to(eb[0:1,:],(128,128)).T[0:64,:]
    gap = eb-jnp.broadcast_to(ea[0:1,:],(64,128))
    dip = t*(1.0/math.sqrt(NORB))
    sq = jnp.where(lane>=32,dip*dip,0.0)
    st = (sq+pltpu.roll(sq,32,1)+pltpu.roll(sq,64,1)+pltpu.roll(sq,96,1))*(0.01/math.pi)
    base = (64*(lane8//32)).astype(f32)+0.5
    for w in range(64):
        om = -0.3+0.6*(base+float(w))/256.0
        tot = jnp.zeros((8,128),f32)
        for b in range(8):
            x = om-gap[8*b:8*b+8,:]
            tot = tot+st[8*b:8*b+8,:]/(x*x+0.0001)
        acc[w:w+1,:] = jnp.sum(tot,axis=0,keepdims=True)
    sel = (lane8//32==lax.broadcasted_iota(jnp.int32,(8,128),0)).astype(f32)
    m = hdot(sel,jnp.concatenate([acc[...],acc[...]],axis=0),NT)*(1.0/(512.0*512.0))
    m = jnp.concatenate([jnp.where(lane8[0:1]<64,m[0:1],m[1:2]),jnp.where(lane8[0:1]<64,m[2:3],m[3:4])],axis=0)
    w_ref[...] = jnp.broadcast_to(m[None],(128,2,128))

def tile(pos, r, li):
    return call(tile_kernel,"tile",(pos,r,li),[sds(32,64),sds(3,32,64),sds(128,2,128)],10000000,[pltpu.VMEM((8,128),f32),pltpu.VMEM((64,128),f32)],vmem=24)

def rotate_kernel(pos, x_ref, li_ref, *o_refs):
    xh, xl = split(x_ref[...])
    for i in range(4):
        at = [pl.ds(pl.multiple_of(64*jnp.bitwise_xor(pos[2],2*i+j),64),64) for j in range(2)]
        lh, ll = split(jnp.concatenate([li_ref[a,:] for a in at],axis=0))
        o = bdot(lh,xh,NN)+bdot(ll,xh,NN)+bdot(lh,xl,NN)
        o_refs[2*i][...] = o[0:64]; o_refs[2*i+1][...] = o[64:128]

def rotate(pos, x, li):
    return call(rotate_kernel,"rotate",(pos,x,li),[sds(64,512)]*8,3*2*512**3,vmem=56)

def gather_kernel(pos, *refs):
    for r in range(8):
        refs[8][:,pl.ds(pl.multiple_of(512*jnp.bitwise_xor(pos[2],r),512),512)] = refs[r][...]

def gather(pos, pieces):
    return call(gather_kernel,"gather",(pos,*pieces),sds(64,4096),1000)

SLABS = ("gq","c")
PEERS = ("gq","gy")
ALL = ("gq","c","gy")

def swap(x, axis):
    return lax.all_to_all(x,axis,split_axis=0,concat_axis=0,tiled=True)

def chain(n):
    return [(i,i+1) for i in range(n-1)], [(i+1,i) for i in range(n-1)]

def shards(hopping_blocks, neighbors, orbital_grid, trial_block):
    gq = lax.axis_index("gq"); c = lax.axis_index("c"); gy = lax.axis_index("gy")
    pos = jnp.stack([gq,c,gy])
    near = neighbors.T
    up, down = chain(16)
    vt = trial_block.T
    sup, sdown, grid = payload(pos,near,hopping_blocks,vt,orbital_grid)
    plo = lax.ppermute(sup,SLABS,up)
    phi = lax.ppermute(sdown,SLABS,down)
    a2, y0, p0, own = prep(pos,hopping_blocks,vt)
    a2h, y0h, p0h = halo_prep(plo,phi)
    y1, p1, y1h, p1h = step(pos,near,a2,a2h,p0,p0h,y0,y0h,wide=True)
    ye, slo, shi = edge(pos,near,a2,p1,p1h,y1,y0)
    lo = lax.ppermute(shi,SLABS,up)
    hi = lax.ppermute(slo,SLABS,down)
    y2, p2 = inner(pos,near,a2,p1,ye,y1,y0)
    y2h, p2h = unpack(lo,hi)
    y3, p3, y3h, p3h = step(pos,near,a2,a2h,p2,p2h,y2,y2h,y1,y1h,wide=True)
    sent, = step(pos,near,a2,a2h,p3,p3h,y3,y3h,y2,y2h,last=True)

    x = swap(sent,"gy").reshape(512,512)
    pair = [(i,i^1) for i in range(16)]
    other = lax.ppermute(x,SLABS,pair)
    hi = lax.ppermute(x[:,:256],ALL,chain(128)[1])
    part = gram(pos,x,other)
    part, xa = lax.optimization_barrier((part,x))
    yt = applied(pos,near,xa,hi,own)
    summed, yt = lax.optimization_barrier((swap(part,PEERS),yt))
    ot = lax.ppermute(yt,SLABS,[(i+1,i) for i in range(0,16,2)])
    both, ot = lax.optimization_barrier((total(summed),ot))
    g = swap(both,ALL).reshape(8,2,64,256)
    s = moments(pos,x,other,yt,ot,grid,plo,phi)
    s, g = lax.optimization_barrier((s,g))
    li = chol(g,1.0/NORB)
    q = rotate(pos,x,li)
    s, _ = lax.optimization_barrier((swap(s,PEERS),q[0]))
    rows = swap(half(pos,s,li),ALL).reshape(8,2,64,128)
    projected, dipoles, spec = tile(pos,rows,li)
    q = [q[0]]+[lax.ppermute(q[r],"gy",[(i,i^r) for i in range(8)]) for r in range(1,8)]
    orthonormal = gather(pos,q).T
    spectrum = jnp.sum(swap(spec,ALL),axis=0).reshape(256)
    return orthonormal, projected, dipoles, spectrum

def solution(mesh):
    P = jax.sharding.PartitionSpec
    fine = jax.sharding.Mesh(mesh.devices.reshape(8,2,8),ALL)
    return jax.shard_map(shards, mesh=fine,
        in_specs=(P(SLABS,None,None,None),P(SLABS,None),P(None,SLABS),P(SLABS,"gy")),
        out_specs=(P(SLABS,"gy"),P(SLABS,"gy"),P(None,SLABS,"gy"),P()),
        check_vma=False)
```
